32 devices in a mesh: grp: 2 (over x), gx: 4 (over z), gy: 4 (over y, core).
Axes of the slice: x: 2, y: 2, z: 4, core: 2. Of those that a mesh axis runs over, the one named last changes fastest.
Arguments:
- zonal_boundary_speed: float32 [32, 4, 4, 512], P(None, 'gy', 'grp', 'gx'), may hold values from -0.2 to 0.2
- meridional_boundary_speed: float32 [32, 4, 4, 512], P(None, 'gy', 'grp', 'gx'), may hold values from -0.2 to 0.2
- potential_warmth: float32 [32, 4, 4, 512], P(None, 'gy', 'grp', 'gx'), may hold values from 2 to 28
- saltiness_field: float32 [32, 4, 4, 512], P(None, 'gy', 'grp', 'gx'), may hold values from 33 to 37
- quiescent_mixing_profile: float32 [32, 4, 4, 512], P(None, 'gy', 'grp', 'gx'), may hold values from 0.005 to 0.05
- substance_amounts: float32 [19, 32, 16, 512], P(None, 'grp', 'gy', 'gx'), may hold values from 0.1 to 3
- submerged_layer_number: int32 [16, 512], P('gy', 'gx'), may hold values from 0 to 32
- solar_radiation: float32 [16, 512], P('gy', 'gx'), may hold values from 0.2 to 1
- interaction_rates: float32 [19, 19], replicated, may hold values from -1.25 to 1.25
- photosynthetic_rates: float32 [19], replicated, may hold values from 0.1 to 1
- saturation_irradiance: float32 [19], replicated, may hold values from 0.05 to 0.5
- pigment_per_tracer: float32 [19], replicated, may hold values from 0.01 to 0.1
Outputs:
- east_final: float32 [32, 4, 4, 512], P(None, 'gy', 'grp', 'gx')
- north_final: float32 [32, 4, 4, 512], P(None, 'gy', 'grp', 'gx')
- temperature_final: float32 [32, 4, 4, 512], P(None, 'gy', 'grp', 'gx')
- salinity_final: float32 [32, 4, 4, 512], P(None, 'gy', 'grp', 'gx')
- tracers_final: float32 [19, 32, 16, 512], P(None, 'grp', 'gy', 'gx')
The draws below stay inside these ranges and needn't reach their ends.
All inputs are finite; a program needn't handle non-finite values.
Results may differ from the reference program's by a relative error of at most 0.0001.
Values sent between devices are 32-bit elements; how exact they have to be, the bound alone decides.
No kernel may reach another device: no remote copies, remote signals or barrier semaphores. Data moves between devices by JAX's collectives and lax.ppermute only.
A program may use at most 64 MiB of HBM per device.

```python
import math
import jax
import jax.numpy as jnp
from jax import lax

NTR = 19
DEPTH_LAYERS = 32
PIECE_LATITUDES = 4
STEPS = 2
MESH_WIDTH = 512
NY = 16
MERIDIAN_PIECES = 4


def plant(values, key, low, high):
    longest = values.shape.index(max(values.shape))
    spots = []
    for shift in (0, 1):
        where = [jax.random.randint(jax.random.fold_in(key, axis), (), 0, length) for axis, length in enumerate(values.shape)]
        where[longest] = (where[longest] + shift) % values.shape[longest]
        spots.append(tuple(where))
    return values.at[spots[0]].set(low).at[spots[1]].set(high)


def shard_levels(key, extent, split, least, largest):
    def one(axis_at, parts):
        steps = jax.random.uniform(jax.random.fold_in(jax.random.fold_in(key, 6), axis_at), (parts,), jnp.float32, least / len(split), largest / len(split))
        return jnp.repeat(jnp.exp(steps), extent[axis_at] // parts).reshape((-1,) + (1,) * (len(extent) - axis_at - 1))

    level = one(*split[0])
    for cut in split[1:]:
        level = level * one(*cut)
    return level


def gaussian(stream_key, dims, width, limit, dtype=jnp.bfloat16):
    result = width * jax.random.normal(stream_key, dims, jnp.float32)
    return jnp.clip(result, min=-limit, max=limit).astype(dtype)


def setup_inputs(seed: int = 0) -> dict:
    keys = jax.random.split(jax.random.key(seed), 13)
    return {
        "zonal_boundary_speed": jnp.clip(jax.random.uniform(keys[0], (DEPTH_LAYERS, MERIDIAN_PIECES, PIECE_LATITUDES, MESH_WIDTH), jnp.float32, -0.2, 0.2) * shard_levels(keys[0], (DEPTH_LAYERS, MERIDIAN_PIECES, PIECE_LATITUDES, MESH_WIDTH), ((1, 4), (2, 2), (3, 4)), -0.4, 0.0), -0.2, 0.2),
        "meridional_boundary_speed": jnp.clip(jax.random.uniform(keys[1], (DEPTH_LAYERS, MERIDIAN_PIECES, PIECE_LATITUDES, MESH_WIDTH), jnp.float32, -0.2, 0.2) * shard_levels(keys[1], (DEPTH_LAYERS, MERIDIAN_PIECES, PIECE_LATITUDES, MESH_WIDTH), ((1, 4), (2, 2), (3, 4)), -0.4, 0.0), -0.2, 0.2),
        "potential_warmth": jnp.clip(2.0 + 26.0 * jax.random.uniform(keys[2], (DEPTH_LAYERS, MERIDIAN_PIECES, PIECE_LATITUDES, MESH_WIDTH), jnp.float32) ** shard_levels(keys[2], (DEPTH_LAYERS, MERIDIAN_PIECES, PIECE_LATITUDES, MESH_WIDTH), ((1, 4), (2, 2), (3, 4)), -0.2, 0.2), 2.0, 28.0),
        "saltiness_field": jnp.clip(33.0 + 4.0 * jax.random.uniform(keys[3], (DEPTH_LAYERS, MERIDIAN_PIECES, PIECE_LATITUDES, MESH_WIDTH), jnp.float32) ** shard_levels(keys[3], (DEPTH_LAYERS, MERIDIAN_PIECES, PIECE_LATITUDES, MESH_WIDTH), ((1, 4), (2, 2), (3, 4)), -0.2, 0.2), 33.0, 37.0),
        "quiescent_mixing_profile": jnp.clip(jnp.exp(math.log(0.05) - 2.3025851 * jax.random.uniform(keys[4], (DEPTH_LAYERS, MERIDIAN_PIECES, PIECE_LATITUDES, MESH_WIDTH), jnp.float32) ** shard_levels(keys[4], (DEPTH_LAYERS, MERIDIAN_PIECES, PIECE_LATITUDES, MESH_WIDTH), ((1, 4), (2, 2), (3, 4)), -0.2, 0.2)), 0.005, 0.05),
        "substance_amounts": jnp.clip(jnp.exp(math.log(3.0) - 3.4011974 * jax.random.uniform(keys[5], (NTR, DEPTH_LAYERS, NY, MESH_WIDTH), jnp.float32) ** shard_levels(keys[5], (NTR, DEPTH_LAYERS, NY, MESH_WIDTH), ((1, 2), (2, 4), (3, 4)), -0.2, 0.2)), 0.1, 3.0),
        "submerged_layer_number": plant(jax.random.randint(keys[6], (NY, MESH_WIDTH), 0, DEPTH_LAYERS + 1), jax.random.fold_in(keys[6], 1), 0, DEPTH_LAYERS).astype(jnp.int32),
        "solar_radiation": jnp.clip(jnp.exp(math.log(1.0) - 1.609438 * jax.random.uniform(keys[7], (NY, MESH_WIDTH), jnp.float32) ** shard_levels(keys[7], (NY, MESH_WIDTH), ((0, 4), (1, 4)), -0.2, 0.2)), 0.2, 1.0),
        "interaction_rates": gaussian(keys[8], (NTR, NTR), NTR ** -0.5, 1.25, jnp.float32),
        "photosynthetic_rates": jnp.clip(jnp.exp(jax.random.uniform(keys[9], (NTR,), jnp.float32, math.log(0.1), math.log(1.0))), 0.1, 1.0),
        "saturation_irradiance": jnp.clip(jnp.exp(jax.random.uniform(keys[10], (NTR,), jnp.float32, math.log(0.05), math.log(0.5))), 0.05, 0.5),
        "pigment_per_tracer": jnp.clip(jnp.exp(jax.random.uniform(keys[11], (NTR,), jnp.float32, math.log(0.01), math.log(0.1))), 0.01, 0.1),
    }


WATER_ATTEN = 0.01
PIGMENT_ATTEN = 0.05
WARMING_UPTAKE = 5.0
WARM_EXPANSION = 0.2
SALT_EXPANSION = 0.8
CONVECT_MIX = 0.15
SIDE_DIFFUSE = 0.05
WARMING_FACTOR = 0.0633
TIME_STEP = 0.5


def trim_axis(values, dimension_slot, start, stop):
    leading = (slice(None),) * (values.ndim + dimension_slot)
    return values[leading + (slice(start, stop),)]


def pad_axis(values, dimension_slot):
    widths = [(0, 0)] * values.ndim
    widths[dimension_slot] = (1, 1)
    return jnp.pad(values, widths)


def face_divergence(tracer_amounts, velocity, submerged_mask, dimension_slot):
    lower_conc = trim_axis(tracer_amounts, dimension_slot, None, -1)
    upper_conc = trim_axis(tracer_amounts, dimension_slot, 1, None)
    face_speed = trim_axis(velocity, dimension_slot, None, -1)
    opening = trim_axis(submerged_mask, dimension_slot, None, -1) * trim_axis(submerged_mask, dimension_slot, 1, None)
    flux_face = opening * (jnp.maximum(face_speed, 0.0) * lower_conc + jnp.minimum(face_speed, 0.0) * upper_conc - SIDE_DIFFUSE * (upper_conc - lower_conc))
    return trim_axis(flux_face, dimension_slot, 1, None) - trim_axis(flux_face, dimension_slot, None, -1)


def level_divergence(tracer_amounts, mixing_coefficient):
    flux_face = trim_axis(mixing_coefficient, -3, None, -1) * (trim_axis(tracer_amounts, -3, 1, None) - trim_axis(tracer_amounts, -3, None, -1))
    return trim_axis(flux_face, -3, 1, None) - trim_axis(flux_face, -3, None, -1)


def light_columns(pigment, surface):
    attenuation = WATER_ATTEN + PIGMENT_ATTEN * pigment
    above = jnp.cumsum(attenuation, axis=0) - attenuation
    top_light = surface * jnp.exp(-above)
    return top_light * (1.0 - jnp.exp(-attenuation)), top_light * jnp.exp(-0.5 * attenuation)


def marine_advance(zonal_transport, meridional_transport, thermal_mesh, brine_values, quiescent_mixing, radiative_warming, submerged_mask):
    thermal_mesh = thermal_mesh + WARMING_UPTAKE * radiative_warming * submerged_mask
    water_buoyancy = SALT_EXPANSION * brine_values - WARM_EXPANSION * thermal_mesh
    strat = water_buoyancy[1:] - water_buoyancy[:-1]
    face_mix = (0.5 * (quiescent_mixing[:-1] + quiescent_mixing[1:]) + CONVECT_MIX * jax.nn.sigmoid(-strat)) * submerged_mask[1:]
    bottom = jnp.zeros_like(face_mix[:1])
    mixing_coefficient = jnp.concatenate([face_mix, bottom], axis=0)

    def turbulent_stirring(field):
        flux_face = face_mix * (field[1:] - field[:-1])
        return field + jnp.concatenate([flux_face, bottom], axis=0) - jnp.concatenate([bottom, flux_face], axis=0)

    return turbulent_stirring(zonal_transport), turbulent_stirring(meridional_transport), turbulent_stirring(thermal_mesh), turbulent_stirring(brine_values), mixing_coefficient


def chemical_kinetics(tracer_amounts, thermal_mesh, photosynthetic_radiance, submerged_mask, interaction_rates, photosynthetic_rates, saturation_irradiance):
    thermal_multiplier = jnp.exp(WARMING_FACTOR * (thermal_mesh - 20.0))
    mixed_terms = jnp.einsum("ij,jzyx->izyx", interaction_rates, tracer_amounts, precision=lax.Precision.HIGHEST)
    light_limit = photosynthetic_radiance / (photosynthetic_radiance + saturation_irradiance[:, None, None, None])
    return TIME_STEP * submerged_mask * (thermal_multiplier * mixed_terms + photosynthetic_rates[:, None, None, None] * light_limit * tracer_amounts)


def reference(zonal_boundary_speed, meridional_boundary_speed, potential_warmth, saltiness_field, quiescent_mixing_profile, substance_amounts, submerged_layer_number, solar_radiation, interaction_rates, photosynthetic_rates, saturation_irradiance, pigment_per_tracer):
    mesh_shape_sizes = (DEPTH_LAYERS, NY, MESH_WIDTH)
    zonal_transport = zonal_boundary_speed.reshape(mesh_shape_sizes)
    meridional_transport = meridional_boundary_speed.reshape(mesh_shape_sizes)
    thermal_mesh = potential_warmth.reshape(mesh_shape_sizes)
    brine_values = saltiness_field.reshape(mesh_shape_sizes)
    quiescent_mixing = quiescent_mixing_profile.reshape(mesh_shape_sizes)
    submerged_mask = (lax.broadcasted_iota(jnp.int32, mesh_shape_sizes, 0) < submerged_layer_number[None]).astype(jnp.float32)
    tracer_amounts = substance_amounts
    for repeat in range(STEPS):
        pigment = jnp.einsum("i,izyx->zyx", pigment_per_tracer, tracer_amounts, precision=lax.Precision.HIGHEST)
        radiative_warming, photosynthetic_radiance = light_columns(pigment, solar_radiation[None])
        zonal_transport, meridional_transport, thermal_mesh, brine_values, mixing_coefficient = marine_advance(zonal_transport, meridional_transport, thermal_mesh, brine_values, quiescent_mixing, radiative_warming, submerged_mask)
        zonal_increment = face_divergence(pad_axis(tracer_amounts, -1), pad_axis(zonal_transport, -1), pad_axis(submerged_mask, -1), -1)
        meridional_increment = face_divergence(pad_axis(tracer_amounts, -2), pad_axis(meridional_transport, -2), pad_axis(submerged_mask, -2), -2)
        depthwise_transfer = level_divergence(pad_axis(tracer_amounts, -3), pad_axis(mixing_coefficient, -3))
        tracer_amounts = tracer_amounts - zonal_increment - meridional_increment + depthwise_transfer + chemical_kinetics(tracer_amounts, thermal_mesh, photosynthetic_radiance, submerged_mask, interaction_rates, photosynthetic_rates, saturation_irradiance)
    result_dimensions = zonal_boundary_speed.shape
    return (zonal_transport.reshape(result_dimensions), meridional_transport.reshape(result_dimensions), thermal_mesh.reshape(result_dimensions), brine_values.reshape(result_dimensions), tracer_amounts)
```

```python
import functools

import jax
import jax.numpy as jnp
from jax import lax
from jax.experimental import pallas as pl
from jax.experimental.pallas import tpu as pltpu
from jax.sharding import PartitionSpec as P

STEPS = 2

WATER_ATTEN = 0.01
PIGMENT_ATTEN = 0.05
WARMING_UPTAKE = 5.0
WARM_EXPANSION = 0.2
SALT_EXPANSION = 0.8
CONVECT_MIX = 0.15
SIDE_DIFFUSE = 0.05
WARMING_FACTOR = 0.0633
TIME_STEP = 0.5

SUB = 8
AXES = ("grp", "gx", "gy")
VMEM_LIMIT = 48 * 1024 * 1024

F32 = jnp.float32


def vmem():
    return pl.BlockSpec(memory_space=pltpu.VMEM)


def smem():
    return pl.BlockSpec(memory_space=pltpu.SMEM)


def shape(*dims):
    return jax.ShapeDtypeStruct(dims, F32)


def turn(x, shift, axis):
    shift = shift % x.shape[axis]
    return x if shift == 0 else pltpu.roll(x, shift, axis)


def iota(x, axis):
    return lax.broadcasted_iota(jnp.int32, x, axis)


def pairing(sizes, axis, odd):
    size_g, size_x, size_y = sizes

    def partner(g, x, y):
        i, n = (x, size_x) if axis == "gx" else (y, size_y)
        j = i + 1 if i % 2 == odd else i - 1
        if 0 <= j < n:
            return (g, j, y) if axis == "gx" else (g, x, j)
        if axis == "gx":
            return (g, x, y ^ 1) if (y ^ 1) < size_y else (g, x, y)
        return (g ^ 1, x, y) if (g ^ 1) < size_g else (g, x, y)

    def index(g, x, y):
        return (g * size_x + x) * size_y + y

    return [
        (index(g, x, y), index(*partner(g, x, y)))
        for g in range(size_g)
        for x in range(size_x)
        for y in range(size_y)
    ]


def from_others(value, count):
    return [
        lax.ppermute(value, "grp", [(i, (i + k) % count) for i in range(count)])
        for k in range(1, count)
    ]


def pick(mine, others, k):
    value = mine
    for at, other in enumerate(others):
        value = jnp.where(k == at + 1, other, value)
    return value


def pack_sides(c, t, left, right):
    lane = iota(c.shape, 1)
    left = jnp.where(lane == t, turn(c, t, 1), left)
    right = jnp.where(lane == t, turn(c, t + 1, 1), right)
    return left, right


def write_levels(c, t, lev_refs, g):
    if len(lev_refs) == 1:
        lev_refs[0][t] = jnp.where(g == 0, c[-SUB:], c[:SUB])
    else:
        lev_refs[0][t] = c[-SUB:]
        lev_refs[1][t] = c[:SUB]


def prep_kernel(rows, count, pig_ref, c_ref, p_ref, left_ref, right_ref, first_ref, last_ref, *lev_refs):
    g = lax.axis_index("grp")
    tracers, cells, _ = c_ref.shape
    levels = cells // rows
    pigment = left = right = jnp.zeros(c_ref.shape[1:], F32)
    for t in range(tracers):
        c = c_ref[t]
        pigment = pigment + pig_ref[t] * c
        left, right = pack_sides(c, t, left, right)
        first_ref[t] = c_ref[t, pl.ds(0, levels, stride=rows), :]
        last_ref[t] = c_ref[t, pl.ds(rows - 1, levels, stride=rows), :]
        write_levels(c, t, lev_refs, g)
    p_ref[...] = pigment
    left_ref[...] = left
    right_ref[...] = right


def ocean_kernel(rows, count, tracers, first_step, last_step, *refs):
    refs = list(refs)

    def take(n):
        out = refs[:n]
        del refs[:n]
        return out

    depth_ref, solar_ref, left_in, right_in, first_in, last_in, p_own = take(7)
    p_others = take(count - 1)
    if first_step:
        own_fields = take(5)
        other_fields = [take(5) for _ in range(count - 1)]
    else:
        full_in = take(5)
    band_ref, msg_xa, msg_xb, msg_ya, msg_yb = take(5)
    final_out = take(4) if last_step else []
    full_out = [] if last_step else take(5)
    (p_full, depth_s, solar_s, *scratch) = take(3 + 12)
    g = lax.axis_index("grp")
    x = lax.axis_index("gx")
    y = lax.axis_index("gy")
    cells, width = p_own.shape
    levels = cells // rows
    total = count * cells
    all_levels = total // rows
    strip = rows // count

    for b in range(count):
        k = lax.rem(g - b + count, count)
        p_full[pl.ds(b * cells, cells), :] = pick(p_own[...], [o[...] for o in p_others], k)
    fields = scratch[:5]
    if first_step:
        for at in range(5):
            for s in range(count):
                k = lax.rem(g - s + count, count)
                for r in range(strip):
                    here = pl.ds(r, all_levels, stride=strip)
                    fields[at][pl.ds(s * strip + r, all_levels, stride=rows), :] = pick(
                        own_fields[at][here, :], [o[at][here, :] for o in other_fields], k
                    )
    else:
        fields = full_in
    for r in range(0, SUB, rows):
        depth_s[pl.ds(r, rows), :] = depth_ref[...]
        solar_s[pl.ds(r, rows), :] = solar_ref[...]

    def spread(ref):
        v = ref[...]
        return jnp.broadcast_to(v[None], (total // SUB, SUB, width)).reshape(total, width)

    row = iota((total, width), 0)
    wet = jnp.where(row // rows < spread(depth_s), 1.0, 0.0)
    att = WATER_ATTEN + PIGMENT_ATTEN * p_full[...]
    summed = att
    step = rows
    while step < total:
        summed = summed + jnp.where(row >= step, turn(summed, step, 0), 0.0)
        step *= 2
    top = spread(solar_s) * jnp.exp(att - summed)
    par = top * jnp.exp(-0.5 * att)
    east, north, temp, sal, mixing = [f[...] for f in fields]
    temp = temp + WARMING_UPTAKE * (top * (1.0 - jnp.exp(-att))) * wet

    def below(v):
        return turn(v, -rows, 0)

    density = SALT_EXPANSION * sal - WARM_EXPANSION * temp
    face = 0.5 * (mixing + below(mixing)) + CONVECT_MIX / (1.0 + jnp.exp(below(density) - density))
    face = jnp.where(row < total - rows, face * below(wet), 0.0)

    def stir(v):
        flux = face * (below(v) - v)
        return v + flux - turn(flux, rows, 0)

    out = [stir(v) for v in (east, north, temp, sal)]
    for at, v in enumerate(out):
        if last_step:
            scratch[5 + at][...] = v
        else:
            full_out[at][...] = v
    if not last_step:
        full_out[4][...] = mixing
    stored = scratch[5:9] if last_step else full_out
    scratch[9][...] = face
    scratch[10][...] = par
    scratch[11][...] = wet

    if last_step:
        for at in range(4):
            for r in range(strip):
                value = stored[at][pl.ds(r, all_levels, stride=rows), :]
                for s in range(1, count):
                    value = jnp.where(
                        g == s, stored[at][pl.ds(s * strip + r, all_levels, stride=rows), :], value
                    )
                final_out[at][pl.ds(r, all_levels, stride=strip), :] = value

    band = pl.ds(pl.multiple_of(g * cells, SUB), cells)
    above = pl.ds(pl.multiple_of(lax.max(g * cells - SUB, 0), SUB), SUB)
    face_band = scratch[9][band, :]
    lifted = jnp.concatenate([scratch[9][above, :], face_band], axis=0)
    lifted = turn(lifted, rows, 0)[SUB:]
    lifted = jnp.where((iota((cells, width), 0) < rows) & (g == 0), 0.0, lifted)
    u = stored[0][band, :]
    wet_band = scratch[11][band, :]
    band_ref[0] = u
    band_ref[1] = stored[1][band, :]
    band_ref[2] = stored[2][band, :]
    band_ref[3] = face_band
    band_ref[4] = lifted
    band_ref[5] = scratch[10][band, :]
    band_ref[6] = wet_band

    left, right = pack_sides(wet_band, tracers + 1, left_in[...], right_in[...])
    _, right = pack_sides(u, tracers, left, right)
    even = lax.rem(x, 2) == 0
    msg_xa[...] = jnp.where(even, right, left)
    msg_xb[...] = jnp.where(even, left, right)
    even = lax.rem(y, 2) == 0
    for t in range(tracers):
        msg_ya[t] = jnp.where(even, last_in[t], first_in[t])
        msg_yb[t] = jnp.where(even, first_in[t], last_in[t])
    speed = band_ref[1, pl.ds(rows - 1, levels, stride=rows), :]
    wet_first = band_ref[6, pl.ds(0, levels, stride=rows), :]
    wet_last = band_ref[6, pl.ds(rows - 1, levels, stride=rows), :]
    msg_ya[tracers] = speed
    msg_yb[tracers] = speed
    msg_ya[tracers + 1] = jnp.where(even, wet_last, wet_first)
    msg_yb[tracers + 1] = jnp.where(even, wet_first, wet_last)


def tracer_kernel(rows, count, sizes, last_step, *refs):
    refs = list(refs)

    def take(n):
        out = refs[:n]
        del refs[:n]
        return out

    photo_ref, sat_ref, pig_ref, rates_ref, c_ref, band_ref = take(6)
    got_xa, got_xb, got_ya, got_yb = take(4)
    lev_in = take(1 if count == 2 else 2)
    (out_ref,) = take(1)
    if not last_step:
        p_ref, left_ref, right_ref, first_ref, last_ref = take(5)
        lev_out = take(1 if count == 2 else 2)
    south_s, north_s, mix_s = take(3)
    _, size_x, size_y = sizes
    g = lax.axis_index("grp")
    x = lax.axis_index("gx")
    y = lax.axis_index("gy")
    tracers, cells, width = c_ref.shape
    levels = cells // rows
    blocks = cells // SUB
    lane = iota((cells, width), 1)
    row = iota((cells, width), 0)
    at_row = lax.rem(row, rows)

    depth = tracers * SUB
    spread = jnp.where(iota((depth, tracers), 0) // SUB == iota((depth, tracers), 1), 1.0, 0.0)
    spread_t = jnp.where(iota((tracers, depth), 1) // SUB == iota((tracers, depth), 0), 1.0, 0.0)
    dot = functools.partial(jnp.dot, preferred_element_type=F32)
    exact = functools.partial(dot, precision=lax.Precision.HIGHEST)
    weights = exact(exact(spread, rates_ref[...]), spread_t)
    weights = jnp.where(
        lax.rem(iota((depth, depth), 0), SUB) == lax.rem(iota((depth, depth), 1), SUB), weights, 0.0
    )

    def halves(v):
        high = v.astype(jnp.bfloat16)
        return high, (v - high.astype(F32)).astype(jnp.bfloat16)

    w_high, w_low = halves(weights)
    for b in range(blocks):
        cut = c_ref[:, pl.ds(b * SUB, SUB), :].reshape(depth, width)
        c_high, c_low = halves(cut)
        mixed = dot(w_high, c_high) + (dot(w_high, c_low) + dot(w_low, c_high))
        mix_s[:, pl.ds(b * SUB, SUB), :] = mixed.reshape(tracers, SUB, width)

    even = lax.rem(x, 2) == 0
    west = jnp.where(even, got_xb[...], got_xa[...])
    east = jnp.where(even, got_xa[...], got_xb[...])
    even = lax.rem(y, 2) == 0
    for t in range(tracers + 2):
        south_s[t, pl.ds(0, levels, stride=rows), :] = jnp.where(even, got_yb[t], got_ya[t])
        north_s[t, pl.ds(rows - 1, levels, stride=rows), :] = jnp.where(even, got_ya[t], got_yb[t])

    def from_west(v, slot):
        return jnp.where(lane == 0, turn(west, -slot, 1), turn(v, 1, 1))

    def from_east(v, slot):
        return jnp.where(lane == width - 1, turn(east, -1 - slot, 1), turn(v, -1, 1))

    def from_south(v, slot):
        return jnp.where(at_row == 0, south_s[slot], turn(v, 1, 0))

    def from_north(v, slot):
        return jnp.where(at_row == rows - 1, north_s[slot], turn(v, -1, 0))

    u = band_ref[0]
    v = band_ref[1]
    wet = band_ref[6]
    open_w = wet * jnp.where((lane == 0) & (x == 0), 0.0, from_west(wet, tracers + 1))
    open_e = wet * jnp.where((lane == width - 1) & (x == size_x - 1), 0.0, from_east(wet, tracers + 1))
    open_s = wet * jnp.where((at_row == 0) & (y == 0), 0.0, from_south(wet, tracers + 1))
    open_n = wet * jnp.where((at_row == rows - 1) & (y == size_y - 1), 0.0, from_north(wet, tracers + 1))

    def lower(opening, speed):
        return opening * (jnp.maximum(speed, 0.0) + SIDE_DIFFUSE)

    def upper(opening, speed):
        return opening * (jnp.minimum(speed, 0.0) - SIDE_DIFFUSE)

    u_w = from_west(u, tracers)
    v_s = from_south(v, tracers)
    k_w = lower(open_w, u_w)
    k_e = -upper(open_e, u)
    k_s = lower(open_s, v_s)
    k_n = -upper(open_n, v)
    k_d = band_ref[3]
    k_u = band_ref[4]
    k_c = 1.0 - lower(open_e, u) + upper(open_w, u_w) - lower(open_n, v) + upper(open_s, v_s) - k_d - k_u
    par = band_ref[5]
    warm = TIME_STEP * wet * jnp.exp(WARMING_FACTOR * (band_ref[2] - 20.0))
    lit = TIME_STEP * wet * par

    if not last_step:
        pigment = left = right = jnp.zeros((cells, width), F32)
    for t in range(tracers):
        c = c_ref[t]
        up8, down8 = lev_in[0][t], lev_in[-1][t]
        c_u = turn(jnp.concatenate([up8, c], axis=0), rows, 0)[SUB:]
        c_d = turn(jnp.concatenate([c, down8], axis=0), -rows, 0)[:cells]
        new = (
            (k_c + photo_ref[t] * (lit / (par + sat_ref[t]))) * c
            + k_w * from_west(c, t)
            + k_e * from_east(c, t)
            + k_s * from_south(c, t)
            + k_n * from_north(c, t)
            + k_u * c_u
            + k_d * c_d
            + warm * mix_s[t]
        )
        out_ref[t] = new
        if not last_step:
            pigment = pigment + pig_ref[t] * new
            left, right = pack_sides(new, t, left, right)
            first_ref[t] = out_ref[t, pl.ds(0, levels, stride=rows), :]
            last_ref[t] = out_ref[t, pl.ds(rows - 1, levels, stride=rows), :]
            write_levels(new, t, lev_out, g)
    if not last_step:
        p_ref[...] = pigment
        left_ref[...] = left
        right_ref[...] = right


def call(kernel, ins, in_specs, outs, scratch=(), flops=0):
    return pl.pallas_call(
        kernel,
        in_specs=in_specs,
        out_specs=[vmem() for _ in outs],
        out_shape=outs,
        scratch_shapes=list(scratch),
        compiler_params=pltpu.CompilerParams(vmem_limit_bytes=VMEM_LIMIT),
        cost_estimate=pl.CostEstimate(flops=flops, bytes_accessed=1 << 20, transcendentals=0),
    )(*ins)


def per_device(
    sizes,
    zonal_boundary_speed,
    meridional_boundary_speed,
    potential_warmth,
    saltiness_field,
    quiescent_mixing_profile,
    substance_amounts,
    submerged_layer_number,
    solar_radiation,
    interaction_rates,
    photosynthetic_rates,
    saturation_irradiance,
    pigment_per_tracer,
):
    count = sizes[0]
    result_dimensions = zonal_boundary_speed.shape
    all_levels, _, strip, width = result_dimensions
    tracers, levels, rows, _ = substance_amounts.shape
    cells = levels * rows
    total = all_levels * rows
    lev_n = 1 if count == 2 else 2

    own = [
        f.reshape(all_levels * strip, width)
        for f in (
            zonal_boundary_speed,
            meridional_boundary_speed,
            potential_warmth,
            saltiness_field,
            quiescent_mixing_profile,
        )
    ]
    c = substance_amounts.reshape(tracers, cells, width)
    others = [from_others(f, count) for f in own]

    packs = [
        shape(cells, width),
        shape(cells, width),
        shape(cells, width),
        shape(tracers, levels, width),
        shape(tracers, levels, width),
    ] + [shape(tracers, SUB, width)] * lev_n
    prepared = call(
        functools.partial(prep_kernel, rows, count),
        (pigment_per_tracer, c),
        [smem(), vmem()],
        packs,
        flops=1 << 20,
    )
    full = None
    for step in range(STEPS):
        first_step, last_step = step == 0, step == STEPS - 1
        pigment, left, right, first, last, *lev = prepared
        p_others = from_others(pigment, count)
        if count == 2:
            lev = from_others(lev[0], count)
        else:
            lev = [
                lax.ppermute(lev[0], "grp", [(i, (i + 1) % count) for i in range(count)]),
                lax.ppermute(lev[1], "grp", [((i + 1) % count, i) for i in range(count)]),
            ]
        if first_step:
            fields = own + [others[at][k] for k in range(count - 1) for at in range(5)]
        else:
            fields = full
        ins = [submerged_layer_number, solar_radiation, left, right, first, last, pigment, *p_others, *fields]
        msg_rows = shape(tracers + 2, levels, width)
        msg_cols = shape(cells, width)
        outs = [shape(7, cells, width), msg_cols, msg_cols, msg_rows, msg_rows]
        if last_step:
            outs += [shape(all_levels * strip, width)] * 4
        else:
            outs += [shape(total, width)] * 5
        column = pltpu.VMEM((total, width), F32)
        band, xa, xb, ya, yb, *full = call(
            functools.partial(ocean_kernel, rows, count, tracers, first_step, last_step),
            ins,
            [vmem() for _ in ins],
            outs,
            [column, pltpu.VMEM((SUB, width), jnp.int32), pltpu.VMEM((SUB, width), F32)] + [column] * 12,
            flops=1 << 20,
        )
        xa = lax.ppermute(xa, AXES, pairing(sizes, "gx", 0))
        xb = lax.ppermute(xb, AXES, pairing(sizes, "gx", 1))
        ya = lax.ppermute(ya, AXES, pairing(sizes, "gy", 0))
        yb = lax.ppermute(yb, AXES, pairing(sizes, "gy", 1))
        ins = [
            photosynthetic_rates,
            saturation_irradiance,
            pigment_per_tracer,
            interaction_rates,
            c,
            band,
            xa,
            xb,
            ya,
            yb,
            *lev,
        ]
        c, *prepared = call(
            functools.partial(tracer_kernel, rows, count, sizes, last_step),
            ins,
            [smem(), smem(), smem()] + [vmem() for _ in ins[3:]],
            [shape(tracers, cells, width)] + ([] if last_step else packs),
            [pltpu.VMEM((tracers + 2, cells, width), F32)] * 2 + [pltpu.VMEM((tracers, cells, width), F32)],
            flops=1 << 22,
        )
    return tuple(f.reshape(result_dimensions) for f in full) + (c.reshape(substance_amounts.shape),)


def solution(mesh):
    ocean = P(None, "gy", "grp", "gx")
    tracer = P(None, "grp", "gy", "gx")
    surface = P("gy", "gx")
    sizes = tuple(mesh.shape[a] for a in AXES)
    return jax.shard_map(
        functools.partial(per_device, sizes),
        mesh=mesh,
        in_specs=(ocean,) * 5 + (tracer, surface, surface) + (P(),) * 4,
        out_specs=(ocean,) * 4 + (tracer,),
        check_vma=False,
    )
```

```python
import functools

import jax
import jax.numpy as jnp
from jax import lax
from jax.experimental import pallas as pl
from jax.experimental.pallas import tpu as pltpu
from jax.sharding import PartitionSpec as P

STEPS = 2

WATER_ATTEN = 0.01
PIGMENT_ATTEN = 0.05
WARMING_UPTAKE = 5.0
WARM_EXPANSION = 0.2
SALT_EXPANSION = 0.8
CONVECT_MIX = 0.15
SIDE_DIFFUSE = 0.05
WARMING_FACTOR = 0.0633
TIME_STEP = 0.5

SUB = 8
AXES = ("grp", "gx", "gy")
VMEM_LIMIT = 48 * 1024 * 1024

F32 = jnp.float32


def vmem():
    return pl.BlockSpec(memory_space=pltpu.VMEM)


def hbm():
    return pl.BlockSpec(memory_space=pltpu.HBM)


def smem():
    return pl.BlockSpec(memory_space=pltpu.SMEM)


def shape(*dims):
    return jax.ShapeDtypeStruct(dims, F32)


def turn(x, shift, axis):
    shift = shift % x.shape[axis]
    return x if shift == 0 else pltpu.roll(x, shift, axis)


def iota(x, axis):
    return lax.broadcasted_iota(jnp.int32, x, axis)


def pairing(sizes, axis, odd):
    size_g, size_x, size_y = sizes

    def partner(g, x, y):
        i, n = (x, size_x) if axis == "gx" else (y, size_y)
        j = i + 1 if i % 2 == odd else i - 1
        if 0 <= j < n:
            return (g, j, y) if axis == "gx" else (g, x, j)
        if axis == "gx":
            return (g, x, y ^ 1) if (y ^ 1) < size_y else (g, x, y)
        return (g ^ 1, x, y) if (g ^ 1) < size_g else (g, x, y)

    def index(g, x, y):
        return (g * size_x + x) * size_y + y

    return [
        (index(g, x, y), index(*partner(g, x, y)))
        for g in range(size_g)
        for x in range(size_x)
        for y in range(size_y)
    ]


def from_others(value, count):
    return [
        lax.ppermute(value, "grp", [(i, (i + k) % count) for i in range(count)])
        for k in range(1, count)
    ]


class Refs:
    def __init__(self, refs):
        self.refs = list(refs)

    def take(self, n):
        out, self.refs = self.refs[:n], self.refs[n:]
        return out


def pick(mine, others, k):
    value = mine
    for at, other in enumerate(others):
        value = jnp.where(k == at + 1, other, value)
    return value


def pack_sides(c, slot, left, right):
    lane = iota(c.shape, 1)
    left = jnp.where(lane == slot, turn(c, slot, 1), left)
    right = jnp.where(lane == slot, turn(c, slot + 1, 1), right)
    return left, right


def level_base(cells, count):
    return cells if count == 2 else SUB


def message_shapes(tracers, rows, cells, width, count):
    height = level_base(cells, count) + tracers * rows + SUB
    height += -height % SUB
    if count == 2:
        return [shape(height, width)]
    return [shape(cells, width), shape(height, width), shape(height, width)]


def write_levels(last, first, t, rows, cells, msgs, g):
    if len(msgs) == 1:
        msgs[0][pl.ds(cells + t * rows, rows), :] = jnp.where(g == 0, last[SUB - rows :], first[:rows])
    else:
        msgs[1][pl.ds(SUB + t * rows, rows), :] = last[SUB - rows :]
        msgs[2][pl.ds(SUB + t * rows, rows), :] = first[:rows]


def raw_kernel(rows, *refs):
    *fields, depth_hbm, solar_hbm, out_ref, depth_ref, solar_ref, depth_s, solar_s, sems = refs
    copies = [pltpu.make_async_copy(f, out_ref.at[at], sems.at[at]) for at, f in enumerate(fields)]
    n = len(fields)
    copies.append(pltpu.make_async_copy(depth_hbm, depth_s, sems.at[n]))
    copies.append(pltpu.make_async_copy(solar_hbm, solar_s, sems.at[n + 1]))
    for copy in copies:
        copy.start()
    for copy in copies:
        copy.wait()
    for r in range(0, SUB, rows):
        depth_ref[pl.ds(r, rows), :] = depth_s[...]
        solar_ref[pl.ds(r, rows), :] = solar_s[...]


def chunks(n, parts):
    step = -(-n // parts)
    return [(a, min(step, n - a)) for a in range(0, n, step)]


def prep_kernel(rows, count, pig_ref, c_hbm, c_ref, *refs):
    *msgs, sems = refs
    g = lax.axis_index("grp")
    tracers, cells, _ = c_ref.shape
    cuts = chunks(tracers, sems.shape[0])
    copies = [
        pltpu.make_async_copy(c_hbm.at[pl.ds(a, n)], c_ref.at[pl.ds(a, n)], sems.at[i])
        for i, (a, n) in enumerate(cuts)
    ]
    for copy in copies:
        copy.start()
    pigment = jnp.zeros(c_ref.shape[1:], F32)
    for copy, (a, n) in zip(copies, cuts):
        copy.wait()
        for t in range(a, a + n):
            c = c_ref[t]
            pigment = pigment + pig_ref[t] * c
            write_levels(c[cells - SUB :], c[:SUB], t, rows, cells, msgs, g)
    msgs[0][pl.ds(0, cells), :] = pigment


def halves(v):
    high = v.astype(jnp.bfloat16)
    return high, (v - high.astype(F32)).astype(jnp.bfloat16)


def dot(a, b, **kw):
    return jnp.dot(a, b, preferred_element_type=F32, **kw)


def spread_rates(rates, tracers):
    exact = functools.partial(dot, precision=lax.Precision.HIGHEST)
    depth = tracers * SUB
    spread = jnp.where(iota((depth, tracers), 0) // SUB == iota((depth, tracers), 1), 1.0, 0.0)
    spread_t = jnp.where(iota((tracers, depth), 1) // SUB == iota((tracers, depth), 0), 1.0, 0.0)
    weights = exact(exact(spread, rates), spread_t)
    return jnp.where(
        lax.rem(iota((depth, depth), 0), SUB) == lax.rem(iota((depth, depth), 1), SUB), weights, 0.0
    )


def mix(weights, c_ref, mix_ref):
    tracers, cells, width = c_ref.shape
    w_high, w_low = halves(weights)
    for b in range(cells // SUB):
        here = pl.ds(b * SUB, SUB)
        c_high, c_low = halves(c_ref[:, here, :].reshape(tracers * SUB, width))
        mixed = dot(w_high, c_high) + (dot(w_high, c_low) + dot(w_low, c_high))
        mix_ref[:, here, :] = mixed.reshape(tracers, SUB, width)


def pack(rows, c_ref, pigment, msg_xa, msg_xb, msg_ya, msg_yb, p_s):
    tracers, cells, _ = c_ref.shape
    levels = cells // rows
    x_even = lax.rem(lax.axis_index("gx"), 2) == 0
    y_even = lax.rem(lax.axis_index("gy"), 2) == 0
    p_s[...] = pigment
    left = right = jnp.zeros(c_ref.shape[1:], F32)
    left, right = pack_sides(pigment, tracers + 2, left, right)
    for t in range(tracers):
        left, right = pack_sides(c_ref[t], t, left, right)
    msg_xa[...] = jnp.where(x_even, right, left)
    msg_xb[...] = jnp.where(x_even, left, right)

    def put(slot, first, last):
        msg_ya[slot] = jnp.where(y_even, last, first)
        msg_yb[slot] = jnp.where(y_even, first, last)

    for t in range(tracers):
        put(
            t,
            c_ref[t, pl.ds(0, levels, stride=rows), :],
            c_ref[t, pl.ds(rows - 1, levels, stride=rows), :],
        )
    put(
        tracers + 2,
        p_s[pl.ds(0, levels, stride=rows), :],
        p_s[pl.ds(rows - 1, levels, stride=rows), :],
    )


def pack_kernel(rows, *refs):
    c_ref, rates_ref, p_msg, msg_xa, msg_xb, msg_ya, msg_yb, w_ref, mix_ref, p_s = refs
    tracers, cells, _ = c_ref.shape
    pack(rows, c_ref, p_msg[pl.ds(0, cells), :], msg_xa, msg_xb, msg_ya, msg_yb, p_s)
    weights = spread_rates(rates_ref[...], tracers)
    w_ref[...] = weights
    mix(weights, c_ref, mix_ref)


def ocean_kernel(rows, count, tracers, first_step, *refs):
    refs = Refs(refs)
    depth_ref, solar_ref = refs.take(2)
    in_xa, in_xb, in_ya, in_yb = refs.take(4)
    p_own, *p_others = refs.take(count)
    if first_step:
        own_fields, *other_fields = refs.take(count)
    else:
        fields = refs.take(5)
    band_ref, msg_xa, msg_xb, msg_ya, msg_yb = refs.take(5)
    full_out = refs.take(5 if first_step else 4)
    (p_full,) = refs.take(1)
    if first_step:
        fields = refs.take(5)
    face_s, par_s, wet_s = refs.take(3)
    g = lax.axis_index("grp")
    cells, width = in_xa.shape
    levels = cells // rows
    total = count * cells
    all_levels = total // rows
    strip = rows // count

    for b in range(count):
        k = lax.rem(g - b + count, count)
        p_full[pl.ds(b * cells, cells), :] = pick(
            p_own[pl.ds(0, cells), :], [o[pl.ds(0, cells), :] for o in p_others], k
        )
    if first_step:
        for at in range(5):
            for s in range(count):
                k = lax.rem(g - s + count, count)
                for r in range(strip):
                    here = pl.ds(r, all_levels, stride=strip)
                    fields[at][pl.ds(s * strip + r, all_levels, stride=rows), :] = pick(
                        own_fields[at, here, :], [o[at, here, :] for o in other_fields], k
                    )

    def spread(ref):
        return jnp.broadcast_to(ref[...][None], (total // SUB, SUB, width)).reshape(total, width)

    row = iota((total, width), 0)
    wet = jnp.where(row // rows < spread(depth_ref), 1.0, 0.0)
    att = WATER_ATTEN + PIGMENT_ATTEN * p_full[...]
    summed = att
    step = rows
    while step < total:
        summed = summed + jnp.where(row >= step, turn(summed, step, 0), 0.0)
        step *= 2
    top = spread(solar_ref) * jnp.exp(att - summed)
    par = top * jnp.exp(-0.5 * att)
    east, north, temp, sal, mixing = [f[...] for f in fields]
    temp = temp + WARMING_UPTAKE * (top * (1.0 - jnp.exp(-att))) * wet

    def below(v):
        return turn(v, -rows, 0)

    density = SALT_EXPANSION * sal - WARM_EXPANSION * temp
    face = 0.5 * (mixing + below(mixing)) + CONVECT_MIX / (1.0 + jnp.exp(below(density) - density))
    face = jnp.where(row < total - rows, face * below(wet), 0.0)

    def stir(v):
        flux = face * (below(v) - v)
        return v + flux - turn(flux, rows, 0)

    for at, v in enumerate((east, north, temp, sal)):
        full_out[at][...] = stir(v)
    if first_step:
        full_out[4][...] = mixing
    face_s[...] = face
    par_s[...] = par
    wet_s[...] = wet

    band = pl.ds(pl.multiple_of(g * cells, SUB), cells)
    above = pl.ds(pl.multiple_of(lax.max(g * cells - SUB, 0), SUB), SUB)
    face_band = face_s[band, :]
    lifted = turn(jnp.concatenate([face_s[above, :], face_band], axis=0), rows, 0)[SUB:]
    lifted = jnp.where((iota((cells, width), 0) < rows) & (g == 0), 0.0, lifted)
    u = full_out[0][band, :]
    wet_band = wet_s[band, :]
    band_ref[0] = u
    band_ref[1] = full_out[1][band, :]
    band_ref[2] = full_out[2][band, :]
    band_ref[3] = face_band
    band_ref[4] = lifted
    band_ref[5] = par_s[band, :]
    band_ref[6] = wet_band

    x_even = lax.rem(lax.axis_index("gx"), 2) == 0
    y_even = lax.rem(lax.axis_index("gy"), 2) == 0
    xa, xb = in_xa[...], in_xb[...]
    left, right = jnp.where(x_even, xb, xa), jnp.where(x_even, xa, xb)
    left, right = pack_sides(wet_band, tracers + 1, left, right)
    _, right = pack_sides(u, tracers, left, right)
    msg_xa[...] = jnp.where(x_even, right, left)
    msg_xb[...] = jnp.where(x_even, left, right)
    for t in (*range(tracers), tracers + 2):
        msg_ya[t] = in_ya[t]
        msg_yb[t] = in_yb[t]
    speed = band_ref[1, pl.ds(rows - 1, levels, stride=rows), :]
    wet_first = band_ref[6, pl.ds(0, levels, stride=rows), :]
    wet_last = band_ref[6, pl.ds(rows - 1, levels, stride=rows), :]
    msg_ya[tracers] = speed
    msg_yb[tracers] = speed
    msg_ya[tracers + 1] = jnp.where(y_even, wet_last, wet_first)
    msg_yb[tracers + 1] = jnp.where(y_even, wet_first, wet_last)


def own_strip_kernel(rows, count, *refs):
    refs = Refs(refs)
    full, outs, strips = refs.take(4), refs.take(4), refs.take(4)
    (sems,) = refs.take(1)
    g = lax.axis_index("grp")
    strip = rows // count
    all_levels = full[0].shape[0] // rows
    copies = [pltpu.make_async_copy(strips[at], outs[at], sems.at[at]) for at in range(4)]
    for at in range(4):
        for r in range(strip):
            value = full[at][pl.ds(r, all_levels, stride=rows), :]
            for s in range(1, count):
                value = jnp.where(g == s, full[at][pl.ds(s * strip + r, all_levels, stride=rows), :], value)
            strips[at][pl.ds(r, all_levels, stride=strip), :] = value
        copies[at].start()
    for copy in copies:
        copy.wait()


def inner_kernel(rows, count, last_step, *refs):
    refs = Refs(refs)
    photo_ref, sat_ref, pig_ref, c_ref, mix_ref, band_ref = refs.take(6)
    lev_in = refs.take(1 if count == 2 else 2)
    (part_ref,) = refs.take(1)
    p_part = None if last_step else refs.take(1)[0]
    tracers, cells, width = c_ref.shape
    k_d = band_ref[3]
    k_u = band_ref[4]
    k_c = 1.0 - k_d - k_u
    par = band_ref[5]
    lit = TIME_STEP * band_ref[6]
    warm = lit * jnp.exp(WARMING_FACTOR * (band_ref[2] - 20.0))
    lit = lit * par
    pigment = jnp.zeros((cells, width), F32)
    for t in range(tracers):
        c = c_ref[t]
        at = level_base(cells, count) + t * rows
        up8 = lev_in[0][pl.ds(at + rows - SUB, SUB), :]
        down8 = lev_in[-1][pl.ds(at, SUB), :]
        c_u = turn(jnp.concatenate([up8, c], axis=0), rows, 0)[SUB:]
        c_d = turn(jnp.concatenate([c, down8], axis=0), -rows, 0)[:cells]
        part = (
            (k_c + photo_ref[t] * (lit / (par + sat_ref[t]))) * c + k_u * c_u + k_d * c_d + warm * mix_ref[t]
        )
        part_ref[t] = part
        if not last_step:
            pigment = pigment + pig_ref[t] * part
    if not last_step:
        p_part[...] = pigment


class Sides:
    def __init__(self, rows, cells, width, got, spread_s):
        got_xa, got_xb, self.got_ya, self.got_yb = got
        self.rows, self.spread_s = rows, spread_s
        x_even = lax.rem(lax.axis_index("gx"), 2) == 0
        self.y_even = lax.rem(lax.axis_index("gy"), 2) == 0
        self.west = jnp.where(x_even, got_xb[...], got_xa[...])
        self.east = jnp.where(x_even, got_xa[...], got_xb[...])
        self.lane = iota((cells, width), 1)
        self.at_row = lax.rem(iota((cells, width), 0), rows)
        self.levels = cells // rows

    def columns(self, v, slot):
        last = v.shape[1] - 1
        return (
            jnp.where(self.lane == 0, turn(self.west, -slot, 1), turn(v, 1, 1)),
            jnp.where(self.lane == last, turn(self.east, -1 - slot, 1), turn(v, -1, 1)),
        )

    def spread(self, slot):
        ya, yb = self.got_ya[slot], self.got_yb[slot]
        self.spread_s[slot, pl.ds(0, self.levels, stride=self.rows), :] = jnp.where(self.y_even, yb, ya)
        self.spread_s[slot, pl.ds(self.rows - 1, self.levels, stride=self.rows), :] = jnp.where(
            self.y_even, ya, yb
        )

    def rows_of(self, v, slot):
        outer = self.spread_s[slot]
        return (
            jnp.where(self.at_row == 0, outer, turn(v, 1, 0)),
            jnp.where(self.at_row == self.rows - 1, outer, turn(v, -1, 0)),
        )


def side_coefficients(sides, band_ref, tracers, sizes):
    _, size_x, size_y = sizes
    x = lax.axis_index("gx")
    y = lax.axis_index("gy")
    lane, at_row = sides.lane, sides.at_row
    u = band_ref[0]
    v = band_ref[1]
    wet = band_ref[6]
    wet_w, wet_e = sides.columns(wet, tracers + 1)
    wet_s, wet_n = sides.rows_of(wet, tracers + 1)
    open_w = wet * jnp.where((lane == 0) & (x == 0), 0.0, wet_w)
    open_e = wet * jnp.where((lane == wet.shape[1] - 1) & (x == size_x - 1), 0.0, wet_e)
    open_s = wet * jnp.where((at_row == 0) & (y == 0), 0.0, wet_s)
    open_n = wet * jnp.where((at_row == sides.rows - 1) & (y == size_y - 1), 0.0, wet_n)

    def lower(opening, speed):
        return opening * (jnp.maximum(speed, 0.0) + SIDE_DIFFUSE)

    def upper(opening, speed):
        return opening * (jnp.minimum(speed, 0.0) - SIDE_DIFFUSE)

    u_w, _ = sides.columns(u, tracers)
    v_s, _ = sides.rows_of(v, tracers)
    k_h = upper(open_w, u_w) - lower(open_e, u) + upper(open_s, v_s) - lower(open_n, v)
    return lower(open_w, u_w), -upper(open_e, u), lower(open_s, v_s), -upper(open_n, v), k_h


def sideways(sides, factors, v, slot):
    k_w, k_e, k_s, k_n, k_h = factors
    v_w, v_e = sides.columns(v, slot)
    v_s, v_n = sides.rows_of(v, slot)
    return (k_w * v_w + k_e * v_e) + (k_s * v_s + k_n * v_n) + k_h * v


def early_kernel(rows, count, sizes, *refs):
    refs = Refs(refs)
    c_ref, band_ref = refs.take(2)
    got = refs.take(4)
    p_msg, part_ref, p_part = refs.take(3)
    k_ref, spread_s = refs.take(2)
    msgs = refs.take(1 if count == 2 else 3)
    g = lax.axis_index("grp")
    tracers, cells, width = c_ref.shape
    sides = Sides(rows, cells, width, got, spread_s)
    for slot in range(tracers + 3):
        sides.spread(slot)
    factors = side_coefficients(sides, band_ref, tracers, sizes)
    for at, k in enumerate(factors):
        k_ref[at] = k
    msgs[0][pl.ds(0, cells), :] = p_part[...] + sideways(sides, factors, p_msg[pl.ds(0, cells), :], tracers + 2)

    lane = sides.lane[:SUB]
    at_row = sides.at_row[:SUB]

    def block(at, outermost, t):
        k_w, k_e, k_s, k_n, k_h = [k_ref[i, pl.ds(at, SUB), :] for i in range(5)]
        v = c_ref[t, pl.ds(at, SUB), :]
        outer = spread_s[t, pl.ds(at, SUB), :]
        v_w = jnp.where(lane == 0, turn(sides.west[at : at + SUB], -t, 1), turn(v, 1, 1))
        v_e = jnp.where(lane == width - 1, turn(sides.east[at : at + SUB], -1 - t, 1), turn(v, -1, 1))
        v_s = jnp.where(at_row == 0, outer, turn(v, 1, 0))
        v_n = jnp.where(at_row == rows - 1, outer, turn(v, -1, 0))
        side = (k_w * v_w + k_e * v_e) + (k_s * v_s + k_n * v_n) + k_h * v
        return part_ref[t, pl.ds(at, SUB), :] + side

    for t in range(tracers):
        write_levels(block(cells - SUB, True, t), block(0, False, t), t, rows, cells, msgs, g)


def step_kernel(rows, *refs):
    refs = Refs(refs)
    c_ref, part_ref, k_ref, spread_s = refs.take(4)
    got_xa, got_xb = refs.take(2)
    w_ref, p_msg = refs.take(2)
    out_ref, msg_xa, msg_xb, msg_ya, msg_yb, mix_ref, p_s = refs.take(7)
    tracers, cells, width = c_ref.shape
    sides = Sides(rows, cells, width, (got_xa, got_xb, None, None), spread_s)
    factors = [k_ref[i] for i in range(5)]
    for t in range(tracers):
        out_ref[t] = part_ref[t] + sideways(sides, factors, c_ref[t], t)
    pack(rows, out_ref, p_msg[pl.ds(0, cells), :], msg_xa, msg_xb, msg_ya, msg_yb, p_s)
    mix(w_ref[...], out_ref, mix_ref)


def final_kernel(rows, sizes, *refs):
    refs = Refs(refs)
    c_ref, part_ref, band_ref = refs.take(3)
    got = refs.take(4)
    out_hbm, spread_s, new_s, sems = refs.take(4)
    tracers, cells, width = c_ref.shape
    sides = Sides(rows, cells, width, got, spread_s)
    for slot in (tracers, tracers + 1):
        sides.spread(slot)
    factors = side_coefficients(sides, band_ref, tracers, sizes)
    copies = []
    for i, (a, n) in enumerate(chunks(tracers, sems.shape[0])):
        for t in range(a, a + n):
            sides.spread(t)
            new_s[t] = part_ref[t] + sideways(sides, factors, c_ref[t], t)
        copies.append(pltpu.make_async_copy(new_s.at[pl.ds(a, n)], out_hbm.at[pl.ds(a, n)], sems.at[i]))
        copies[-1].start()
    for copy in copies:
        copy.wait()


def call(kernel, ins, outs, in_specs=None, out_specs=None, scratch=(), flops=1 << 20):
    return pl.pallas_call(
        kernel,
        in_specs=[vmem() for _ in ins] if in_specs is None else in_specs,
        out_specs=[vmem() for _ in outs] if out_specs is None else out_specs,
        out_shape=outs,
        scratch_shapes=list(scratch),
        compiler_params=pltpu.CompilerParams(vmem_limit_bytes=VMEM_LIMIT),
        cost_estimate=pl.CostEstimate(flops=flops, bytes_accessed=1 << 20, transcendentals=0),
    )(*ins)


def per_device(
    sizes,
    zonal_boundary_speed,
    meridional_boundary_speed,
    potential_warmth,
    saltiness_field,
    quiescent_mixing_profile,
    substance_amounts,
    submerged_layer_number,
    solar_radiation,
    interaction_rates,
    photosynthetic_rates,
    saturation_irradiance,
    pigment_per_tracer,
):
    count = sizes[0]
    result_dimensions = zonal_boundary_speed.shape
    all_levels, _, strip, width = result_dimensions
    tracers, levels, rows, _ = substance_amounts.shape
    cells = levels * rows
    total = all_levels * rows
    strip_cells = all_levels * strip
    dma = pltpu.SemaphoreType.DMA
    column = pltpu.VMEM((total, width), F32)
    band_s = pltpu.VMEM((cells, width), F32)
    params = [photosynthetic_rates, saturation_irradiance, pigment_per_tracer]

    own = [
        f.reshape(strip_cells, width)
        for f in (
            zonal_boundary_speed,
            meridional_boundary_speed,
            potential_warmth,
            saltiness_field,
            quiescent_mixing_profile,
        )
    ]
    surface = [submerged_layer_number, solar_radiation]
    raw, depth, solar = call(
        functools.partial(raw_kernel, rows),
        own + surface,
        [shape(5, strip_cells, width), jax.ShapeDtypeStruct((SUB, width), jnp.int32), shape(SUB, width)],
        in_specs=[hbm()] * 7,
        scratch=[pltpu.VMEM((rows, width), jnp.int32), pltpu.VMEM((rows, width), F32), dma((7,))],
    )
    raw_others = from_others(raw, count)

    msg_levels = message_shapes(tracers, rows, cells, width, count)
    cols = shape(cells, width)
    lines = shape(tracers + 3, levels, width)
    sides = [cols, cols, lines, lines]
    field = shape(tracers, cells, width)
    c, *msgs = call(
        functools.partial(prep_kernel, rows, count),
        [pigment_per_tracer, substance_amounts.reshape(tracers, cells, width)],
        [field, *msg_levels],
        in_specs=[smem(), hbm()],
        scratch=[dma((4,))],
    )
    full = None
    for step in range(STEPS):
        first_step, last_step = step == 0, step == STEPS - 1
        p_others = from_others(msgs[0], count)
        if count == 2:
            lev = p_others
        else:
            lev = [
                lax.ppermute(msgs[1], "grp", [(i, (i + 1) % count) for i in range(count)]),
                lax.ppermute(msgs[2], "grp", [((i + 1) % count, i) for i in range(count)]),
            ]
        if first_step:
            xa, xb, ya, yb, weights, mixed = call(
                functools.partial(pack_kernel, rows),
                [c, interaction_rates, msgs[0]],
                [*sides, shape(tracers * SUB, tracers * SUB), field],
                scratch=[band_s],
                flops=1 << 24,
            )
        band, xa, xb, ya, yb, *full = call(
            functools.partial(ocean_kernel, rows, count, tracers, first_step),
            [depth, solar, xa, xb, ya, yb, msgs[0], *p_others, *([raw, *raw_others] if first_step else full)],
            [shape(7, cells, width), *sides, *[shape(total, width)] * (5 if first_step else 4)],
            scratch=[column] * (9 if first_step else 4),
        )
        xa = lax.ppermute(xa, AXES, pairing(sizes, "gx", 0))
        xb = lax.ppermute(xb, AXES, pairing(sizes, "gx", 1))
        ya = lax.ppermute(ya, AXES, pairing(sizes, "gy", 0))
        yb = lax.ppermute(yb, AXES, pairing(sizes, "gy", 1))
        part, *p_part = call(
            functools.partial(inner_kernel, rows, count, last_step),
            [*params, c, mixed, band, *lev],
            [field] + ([] if last_step else [cols]),
            in_specs=[smem()] * 3 + [vmem()] * (3 + len(lev)),
            flops=1 << 24,
        )
        if not last_step:
            k, spread, *msgs_next = call(
                functools.partial(early_kernel, rows, count, sizes),
                [c, band, xa, xb, ya, yb, msgs[0], part, *p_part],
                [shape(5, cells, width), shape(tracers + 3, cells, width), *msg_levels],
            )
            c, xa, xb, ya, yb, mixed = call(
                functools.partial(step_kernel, rows),
                [c, part, k, spread, xa, xb, weights, msgs_next[0]],
                [field, *sides, field],
                scratch=[band_s],
                flops=1 << 24,
            )
            msgs = msgs_next
        else:
            outs = call(
                functools.partial(own_strip_kernel, rows, count),
                full,
                [shape(strip_cells, width)] * 4,
                out_specs=[hbm()] * 4,
                scratch=[pltpu.VMEM((strip_cells, width), F32)] * 4 + [dma((4,))],
                flops=1 << 24,
            )
            (c,) = call(
                functools.partial(final_kernel, rows, sizes),
                [c, part, band, xa, xb, ya, yb],
                [field],
                out_specs=[hbm()],
                scratch=[
                    pltpu.VMEM((tracers + 3, cells, width), F32),
                    pltpu.VMEM((tracers, cells, width), F32),
                    dma((5,)),
                ],
            )
    return tuple(f.reshape(result_dimensions) for f in outs) + (c.reshape(substance_amounts.shape),)


def solution(mesh):
    ocean = P(None, "gy", "grp", "gx")
    tracer = P(None, "grp", "gy", "gx")
    surface = P("gy", "gx")
    sizes = tuple(mesh.shape[a] for a in AXES)
    return jax.shard_map(
        functools.partial(per_device, sizes),
        mesh=mesh,
        in_specs=(ocean,) * 5 + (tracer, surface, surface) + (P(),) * 4,
        out_specs=(ocean,) * 4 + (tracer,),
        check_vma=False,
    )
```

```python
import functools

import jax
import jax.numpy as jnp
from jax import lax
from jax.experimental import pallas as pl
from jax.experimental.pallas import tpu as pltpu
from jax.sharding import PartitionSpec as P

STEPS = 2

WATER_ATTEN = 0.01
PIGMENT_ATTEN = 0.05
WARMING_UPTAKE = 5.0
WARM_EXPANSION = 0.2
SALT_EXPANSION = 0.8
CONVECT_MIX = 0.15
SIDE_DIFFUSE = 0.05
WARMING_FACTOR = 0.0633
TIME_STEP = 0.5

SUB = 8
AXES = ("grp", "gx", "gy")
VMEM_LIMIT = 48 * 1024 * 1024

F32 = jnp.float32


def vmem():
    return pl.BlockSpec(memory_space=pltpu.VMEM)


def hbm():
    return pl.BlockSpec(memory_space=pltpu.HBM)


def smem():
    return pl.BlockSpec(memory_space=pltpu.SMEM)


def shape(*dims):
    return jax.ShapeDtypeStruct(dims, F32)


def turn(x, shift, axis):
    shift = shift % x.shape[axis]
    return x if shift == 0 else pltpu.roll(x, shift, axis)


def iota(x, axis):
    return lax.broadcasted_iota(jnp.int32, x, axis)


def pairing(sizes, axis, odd):
    size_g, size_x, size_y = sizes

    def partner(g, x, y):
        i, n = (x, size_x) if axis == "gx" else (y, size_y)
        j = i + 1 if i % 2 == odd else i - 1
        if 0 <= j < n:
            return (g, j, y) if axis == "gx" else (g, x, j)
        if axis == "gx":
            return (g, x, y ^ 1) if (y ^ 1) < size_y else (g, x, y)
        return (g ^ 1, x, y) if (g ^ 1) < size_g else (g, x, y)

    def index(g, x, y):
        return (g * size_x + x) * size_y + y

    return [
        (index(g, x, y), index(*partner(g, x, y)))
        for g in range(size_g)
        for x in range(size_x)
        for y in range(size_y)
    ]


def from_others(value, count):
    return [
        lax.ppermute(value, "grp", [(i, (i + k) % count) for i in range(count)])
        for k in range(1, count)
    ]


def chunks(n, parts):
    step = -(-n // parts)
    return [(a, min(step, n - a)) for a in range(0, n, step)]


class Refs:
    def __init__(self, refs):
        self.refs = list(refs)

    def take(self, n):
        out, self.refs = self.refs[:n], self.refs[n:]
        return out


def pick(mine, others, k):
    value = mine
    for at, other in enumerate(others):
        value = jnp.where(k == at + 1, other, value)
    return value


def pack_sides(c, slot, left, right):
    lane = iota(c.shape, 1)
    left = jnp.where(lane == slot, turn(c, slot, 1), left)
    right = jnp.where(lane == slot, turn(c, slot + 1, 1), right)
    return left, right


def level_base(cells, count):
    return cells if count == 2 else SUB


def message_shapes(tracers, rows, cells, width, count):
    height = level_base(cells, count) + tracers * rows + (SUB - rows)
    height += -height % SUB
    if count == 2:
        return [shape(height, width)]
    return [shape(cells, width), shape(height, width), shape(height, width)]


def write_levels(last, first, t, rows, cells, msgs, g):
    if len(msgs) == 1:
        msgs[0][pl.ds(cells + t * rows, rows), :] = jnp.where(g == 0, last[SUB - rows :], first[:rows])
    else:
        msgs[1][pl.ds(SUB + t * rows, rows), :] = last[SUB - rows :]
        msgs[2][pl.ds(SUB + t * rows, rows), :] = first[:rows]


def raw_window(rows, count, strip_cells, member):
    if count != 2:
        return 0, strip_cells
    height = strip_cells // 2 + SUB
    return member * (strip_cells - height), height


def window_kernel(rows, count, raw_ref, out_ref):
    g = lax.axis_index("grp")
    low, height = raw_window(rows, count, raw_ref.shape[1], lax.rem(g + 1, count))
    if count == 2:
        low = pl.multiple_of(low, SUB)
    for at in range(raw_ref.shape[0]):
        out_ref[at] = raw_ref[at, pl.ds(low, height), :]


def prep_kernel(rows, count, pig_ref, c_ref, *msgs):
    g = lax.axis_index("grp")
    tracers, cells, _ = c_ref.shape
    pigment = jnp.zeros(c_ref.shape[1:], F32)
    for t in range(tracers):
        c = c_ref[t]
        pigment = pigment + pig_ref[t] * c
        write_levels(c[cells - SUB :], c[:SUB], t, rows, cells, msgs, g)
    msgs[0][pl.ds(0, cells), :] = pigment


def halves(v):
    high = v.astype(jnp.bfloat16)
    return high, (v - high.astype(F32)).astype(jnp.bfloat16)


def dot(a, b, **kw):
    return jnp.dot(a, b, preferred_element_type=F32, **kw)


def spread_rates(rates, tracers):
    exact = functools.partial(dot, precision=lax.Precision.HIGHEST)
    depth = tracers * SUB
    spread = jnp.where(iota((depth, tracers), 0) // SUB == iota((depth, tracers), 1), 1.0, 0.0)
    spread_t = jnp.where(iota((tracers, depth), 1) // SUB == iota((tracers, depth), 0), 1.0, 0.0)
    weights = exact(exact(spread, rates), spread_t)
    return jnp.where(
        lax.rem(iota((depth, depth), 0), SUB) == lax.rem(iota((depth, depth), 1), SUB), weights, 0.0
    )


def mix(weights, c_ref, mix_ref):
    tracers, cells, width = c_ref.shape
    w_high, w_low = halves(weights)
    for b in range(cells // SUB):
        here = pl.ds(b * SUB, SUB)
        c_high, c_low = halves(c_ref[:, here, :].reshape(tracers * SUB, width))
        mixed = dot(w_high, c_high) + (dot(w_high, c_low) + dot(w_low, c_high))
        mix_ref[:, here, :] = mixed.reshape(tracers, SUB, width)


def pack(rows, c_ref, pigment, msg_xa, msg_xb, msg_ya, msg_yb, p_s):
    tracers, cells, _ = c_ref.shape
    levels = cells // rows
    x_even = lax.rem(lax.axis_index("gx"), 2) == 0
    y_even = lax.rem(lax.axis_index("gy"), 2) == 0
    p_s[...] = pigment
    left = right = jnp.zeros(c_ref.shape[1:], F32)
    left, right = pack_sides(pigment, tracers + 2, left, right)
    for t in range(tracers):
        left, right = pack_sides(c_ref[t], t, left, right)
    msg_xa[...] = jnp.where(x_even, right, left)
    msg_xb[...] = jnp.where(x_even, left, right)

    def put(slot, first, last):
        msg_ya[slot] = jnp.where(y_even, last, first)
        msg_yb[slot] = jnp.where(y_even, first, last)

    for t in range(tracers):
        put(
            t,
            c_ref[t, pl.ds(0, levels, stride=rows), :],
            c_ref[t, pl.ds(rows - 1, levels, stride=rows), :],
        )
    put(
        tracers + 2,
        p_s[pl.ds(0, levels, stride=rows), :],
        p_s[pl.ds(rows - 1, levels, stride=rows), :],
    )


def pack_kernel(rows, *refs):
    refs = Refs(refs)
    photo_ref, sat_ref, depth_in, solar_in, c_ref, rates_ref, p_msg = refs.take(7)
    msg_xa, msg_xb, msg_ya, msg_yb, w_ref, mix_ref, tiles_ref, depth_ref, solar_ref, p_s = refs.take(10)
    tracers, cells, width = c_ref.shape
    for r in range(0, SUB, rows):
        depth_ref[pl.ds(r, rows), :] = depth_in[...]
        solar_ref[pl.ds(r, rows), :] = solar_in[...]
    for t in range(tracers):
        tiles_ref[0, t] = jnp.full((SUB, width), photo_ref[t], F32)
        tiles_ref[1, t] = jnp.full((SUB, width), sat_ref[t], F32)
    pack(rows, c_ref, p_msg[pl.ds(0, cells), :], msg_xa, msg_xb, msg_ya, msg_yb, p_s)
    weights = spread_rates(rates_ref[...], tracers)
    w_ref[...] = weights
    mix(weights, c_ref, mix_ref)


def ocean_kernel(rows, count, tracers, first_step, *refs):
    refs = Refs(refs)
    depth_ref, solar_ref = refs.take(2)
    in_xa, in_xb, in_ya, in_yb = refs.take(4)
    p_own, *p_others = refs.take(count)
    if first_step:
        own_fields, *other_fields = refs.take(count)
    else:
        fields = refs.take(5)
    band_ref, msg_xa, msg_xb, msg_ya, msg_yb = refs.take(5)
    full_out = refs.take(5 if first_step else 4)
    (p_full,) = refs.take(1)
    if first_step:
        fields = refs.take(5)
        other_s = refs.take(5 * (count - 1))
    face_s, par_s, wet_s = refs.take(3)
    g = lax.axis_index("grp")
    cells, width = in_xa.shape
    levels = cells // rows
    total = count * cells
    all_levels = total // rows
    strip = rows // count

    for b in range(count):
        k = lax.rem(g - b + count, count)
        p_full[pl.ds(b * cells, cells), :] = pick(
            p_own[pl.ds(0, cells), :], [o[pl.ds(0, cells), :] for o in p_others], k
        )
    if first_step:
        low, height = raw_window(rows, count, all_levels * strip, g)
        if count == 2:
            low = pl.multiple_of(low, SUB)
        for at in range(5):
            for k in range(count - 1):
                other_s[5 * k + at][...] = jnp.zeros((all_levels * strip, width), F32)
                other_s[5 * k + at][pl.ds(low, height), :] = other_fields[k][at]
            for s in range(count):
                k = lax.rem(g - s + count, count)
                for r in range(strip):
                    here = pl.ds(r, all_levels, stride=strip)
                    fields[at][pl.ds(s * strip + r, all_levels, stride=rows), :] = pick(
                        own_fields[at, here, :], [other_s[5 * j + at][here, :] for j in range(count - 1)], k
                    )

    def spread(ref):
        return jnp.broadcast_to(ref[...][None], (total // SUB, SUB, width)).reshape(total, width)

    row = iota((total, width), 0)
    wet = jnp.where(row // rows < spread(depth_ref), 1.0, 0.0)
    att = WATER_ATTEN + PIGMENT_ATTEN * p_full[...]
    summed = att
    step = rows
    while step < total:
        summed = summed + jnp.where(row >= step, turn(summed, step, 0), 0.0)
        step *= 2
    top = spread(solar_ref) * jnp.exp(att - summed)
    par = top * jnp.exp(-0.5 * att)
    east, north, temp, sal, mixing = [f[...] for f in fields]
    temp = temp + WARMING_UPTAKE * (top * (1.0 - jnp.exp(-att))) * wet

    def below(v):
        return turn(v, -rows, 0)

    density = SALT_EXPANSION * sal - WARM_EXPANSION * temp
    face = 0.5 * (mixing + below(mixing)) + CONVECT_MIX / (1.0 + jnp.exp(below(density) - density))
    face = jnp.where(row < total - rows, face * below(wet), 0.0)

    def stir(v):
        flux = face * (below(v) - v)
        return v + flux - turn(flux, rows, 0)

    for at, v in enumerate((east, north, temp, sal)):
        full_out[at][...] = stir(v)
    if first_step:
        full_out[4][...] = mixing
    face_s[...] = face
    par_s[...] = par
    wet_s[...] = wet

    band = pl.ds(pl.multiple_of(g * cells, SUB), cells)
    above = pl.ds(pl.multiple_of(lax.max(g * cells - SUB, 0), SUB), SUB)
    face_band = face_s[band, :]
    lifted = turn(jnp.concatenate([face_s[above, :], face_band], axis=0), rows, 0)[SUB:]
    lifted = jnp.where((iota((cells, width), 0) < rows) & (g == 0), 0.0, lifted)
    u = full_out[0][band, :]
    wet_band = wet_s[band, :]
    band_ref[0] = u
    band_ref[1] = full_out[1][band, :]
    band_ref[2] = full_out[2][band, :]
    band_ref[3] = face_band
    band_ref[4] = lifted
    band_ref[5] = par_s[band, :]
    band_ref[6] = wet_band

    x_even = lax.rem(lax.axis_index("gx"), 2) == 0
    y_even = lax.rem(lax.axis_index("gy"), 2) == 0
    xa, xb = in_xa[...], in_xb[...]
    left, right = jnp.where(x_even, xb, xa), jnp.where(x_even, xa, xb)
    left, right = pack_sides(wet_band, tracers + 1, left, right)
    _, right = pack_sides(u, tracers, left, right)
    msg_xa[...] = jnp.where(x_even, right, left)
    msg_xb[...] = jnp.where(x_even, left, right)
    for t in (*range(tracers), tracers + 2):
        msg_ya[t] = in_ya[t]
        msg_yb[t] = in_yb[t]
    speed = band_ref[1, pl.ds(rows - 1, levels, stride=rows), :]
    wet_first = band_ref[6, pl.ds(0, levels, stride=rows), :]
    wet_last = band_ref[6, pl.ds(rows - 1, levels, stride=rows), :]
    msg_ya[tracers] = speed
    msg_yb[tracers] = speed
    msg_ya[tracers + 1] = jnp.where(y_even, wet_last, wet_first)
    msg_yb[tracers + 1] = jnp.where(y_even, wet_first, wet_last)


def own_strip_kernel(rows, count, *refs):
    refs = Refs(refs)
    full, outs, strips = refs.take(4), refs.take(4), refs.take(4)
    (sems,) = refs.take(1)
    g = lax.axis_index("grp")
    strip = rows // count
    all_levels = full[0].shape[0] // rows
    copies = [pltpu.make_async_copy(strips[at], outs[at], sems.at[at]) for at in range(4)]
    for at in range(4):
        for r in range(strip):
            value = full[at][pl.ds(r, all_levels, stride=rows), :]
            for s in range(1, count):
                value = jnp.where(g == s, full[at][pl.ds(s * strip + r, all_levels, stride=rows), :], value)
            strips[at][pl.ds(r, all_levels, stride=strip), :] = value
        copies[at].start()
    for copy in copies:
        copy.wait()


def inner_kernel(rows, count, last_step, *refs):
    refs = Refs(refs)
    pig_ref, tiles_ref, c_ref, mix_ref, band_ref = refs.take(5)
    lev_in = refs.take(1 if count == 2 else 2)
    (part_ref,) = refs.take(1)
    p_part = None if last_step else refs.take(1)[0]
    tracers, cells, width = c_ref.shape
    k_d = band_ref[3]
    k_u = band_ref[4]
    k_c = 1.0 - k_d - k_u
    par = band_ref[5]
    lit = TIME_STEP * band_ref[6]
    warm = lit * jnp.exp(WARMING_FACTOR * (band_ref[2] - 20.0))
    lit = lit * par
    pigment = jnp.zeros((cells, width), F32)

    def tile(which, t):
        v = tiles_ref[which, t]
        return jnp.broadcast_to(v[None], (cells // SUB, SUB, width)).reshape(cells, width)

    for t in range(tracers):
        c = c_ref[t]
        at = level_base(cells, count) + t * rows
        up8 = lev_in[0][pl.ds(at + rows - SUB, SUB), :]
        down8 = lev_in[-1][pl.ds(at, SUB), :]
        c_u = turn(jnp.concatenate([up8, c], axis=0), rows, 0)[SUB:]
        c_d = turn(jnp.concatenate([c, down8], axis=0), -rows, 0)[:cells]
        part = (
            (k_c + tile(0, t) * (lit / (par + tile(1, t)))) * c + k_u * c_u + k_d * c_d + warm * mix_ref[t]
        )
        part_ref[t] = part
        if not last_step:
            pigment = pigment + pig_ref[t] * part
    if not last_step:
        p_part[...] = pigment


class Sides:
    def __init__(self, rows, cells, width, got, spread_s):
        got_xa, got_xb, self.got_ya, self.got_yb = got
        self.rows, self.spread_s = rows, spread_s
        x_even = lax.rem(lax.axis_index("gx"), 2) == 0
        self.y_even = lax.rem(lax.axis_index("gy"), 2) == 0
        self.west = jnp.where(x_even, got_xb[...], got_xa[...])
        self.east = jnp.where(x_even, got_xa[...], got_xb[...])
        self.lane = iota((cells, width), 1)
        self.at_row = lax.rem(iota((cells, width), 0), rows)
        self.levels = cells // rows

    def columns(self, v, slot):
        last = v.shape[1] - 1
        return (
            jnp.where(self.lane == 0, turn(self.west, -slot, 1), turn(v, 1, 1)),
            jnp.where(self.lane == last, turn(self.east, -1 - slot, 1), turn(v, -1, 1)),
        )

    def spread(self, slot):
        ya, yb = self.got_ya[slot], self.got_yb[slot]
        self.spread_s[slot, pl.ds(0, self.levels, stride=self.rows), :] = jnp.where(self.y_even, yb, ya)
        self.spread_s[slot, pl.ds(self.rows - 1, self.levels, stride=self.rows), :] = jnp.where(
            self.y_even, ya, yb
        )

    def rows_of(self, v, slot):
        outer = self.spread_s[slot]
        return (
            jnp.where(self.at_row == 0, outer, turn(v, 1, 0)),
            jnp.where(self.at_row == self.rows - 1, outer, turn(v, -1, 0)),
        )


def side_coefficients(sides, band_ref, tracers, sizes):
    _, size_x, size_y = sizes
    x = lax.axis_index("gx")
    y = lax.axis_index("gy")
    lane, at_row = sides.lane, sides.at_row
    u = band_ref[0]
    v = band_ref[1]
    wet = band_ref[6]
    wet_w, wet_e = sides.columns(wet, tracers + 1)
    wet_s, wet_n = sides.rows_of(wet, tracers + 1)
    open_w = wet * jnp.where((lane == 0) & (x == 0), 0.0, wet_w)
    open_e = wet * jnp.where((lane == wet.shape[1] - 1) & (x == size_x - 1), 0.0, wet_e)
    open_s = wet * jnp.where((at_row == 0) & (y == 0), 0.0, wet_s)
    open_n = wet * jnp.where((at_row == sides.rows - 1) & (y == size_y - 1), 0.0, wet_n)

    def lower(opening, speed):
        return opening * (jnp.maximum(speed, 0.0) + SIDE_DIFFUSE)

    def upper(opening, speed):
        return opening * (jnp.minimum(speed, 0.0) - SIDE_DIFFUSE)

    u_w, _ = sides.columns(u, tracers)
    v_s, _ = sides.rows_of(v, tracers)
    k_h = upper(open_w, u_w) - lower(open_e, u) + upper(open_s, v_s) - lower(open_n, v)
    return lower(open_w, u_w), -upper(open_e, u), lower(open_s, v_s), -upper(open_n, v), k_h


def sideways(sides, factors, v, slot):
    k_w, k_e, k_s, k_n, k_h = factors
    v_w, v_e = sides.columns(v, slot)
    v_s, v_n = sides.rows_of(v, slot)
    return (k_w * v_w + k_e * v_e) + (k_s * v_s + k_n * v_n) + k_h * v


def early_kernel(rows, count, sizes, *refs):
    refs = Refs(refs)
    c_ref, band_ref = refs.take(2)
    got = refs.take(4)
    p_msg, part_ref, p_part = refs.take(3)
    k_ref, spread_s = refs.take(2)
    msgs = refs.take(1 if count == 2 else 3)
    g = lax.axis_index("grp")
    tracers, cells, width = c_ref.shape
    sides = Sides(rows, cells, width, got, spread_s)
    for slot in range(tracers + 3):
        sides.spread(slot)
    factors = side_coefficients(sides, band_ref, tracers, sizes)
    for at, k in enumerate(factors):
        k_ref[at] = k
    msgs[0][pl.ds(0, cells), :] = p_part[...] + sideways(sides, factors, p_msg[pl.ds(0, cells), :], tracers + 2)

    lane = sides.lane[:SUB]
    at_row = sides.at_row[:SUB]

    def block(at, outermost, t):
        k_w, k_e, k_s, k_n, k_h = [k_ref[i, pl.ds(at, SUB), :] for i in range(5)]
        v = c_ref[t, pl.ds(at, SUB), :]
        outer = spread_s[t, pl.ds(at, SUB), :]
        v_w = jnp.where(lane == 0, turn(sides.west[at : at + SUB], -t, 1), turn(v, 1, 1))
        v_e = jnp.where(lane == width - 1, turn(sides.east[at : at + SUB], -1 - t, 1), turn(v, -1, 1))
        v_s = jnp.where(at_row == 0, outer, turn(v, 1, 0))
        v_n = jnp.where(at_row == rows - 1, outer, turn(v, -1, 0))
        side = (k_w * v_w + k_e * v_e) + (k_s * v_s + k_n * v_n) + k_h * v
        return part_ref[t, pl.ds(at, SUB), :] + side

    for t in range(tracers):
        write_levels(block(cells - SUB, True, t), block(0, False, t), t, rows, cells, msgs, g)


def step_kernel(rows, *refs):
    refs = Refs(refs)
    c_ref, part_ref, k_ref, spread_s = refs.take(4)
    got_xa, got_xb = refs.take(2)
    w_ref, p_msg = refs.take(2)
    out_ref, msg_xa, msg_xb, msg_ya, msg_yb, mix_ref, p_s = refs.take(7)
    tracers, cells, width = c_ref.shape
    sides = Sides(rows, cells, width, (got_xa, got_xb, None, None), spread_s)
    factors = [k_ref[i] for i in range(5)]
    for t in range(tracers):
        out_ref[t] = part_ref[t] + sideways(sides, factors, c_ref[t], t)
    pack(rows, out_ref, p_msg[pl.ds(0, cells), :], msg_xa, msg_xb, msg_ya, msg_yb, p_s)
    mix(w_ref[...], out_ref, mix_ref)


def final_kernel(rows, sizes, *refs):
    refs = Refs(refs)
    c_ref, part_ref, band_ref = refs.take(3)
    got = refs.take(4)
    out_hbm, spread_s, new_s, sems = refs.take(4)
    tracers, cells, width = c_ref.shape
    sides = Sides(rows, cells, width, got, spread_s)
    for slot in (tracers, tracers + 1):
        sides.spread(slot)
    factors = side_coefficients(sides, band_ref, tracers, sizes)
    copies = []
    for i, (a, n) in enumerate(chunks(tracers, sems.shape[0])):
        for t in range(a, a + n):
            sides.spread(t)
            new_s[t] = part_ref[t] + sideways(sides, factors, c_ref[t], t)
        copies.append(pltpu.make_async_copy(new_s.at[pl.ds(a, n)], out_hbm.at[pl.ds(a, n)], sems.at[i]))
        copies[-1].start()
    for copy in copies:
        copy.wait()


def call(kernel, ins, outs, in_specs=None, out_specs=None, scratch=(), flops=1 << 20, vmem_limit=VMEM_LIMIT):
    return pl.pallas_call(
        kernel,
        in_specs=[vmem() for _ in ins] if in_specs is None else in_specs,
        out_specs=[vmem() for _ in outs] if out_specs is None else out_specs,
        out_shape=outs,
        scratch_shapes=list(scratch),
        compiler_params=pltpu.CompilerParams(vmem_limit_bytes=vmem_limit),
        cost_estimate=pl.CostEstimate(flops=flops, bytes_accessed=1 << 20, transcendentals=0),
    )(*ins)


def per_device(
    sizes,
    zonal_boundary_speed,
    meridional_boundary_speed,
    potential_warmth,
    saltiness_field,
    quiescent_mixing_profile,
    substance_amounts,
    submerged_layer_number,
    solar_radiation,
    interaction_rates,
    photosynthetic_rates,
    saturation_irradiance,
    pigment_per_tracer,
):
    count = sizes[0]
    result_dimensions = zonal_boundary_speed.shape
    all_levels, _, strip, width = result_dimensions
    tracers, levels, rows, _ = substance_amounts.shape
    cells = levels * rows
    total = all_levels * rows
    strip_cells = all_levels * strip
    dma = pltpu.SemaphoreType.DMA
    column = pltpu.VMEM((total, width), F32)
    band_s = pltpu.VMEM((cells, width), F32)

    own = [
        f.reshape(strip_cells, width)
        for f in (
            zonal_boundary_speed,
            meridional_boundary_speed,
            potential_warmth,
            saltiness_field,
            quiescent_mixing_profile,
        )
    ]
    which = iota((5, strip_cells, width), 0)
    raw = jnp.broadcast_to(own[0][None], which.shape)
    for at in range(1, 5):
        raw = jnp.where(which == at, own[at][None], raw)
    _, height = raw_window(rows, count, strip_cells, 0)
    (window,) = call(
        functools.partial(window_kernel, rows, count),
        [raw],
        [shape(5, height, width)],
        flops=1 << 30,
    )
    raw_others = from_others(window, count)

    msg_levels = message_shapes(tracers, rows, cells, width, count)
    cols = shape(cells, width)
    lines = shape(tracers + 3, levels, width)
    sides = [cols, cols, lines, lines]
    field = shape(tracers, cells, width)
    c = substance_amounts.reshape(tracers, cells, width)
    msgs = call(
        functools.partial(prep_kernel, rows, count),
        [pigment_per_tracer, c],
        msg_levels,
        in_specs=[smem(), vmem()],
        vmem_limit=VMEM_LIMIT,
    )
    full = None
    for step in range(STEPS):
        first_step, last_step = step == 0, step == STEPS - 1
        p_others = from_others(msgs[0], count)
        if count == 2:
            lev = p_others
        else:
            lev = [
                lax.ppermute(msgs[1], "grp", [(i, (i + 1) % count) for i in range(count)]),
                lax.ppermute(msgs[2], "grp", [((i + 1) % count, i) for i in range(count)]),
            ]
        if first_step:
            xa, xb, ya, yb, weights, mixed, tiles, depth, solar = call(
                functools.partial(pack_kernel, rows),
                [
                    photosynthetic_rates,
                    saturation_irradiance,
                    submerged_layer_number,
                    solar_radiation,
                    c,
                    interaction_rates,
                    msgs[0],
                ],
                [
                    *sides,
                    shape(tracers * SUB, tracers * SUB),
                    field,
                    shape(2, tracers, SUB, width),
                    jax.ShapeDtypeStruct((SUB, width), jnp.int32),
                    shape(SUB, width),
                ],
                in_specs=[smem()] * 2 + [vmem()] * 5,
                scratch=[band_s],
                flops=1 << 24,
            )
        band, xa, xb, ya, yb, *full = call(
            functools.partial(ocean_kernel, rows, count, tracers, first_step),
            [depth, solar, xa, xb, ya, yb, msgs[0], *p_others, *([raw, *raw_others] if first_step else full)],
            [shape(7, cells, width), *sides, *[shape(total, width)] * (5 if first_step else 4)],
            scratch=[column] * (6 if first_step else 1)
            + [pltpu.VMEM((strip_cells, width), F32)] * (5 * (count - 1) if first_step else 0)
            + [column] * 3,
        )
        xa = lax.ppermute(xa, AXES, pairing(sizes, "gx", 0))
        xb = lax.ppermute(xb, AXES, pairing(sizes, "gx", 1))
        ya = lax.ppermute(ya, AXES, pairing(sizes, "gy", 0))
        yb = lax.ppermute(yb, AXES, pairing(sizes, "gy", 1))
        part, *p_part = call(
            functools.partial(inner_kernel, rows, count, last_step),
            [pigment_per_tracer, tiles, c, mixed, band, *lev],
            [field] + ([] if last_step else [cols]),
            in_specs=[smem()] + [vmem()] * (4 + len(lev)),
            flops=1 << 24,
        )
        if not last_step:
            k, spread, *msgs_next = call(
                functools.partial(early_kernel, rows, count, sizes),
                [c, band, xa, xb, ya, yb, msgs[0], part, *p_part],
                [shape(5, cells, width), shape(tracers + 3, cells, width), *msg_levels],
            )
            c, xa, xb, ya, yb, mixed = call(
                functools.partial(step_kernel, rows),
                [c, part, k, spread, xa, xb, weights, msgs_next[0]],
                [field, *sides, field],
                scratch=[band_s],
                flops=1 << 24,
            )
            msgs = msgs_next
        else:
            outs = call(
                functools.partial(own_strip_kernel, rows, count),
                full,
                [shape(strip_cells, width)] * 4,
                out_specs=[hbm()] * 4,
                scratch=[pltpu.VMEM((strip_cells, width), F32)] * 4 + [dma((4,))],
                flops=1 << 24,
            )
            (c,) = call(
                functools.partial(final_kernel, rows, sizes),
                [c, part, band, xa, xb, ya, yb],
                [field],
                out_specs=[hbm()],
                scratch=[
                    pltpu.VMEM((tracers + 3, cells, width), F32),
                    pltpu.VMEM((tracers, cells, width), F32),
                    dma((5,)),
                ],
            )
    return tuple(f.reshape(result_dimensions) for f in outs) + (c.reshape(substance_amounts.shape),)


def solution(mesh):
    ocean = P(None, "gy", "grp", "gx")
    tracer = P(None, "grp", "gy", "gx")
    surface = P("gy", "gx")
    sizes = tuple(mesh.shape[a] for a in AXES)
    return jax.shard_map(
        functools.partial(per_device, sizes),
        mesh=mesh,
        in_specs=(ocean,) * 5 + (tracer, surface, surface) + (P(),) * 4,
        out_specs=(ocean,) * 4 + (tracer,),
        check_vma=False,
    )
```

```python
import functools

import jax
import jax.numpy as jnp
from jax import lax
from jax.experimental import pallas as pl
from jax.experimental.pallas import tpu as pltpu
from jax.sharding import PartitionSpec as P

STEPS = 2

WATER_ATTEN = 0.01
PIGMENT_ATTEN = 0.05
WARMING_UPTAKE = 5.0
WARM_EXPANSION = 0.2
SALT_EXPANSION = 0.8
CONVECT_MIX = 0.15
SIDE_DIFFUSE = 0.05
WARMING_FACTOR = 0.0633
TIME_STEP = 0.5

SUB = 8
AXES = ("grp", "gx", "gy")
VMEM_LIMIT = 48 * 1024 * 1024

F32 = jnp.float32


def vmem():
    return pl.BlockSpec(memory_space=pltpu.VMEM)


def hbm():
    return pl.BlockSpec(memory_space=pltpu.HBM)


def shape(*dims):
    return jax.ShapeDtypeStruct(dims, F32)


def turn(x, shift, axis):
    shift = shift % x.shape[axis]
    return x if shift == 0 else pltpu.roll(x, shift, axis)


def iota(x, axis):
    return lax.broadcasted_iota(jnp.int32, x, axis)


def pairing(sizes, axis, odd):
    size_g, size_x, size_y = sizes

    def partner(g, x, y):
        i, n = (x, size_x) if axis == "gx" else (y, size_y)
        j = i + 1 if i % 2 == odd else i - 1
        if 0 <= j < n:
            return (g, j, y) if axis == "gx" else (g, x, j)
        if axis == "gx":
            return (g, x, y ^ 1) if (y ^ 1) < size_y else (g, x, y)
        return (g ^ 1, x, y) if (g ^ 1) < size_g else (g, x, y)

    def index(g, x, y):
        return (g * size_x + x) * size_y + y

    return [
        (index(g, x, y), index(*partner(g, x, y)))
        for g in range(size_g)
        for x in range(size_x)
        for y in range(size_y)
    ]


def from_others(value, count):
    return [
        lax.ppermute(value, "grp", [(i, (i + k) % count) for i in range(count)])
        for k in range(1, count)
    ]


def chunks(n, parts):
    step = -(-n // parts)
    return [(a, min(step, n - a)) for a in range(0, n, step)]


class Refs:
    def __init__(self, refs):
        self.refs = list(refs)

    def take(self, n):
        out, self.refs = self.refs[:n], self.refs[n:]
        return out


def pick(mine, others, k):
    value = mine
    for at, other in enumerate(others):
        value = jnp.where(k == at + 1, other, value)
    return value


def pack_sides(c, slot, left, right):
    lane = iota(c.shape, 1)
    width = c.shape[1]
    left = jnp.where(lane == (2 * slot - 1) % width, turn(c, 2 * slot - 1, 1), left)
    right = jnp.where(lane == 2 * slot, turn(c, 2 * slot + 1, 1), right)
    return left, right


def compact(rows, cells, count):
    return count == 2 and SUB == 2 * rows and cells >= 2 * SUB


def level_base(rows, cells, count):
    if count != 2:
        return SUB
    return cells // 2 + SUB if compact(rows, cells, count) else cells


def message_shapes(tracers, rows, cells, width, count):
    height = level_base(rows, cells, count) + tracers * rows + (SUB - rows)
    height += -height % SUB
    if count == 2:
        return [shape(height, width)]
    return [shape(cells, width), shape(height, width), shape(height, width)]


def write_levels(last, first, t, rows, base, msgs, g):
    here = pl.ds(base + t * rows, rows)
    if len(msgs) == 1:
        msgs[0][here, :] = jnp.where(g == 0, last[SUB - rows :], first[:rows])
    else:
        msgs[1][here, :] = last[SUB - rows :]
        msgs[2][here, :] = first[:rows]


def in_strip(rows, count, width, member):
    at_row = lax.rem(iota((SUB, width), 0), rows)
    strip = rows // count
    return (at_row >= member * strip) & (at_row < (member + 1) * strip)


def write_pigment(rows, count, p_ref, msg, g):
    cells, width = p_ref.shape
    if not compact(rows, cells, count):
        msg[pl.ds(0, cells), :] = p_ref[...]
        return
    levels, strip = cells // rows, rows // count
    for r in range(strip):
        msg[pl.ds(r, levels, stride=strip), :] = jnp.where(
            g == 0, p_ref[pl.ds(strip + r, levels, stride=rows), :], p_ref[pl.ds(r, levels, stride=rows), :]
        )
    blocks = [p_ref[pl.ds(at, SUB), :] for at in range(0, cells, SUB)]
    inner = blocks[1]
    for block in blocks[2:-1]:
        inner = inner + block
    inner = jnp.zeros_like(inner) if len(blocks) == 2 else inner
    near = jnp.where(g == 0, blocks[-1], blocks[0])
    rest = inner + jnp.where(g == 0, blocks[0], blocks[-1])
    rest = rest + turn(rest, rows, 0)
    msg[pl.ds(cells // 2, SUB), :] = jnp.where(in_strip(rows, count, width, g), near, turn(rest, strip, 0))


def read_pigment(rows, count, msg, other_s, g):
    cells, width = other_s.shape
    if not compact(rows, cells, count):
        return msg[pl.ds(0, cells), :]
    levels, strip = cells // rows, rows // count
    for s in range(count):
        for r in range(strip):
            other_s[pl.ds(s * strip + r, levels, stride=rows), :] = jnp.where(
                g == s, msg[pl.ds(r, levels, stride=strip), :], 0.0
            )
    edge = msg[pl.ds(cells // 2, SUB), :]
    theirs = in_strip(rows, count, width, 1 - g)
    first = other_s[pl.ds(0, SUB), :]
    rest = jnp.where(iota((SUB, width), 0) < rows, turn(edge, strip, 0), 0.0)
    other_s[pl.ds(0, SUB), :] = jnp.where(theirs, jnp.where(g == 0, edge, rest), first)
    last = other_s[pl.ds(cells - SUB, SUB), :]
    other_s[pl.ds(cells - SUB, SUB), :] = jnp.where(theirs & (g == 1), edge, last)
    return other_s[...]


def raw_window(rows, count, strip_cells, member):
    if count != 2:
        return 0, strip_cells
    height = strip_cells // 2 + 2 * (rows // count)
    return member * (strip_cells - height), height


def first_kernel(out_ref):
    out_ref[...] = jnp.zeros(out_ref.shape, F32)


def raw_kernel(rows, count, first_ref, pig_in, *refs):
    *fields, raw_ref, out_ref, pig_out = refs
    g = lax.axis_index("grp")
    pig_out[...] = pig_in[...]
    strip_cells = raw_ref.shape[1]
    low, height = raw_window(rows, count, strip_cells, 0)
    high, _ = raw_window(rows, count, strip_cells, 1)
    for at, field in enumerate(fields):
        raw_ref[at] = field[...]
        lower_part, upper_part = field[pl.ds(low, height), :], field[pl.ds(high, height), :]
        out_ref[pl.ds(at * height, height), :] = jnp.where(g == 0, upper_part, lower_part)


def tile(v, cells):
    width = v.shape[1]
    return jnp.broadcast_to(v[None], (cells // SUB, SUB, width)).reshape(cells, width)


def prep_kernel(rows, count, pig_ref, c_ref, p_ref, *msgs):
    g = lax.axis_index("grp")
    tracers, cells, width = c_ref.shape
    base = level_base(rows, cells, count)
    weights = pig_ref[...]
    pigment = jnp.zeros((cells, width), F32)
    for t in range(tracers):
        c = c_ref[t]
        pigment = pigment + tile(jnp.broadcast_to(weights[:, t : t + 1], (SUB, width)), cells) * c
        write_levels(c[cells - SUB :], c[:SUB], t, rows, base, msgs, g)
    p_ref[...] = pigment
    write_pigment(rows, count, p_ref, msgs[0], g)


def halves(v):
    high = v.astype(jnp.bfloat16)
    return high, (v - high.astype(F32)).astype(jnp.bfloat16)


def dot(a, b, **kw):
    return jnp.dot(a, b, preferred_element_type=F32, **kw)


def spread_rates(rates, tracers):
    exact = functools.partial(dot, precision=lax.Precision.HIGHEST)
    depth = tracers * SUB
    spread = jnp.where(iota((depth, tracers), 0) // SUB == iota((depth, tracers), 1), 1.0, 0.0)
    spread_t = jnp.where(iota((tracers, depth), 1) // SUB == iota((tracers, depth), 0), 1.0, 0.0)
    weights = exact(exact(spread, rates), spread_t)
    return jnp.where(
        lax.rem(iota((depth, depth), 0), SUB) == lax.rem(iota((depth, depth), 1), SUB), weights, 0.0
    )


def mix(weights, c_ref, mix_ref):
    tracers, cells, width = c_ref.shape
    w_high, w_low = halves(weights)
    for b in range(cells // SUB):
        here = pl.ds(b * SUB, SUB)
        c_high, c_low = halves(c_ref[:, here, :].reshape(tracers * SUB, width))
        mixed = dot(w_high, c_high) + (dot(w_high, c_low) + dot(w_low, c_high))
        mix_ref[:, here, :] = mixed.reshape(tracers, SUB, width)


def pack(rows, c_ref, p_ref, msg_xa, msg_xb, msg_ya, msg_yb):
    tracers, cells, _ = c_ref.shape
    levels = cells // rows
    x_even = lax.rem(lax.axis_index("gx"), 2) == 0
    y_even = lax.rem(lax.axis_index("gy"), 2) == 0
    left = right = jnp.zeros(c_ref.shape[1:], F32)
    left, right = pack_sides(p_ref[...], tracers + 2, left, right)
    for t in range(tracers):
        left, right = pack_sides(c_ref[t], t, left, right)
    msg_xa[...] = jnp.where(x_even, right, left)
    msg_xb[...] = jnp.where(x_even, left, right)

    def put(slot, first, last):
        msg_ya[slot] = jnp.where(y_even, last, first)
        msg_yb[slot] = jnp.where(y_even, first, last)

    for t in range(tracers):
        put(
            t,
            c_ref[t, pl.ds(0, levels, stride=rows), :],
            c_ref[t, pl.ds(rows - 1, levels, stride=rows), :],
        )
    put(
        tracers + 2,
        p_ref[pl.ds(0, levels, stride=rows), :],
        p_ref[pl.ds(rows - 1, levels, stride=rows), :],
    )


def pack_kernel(rows, *refs):
    refs = Refs(refs)
    photo_ref, sat_ref, pig_ref, depth_in, solar_in, c_ref, rates_ref, p_ref = refs.take(8)
    msg_xa, msg_xb, msg_ya, msg_yb, w_ref, mix_ref, tiles_ref, depth_ref, solar_ref = refs.take(9)
    tracers, cells, width = c_ref.shape
    for r in range(0, SUB, rows):
        depth_ref[pl.ds(r, rows), :] = depth_in[...]
        solar_ref[pl.ds(r, rows), :] = solar_in[...]
    for at, param in enumerate((photo_ref, sat_ref, pig_ref)):
        values = param[...]
        for t in range(tracers):
            tiles_ref[at, t] = jnp.broadcast_to(values[:, t : t + 1], (SUB, width))
    pack(rows, c_ref, p_ref, msg_xa, msg_xb, msg_ya, msg_yb)
    weights = spread_rates(rates_ref[...], tracers)
    w_ref[...] = weights
    mix(weights, c_ref, mix_ref)


def ocean_kernel(rows, count, tracers, first_step, *refs):
    refs = Refs(refs)
    depth_ref, solar_ref = refs.take(2)
    in_xa, in_xb, in_ya, in_yb = refs.take(4)
    p_own, *p_others = refs.take(count)
    if first_step:
        own_fields, *other_fields = refs.take(count)
    else:
        fields = refs.take(5)
    band_ref, msg_xa, msg_xb, msg_ya, msg_yb = refs.take(5)
    full_out = refs.take(5 if first_step else 4)
    p_full, p_other_s = refs.take(2)
    if first_step:
        fields = refs.take(5)
        other_s = refs.take(5 * (count - 1))
    face_s, par_s, wet_s = refs.take(3)
    g = lax.axis_index("grp")
    cells, width = in_xa.shape
    levels = cells // rows
    total = count * cells
    all_levels = total // rows
    strip = rows // count

    pigments = [read_pigment(rows, count, o, p_other_s, g) for o in p_others]
    for b in range(count):
        k = lax.rem(g - b + count, count)
        p_full[pl.ds(b * cells, cells), :] = pick(p_own[...], pigments, k)
    if first_step:
        strip_cells = all_levels * strip
        for at in range(5):
            for k in range(count - 1):
                other = other_s[5 * k + at]
                low, height = raw_window(rows, count, strip_cells, 0)
                value = other_fields[k][pl.ds(at * height, height), :]
                if count != 2:
                    other[...] = value
                    continue
                high, _ = raw_window(rows, count, strip_cells, 1)
                other[...] = jnp.zeros((strip_cells, width), F32)
                other[pl.ds(low, height), :] = jnp.where(g == 0, value, 0.0)
                kept = jnp.where(iota(value.shape, 0) < low + height - high, other[pl.ds(high, height), :], 0.0)
                other[pl.ds(high, height), :] = jnp.where(g == 1, value, kept)
            for s in range(count):
                k = lax.rem(g - s + count, count)
                for r in range(strip):
                    here = pl.ds(r, all_levels, stride=strip)
                    fields[at][pl.ds(s * strip + r, all_levels, stride=rows), :] = pick(
                        own_fields[at, here, :], [other_s[5 * j + at][here, :] for j in range(count - 1)], k
                    )

    row = iota((total, width), 0)
    wet = jnp.where(row // rows < tile(depth_ref[...], total), 1.0, 0.0)
    att = WATER_ATTEN + PIGMENT_ATTEN * p_full[...]
    summed = att
    step = rows
    while step < total:
        summed = summed + jnp.where(row >= step, turn(summed, step, 0), 0.0)
        step *= 2
    top = tile(solar_ref[...], total) * jnp.exp(att - summed)
    par = top * jnp.exp(-0.5 * att)
    east, north, temp, sal, mixing = [f[...] for f in fields]
    temp = temp + WARMING_UPTAKE * (top * (1.0 - jnp.exp(-att))) * wet

    def below(v):
        return turn(v, -rows, 0)

    density = SALT_EXPANSION * sal - WARM_EXPANSION * temp
    face = 0.5 * (mixing + below(mixing)) + CONVECT_MIX / (1.0 + jnp.exp(below(density) - density))
    face = jnp.where(row < total - rows, face * below(wet), 0.0)

    def stir(v):
        flux = face * (below(v) - v)
        return v + flux - turn(flux, rows, 0)

    for at, v in enumerate((east, north, temp, sal)):
        full_out[at][...] = stir(v)
    if first_step:
        full_out[4][...] = mixing
    face_s[...] = face
    par_s[...] = par
    wet_s[...] = wet

    band = pl.ds(pl.multiple_of(g * cells, SUB), cells)
    above = pl.ds(pl.multiple_of(lax.max(g * cells - SUB, 0), SUB), SUB)
    face_band = face_s[band, :]
    lifted = turn(jnp.concatenate([face_s[above, :], face_band], axis=0), rows, 0)[SUB:]
    lifted = jnp.where((iota((cells, width), 0) < rows) & (g == 0), 0.0, lifted)
    u = full_out[0][band, :]
    wet_band = wet_s[band, :]
    band_ref[0] = u
    band_ref[1] = full_out[1][band, :]
    band_ref[2] = full_out[2][band, :]
    band_ref[3] = face_band
    band_ref[4] = lifted
    band_ref[5] = par_s[band, :]
    band_ref[6] = wet_band

    x_even = lax.rem(lax.axis_index("gx"), 2) == 0
    y_even = lax.rem(lax.axis_index("gy"), 2) == 0
    xa, xb = in_xa[...], in_xb[...]
    left, right = jnp.where(x_even, xb, xa), jnp.where(x_even, xa, xb)
    left, right = pack_sides(wet_band, tracers + 1, left, right)
    _, right = pack_sides(u, tracers, left, right)
    msg_xa[...] = jnp.where(x_even, right, left)
    msg_xb[...] = jnp.where(x_even, left, right)
    for t in (*range(tracers), tracers + 2):
        msg_ya[t] = in_ya[t]
        msg_yb[t] = in_yb[t]
    speed = band_ref[1, pl.ds(rows - 1, levels, stride=rows), :]
    wet_first = band_ref[6, pl.ds(0, levels, stride=rows), :]
    wet_last = band_ref[6, pl.ds(rows - 1, levels, stride=rows), :]
    msg_ya[tracers] = speed
    msg_yb[tracers] = speed
    msg_ya[tracers + 1] = jnp.where(y_even, wet_last, wet_first)
    msg_yb[tracers + 1] = jnp.where(y_even, wet_first, wet_last)


def start_own_strip(rows, count, g, full, outs, strips, sems):
    strip = rows // count
    all_levels = full[0].shape[0] // rows
    copies = [pltpu.make_async_copy(strips[at], outs[at], sems.at[at]) for at in range(4)]
    for at in range(4):
        for r in range(strip):
            value = full[at][pl.ds(r, all_levels, stride=rows), :]
            for s in range(1, count):
                value = jnp.where(g == s, full[at][pl.ds(s * strip + r, all_levels, stride=rows), :], value)
            strips[at][pl.ds(r, all_levels, stride=strip), :] = value
        copies[at].start()
    return copies


def lower(opening, speed):
    return opening * (jnp.maximum(speed, 0.0) + SIDE_DIFFUSE)


def upper(opening, speed):
    return opening * (jnp.minimum(speed, 0.0) - SIDE_DIFFUSE)


def inner_kernel(rows, count, last_step, *refs):
    refs = Refs(refs)
    tiles_ref, c_ref, mix_ref, band_ref = refs.take(4)
    lev_in = refs.take(1 if count == 2 else 2)
    if last_step:
        full = refs.take(4)
    (part_ref,) = refs.take(1)
    if last_step:
        outs, strips = refs.take(4), refs.take(4)
        (sems,) = refs.take(1)
        copies = start_own_strip(rows, count, lax.axis_index("grp"), full, outs, strips, sems)
    else:
        (p_part,) = refs.take(1)
    tracers, cells, width = c_ref.shape
    base = level_base(rows, cells, count)
    lane = iota((cells, width), 1)
    at_row = lax.rem(iota((cells, width), 0), rows)
    u = band_ref[0]
    v = band_ref[1]
    wet = band_ref[6]

    def west(x):
        return turn(x, 1, 1)

    def east(x):
        return turn(x, -1, 1)

    def south(x):
        return turn(x, 1, 0)

    def north(x):
        return turn(x, -1, 0)

    open_w = jnp.where(lane == 0, 0.0, wet * west(wet))
    open_e = jnp.where(lane == width - 1, 0.0, wet * east(wet))
    open_s = jnp.where(at_row == 0, 0.0, wet * south(wet))
    open_n = jnp.where(at_row == rows - 1, 0.0, wet * north(wet))
    k_w = lower(open_w, west(u))
    k_e = -upper(open_e, u)
    k_s = lower(open_s, south(v))
    k_n = -upper(open_n, v)
    k_d = band_ref[3]
    k_u = band_ref[4]
    k_c = (upper(open_w, west(u)) - lower(open_e, u)) + (upper(open_s, south(v)) - lower(open_n, v))
    k_c = 1.0 + (k_c - k_d - k_u)
    par = band_ref[5]
    lit = TIME_STEP * wet
    warm = lit * jnp.exp(WARMING_FACTOR * (band_ref[2] - 20.0))
    lit = lit * par
    pigment = jnp.zeros((cells, width), F32)
    for t in range(tracers):
        c = c_ref[t]
        at = base + t * rows
        up8 = lev_in[0][pl.ds(at + rows - SUB, SUB), :]
        down8 = lev_in[-1][pl.ds(at, SUB), :]
        c_u = turn(jnp.concatenate([up8, c], axis=0), rows, 0)[SUB:]
        c_d = turn(jnp.concatenate([c, down8], axis=0), -rows, 0)[:cells]
        part = (
            (k_c + tile(tiles_ref[0, t], cells) * (lit / (par + tile(tiles_ref[1, t], cells)))) * c
            + (k_u * c_u + k_d * c_d)
            + (k_w * west(c) + k_e * east(c))
            + (k_s * south(c) + k_n * north(c))
            + warm * mix_ref[t]
        )
        part_ref[t] = part
        if not last_step:
            pigment = pigment + tile(tiles_ref[2, t], cells) * part
    if last_step:
        for copy in copies:
            copy.wait()
    else:
        p_part[...] = pigment


def x_halo(got_xa, got_xb):
    x_even = lax.rem(lax.axis_index("gx"), 2) == 0
    xa, xb = got_xa[...], got_xb[...]
    lane = iota(xa.shape, 1)
    return jnp.where((lax.rem(lane, 2) == 0) == x_even, xb, xa)


def spread_rows(rows, got_ya, got_yb, out_ref, slot):
    y_even = lax.rem(lax.axis_index("gy"), 2) == 0
    levels = got_ya.shape[1]
    ya, yb = got_ya[slot], got_yb[slot]
    out_ref[slot, pl.ds(0, levels, stride=rows), :] = jnp.where(y_even, yb, ya)
    out_ref[slot, pl.ds(rows - 1, levels, stride=rows), :] = jnp.where(y_even, ya, yb)


def side_factors(rows, sizes, halo, spread_s, band_ref, tracers):
    _, size_x, size_y = sizes
    x = lax.axis_index("gx")
    y = lax.axis_index("gy")
    u = band_ref[0]
    v = band_ref[1]
    wet = band_ref[6]
    shape2 = wet.shape
    lane = iota(shape2, 1)
    at_row = lax.rem(iota(shape2, 0), rows)
    at_w, at_e, at_s, at_n = lane == 0, lane == shape2[1] - 1, at_row == 0, at_row == rows - 1
    wet_x = wet * turn(halo, -2 * (tracers + 1), 1)
    wet_y = wet * spread_s[tracers + 1]
    open_w = jnp.where(at_w & (x > 0), wet_x, 0.0)
    open_e = jnp.where(at_e & (x < size_x - 1), wet_x, 0.0)
    open_s = jnp.where(at_s & (y > 0), wet_y, 0.0)
    open_n = jnp.where(at_n & (y < size_y - 1), wet_y, 0.0)
    u_w = turn(halo, -2 * tracers, 1)
    v_s = jnp.where(at_s, spread_s[tracers], 0.0)
    k_x = lower(open_w, u_w) - upper(open_e, u)
    k_y = lower(open_s, v_s) - upper(open_n, v)
    k_c = (upper(open_w, u_w) - lower(open_e, u)) + (upper(open_s, v_s) - lower(open_n, v))
    return k_x, k_y, k_c


def sideways(rows, factors, halo, outer, c, slot):
    k_x, k_y, k_c = factors
    at_row = lax.rem(iota(c.shape, 0), rows)
    edge = (at_row == 0) | (at_row == rows - 1)
    return (k_x * turn(halo, -2 * slot, 1) + k_c * c) + jnp.where(edge, k_y * outer, 0.0)


def early_kernel(rows, count, sizes, *refs):
    refs = Refs(refs)
    c_ref, band_ref, got_xa, got_xb, got_ya, got_yb, p_in, part_ref, p_part = refs.take(9)
    k_ref, halo_ref, spread_s, p_ref = refs.take(4)
    msgs = refs.refs
    g = lax.axis_index("grp")
    tracers, cells, width = c_ref.shape
    base = level_base(rows, cells, count)
    halo = x_halo(got_xa, got_xb)
    halo_ref[...] = halo
    for slot in range(tracers + 3):
        spread_rows(rows, got_ya, got_yb, spread_s, slot)
    factors = side_factors(rows, sizes, halo, spread_s, band_ref, tracers)
    for at, k in enumerate(factors):
        k_ref[at] = k
    slot = tracers + 2
    p_ref[...] = p_part[...] + sideways(rows, factors, halo, spread_s[slot], p_in[...], slot)
    write_pigment(rows, count, p_ref, msgs[0], g)

    def block(at, t):
        here = pl.ds(at, SUB)
        cut = [k[at : at + SUB] for k in factors]
        change = sideways(rows, cut, halo[at : at + SUB], spread_s[t, here, :], c_ref[t, here, :], t)
        return part_ref[t, here, :] + change

    for t in range(tracers):
        write_levels(block(cells - SUB, t), block(0, t), t, rows, base, msgs, g)


def step_kernel(rows, *refs):
    refs = Refs(refs)
    c_ref, part_ref, k_ref, halo_ref, spread_s, w_ref, p_ref = refs.take(7)
    out_ref, msg_xa, msg_xb, msg_ya, msg_yb, mix_ref = refs.take(6)
    tracers = c_ref.shape[0]
    factors = [k_ref[i] for i in range(3)]
    halo = halo_ref[...]
    for t in range(tracers):
        out_ref[t] = part_ref[t] + sideways(rows, factors, halo, spread_s[t], c_ref[t], t)
    pack(rows, out_ref, p_ref, msg_xa, msg_xb, msg_ya, msg_yb)
    mix(w_ref[...], out_ref, mix_ref)


def final_kernel(rows, sizes, *refs):
    refs = Refs(refs)
    c_ref, part_ref, band_ref, got_xa, got_xb, got_ya, got_yb = refs.take(7)
    out_hbm, spread_s, new_s, sems = refs.take(4)
    tracers = c_ref.shape[0]
    halo = x_halo(got_xa, got_xb)
    for slot in (tracers, tracers + 1):
        spread_rows(rows, got_ya, got_yb, spread_s, slot)
    factors = side_factors(rows, sizes, halo, spread_s, band_ref, tracers)
    copies = []
    for i, (a, n) in enumerate(chunks(tracers, sems.shape[0])):
        for t in range(a, a + n):
            spread_rows(rows, got_ya, got_yb, spread_s, t)
            new_s[t] = part_ref[t] + sideways(rows, factors, halo, spread_s[t], c_ref[t], t)
        copies.append(pltpu.make_async_copy(new_s.at[pl.ds(a, n)], out_hbm.at[pl.ds(a, n)], sems.at[i]))
        copies[-1].start()
    for copy in copies:
        copy.wait()


def call(kernel, ins, outs, in_specs=None, out_specs=None, scratch=(), flops=1 << 20, vmem_limit=VMEM_LIMIT):
    return pl.pallas_call(
        kernel,
        in_specs=[vmem() for _ in ins] if in_specs is None else in_specs,
        out_specs=[vmem() for _ in outs] if out_specs is None else out_specs,
        out_shape=outs,
        scratch_shapes=list(scratch),
        compiler_params=pltpu.CompilerParams(vmem_limit_bytes=vmem_limit),
        cost_estimate=pl.CostEstimate(flops=flops, bytes_accessed=1 << 20, transcendentals=0),
    )(*ins)


def per_device(
    sizes,
    zonal_boundary_speed,
    meridional_boundary_speed,
    potential_warmth,
    saltiness_field,
    quiescent_mixing_profile,
    substance_amounts,
    submerged_layer_number,
    solar_radiation,
    interaction_rates,
    photosynthetic_rates,
    saturation_irradiance,
    pigment_per_tracer,
):
    count = sizes[0]
    result_dimensions = zonal_boundary_speed.shape
    all_levels, _, strip, width = result_dimensions
    tracers, levels, rows, _ = substance_amounts.shape
    cells = levels * rows
    total = all_levels * rows
    strip_cells = all_levels * strip
    dma = pltpu.SemaphoreType.DMA
    column = pltpu.VMEM((total, width), F32)
    band_s = pltpu.VMEM((cells, width), F32)

    own = [
        f.reshape(strip_cells, width)
        for f in (
            zonal_boundary_speed,
            meridional_boundary_speed,
            potential_warmth,
            saltiness_field,
            quiescent_mixing_profile,
        )
    ]
    _, height = raw_window(rows, count, strip_cells, 0)
    params = [
        p.reshape(1, tracers) for p in (photosynthetic_rates, saturation_irradiance, pigment_per_tracer)
    ]
    (first,) = call(first_kernel, [], [shape(SUB, width)], flops=1 << 30)
    raw, window, pig = call(
        functools.partial(raw_kernel, rows, count),
        [first, params[2], *own],
        [shape(5, strip_cells, width), shape(5 * height, width), shape(1, tracers)],
    )
    raw_others = from_others(window, count)

    msg_levels = message_shapes(tracers, rows, cells, width, count)
    cols = shape(cells, width)
    lines = shape(tracers + 3, levels, width)
    sides = [cols, cols, lines, lines]
    field = shape(tracers, cells, width)
    c = substance_amounts.reshape(tracers, cells, width)
    pigment, *msgs = call(
        functools.partial(prep_kernel, rows, count),
        [pig, c],
        [cols, *msg_levels],
    )
    full = None
    for step in range(STEPS):
        first_step, last_step = step == 0, step == STEPS - 1
        p_others = from_others(msgs[0], count)
        if count == 2:
            lev = p_others
        else:
            lev = [
                lax.ppermute(msgs[1], "grp", [(i, (i + 1) % count) for i in range(count)]),
                lax.ppermute(msgs[2], "grp", [((i + 1) % count, i) for i in range(count)]),
            ]
        if first_step:
            xa, xb, ya, yb, weights, mixed, tiles, depth, solar = call(
                functools.partial(pack_kernel, rows),
                [
                    *params,
                    submerged_layer_number,
                    solar_radiation,
                    c,
                    interaction_rates,
                    pigment,
                ],
                [
                    *sides,
                    shape(tracers * SUB, tracers * SUB),
                    field,
                    shape(3, tracers, SUB, width),
                    jax.ShapeDtypeStruct((SUB, width), jnp.int32),
                    shape(SUB, width),
                ],
                flops=1 << 24,
            )
        band, xa, xb, ya, yb, *full = call(
            functools.partial(ocean_kernel, rows, count, tracers, first_step),
            [depth, solar, xa, xb, ya, yb, pigment, *p_others, *([raw, *raw_others] if first_step else full)],
            [shape(7, cells, width), *sides, *[shape(total, width)] * (5 if first_step else 4)],
            scratch=[column, band_s]
            + [column] * (5 if first_step else 0)
            + [pltpu.VMEM((strip_cells, width), F32)] * (5 * (count - 1) if first_step else 0)
            + [column] * 3,
        )
        xa = lax.ppermute(xa, AXES, pairing(sizes, "gx", 0))
        xb = lax.ppermute(xb, AXES, pairing(sizes, "gx", 1))
        ya = lax.ppermute(ya, AXES, pairing(sizes, "gy", 0))
        yb = lax.ppermute(yb, AXES, pairing(sizes, "gy", 1))
        part, *rest = call(
            functools.partial(inner_kernel, rows, count, last_step),
            [tiles, c, mixed, band, *lev, *(full if last_step else [])],
            [field] + ([shape(strip_cells, width)] * 4 if last_step else [cols]),
            out_specs=[vmem()] + ([hbm()] * 4 if last_step else [vmem()]),
            scratch=[pltpu.VMEM((strip_cells, width), F32)] * 4 + [dma((4,))] if last_step else [],
            flops=1 << 24,
        )
        if not last_step:
            k, halo, spread, pigment_next, *msgs = call(
                functools.partial(early_kernel, rows, count, sizes),
                [c, band, xa, xb, ya, yb, pigment, part, *rest],
                [shape(3, cells, width), cols, shape(tracers + 3, cells, width), cols, *msg_levels],
            )
            pigment = pigment_next
            c, xa, xb, ya, yb, mixed = call(
                functools.partial(step_kernel, rows),
                [c, part, k, halo, spread, weights, pigment],
                [field, *sides, field],
                flops=1 << 24,
            )
        else:
            ocean = rest
            (c,) = call(
                functools.partial(final_kernel, rows, sizes),
                [c, part, band, xa, xb, ya, yb],
                [field],
                out_specs=[hbm()],
                scratch=[
                    pltpu.VMEM((tracers + 3, cells, width), F32),
                    pltpu.VMEM((tracers, cells, width), F32),
                    dma((5,)),
                ],
            )
    return tuple(f.reshape(result_dimensions) for f in ocean) + (c.reshape(substance_amounts.shape),)


def solution(mesh):
    ocean = P(None, "gy", "grp", "gx")
    tracer = P(None, "grp", "gy", "gx")
    surface = P("gy", "gx")
    sizes = tuple(mesh.shape[a] for a in AXES)
    return jax.shard_map(
        functools.partial(per_device, sizes),
        mesh=mesh,
        in_specs=(ocean,) * 5 + (tracer, surface, surface) + (P(),) * 4,
        out_specs=(ocean,) * 4 + (tracer,),
        check_vma=False,
    )
```

```python
import functools

import jax
import jax.numpy as jnp
from jax import lax
from jax.experimental import pallas as pl
from jax.experimental.pallas import tpu as pltpu
from jax.sharding import PartitionSpec as P

STEPS = 2

WATER_ATTEN = 0.01
PIGMENT_ATTEN = 0.05
WARMING_UPTAKE = 5.0
WARM_EXPANSION = 0.2
SALT_EXPANSION = 0.8
CONVECT_MIX = 0.15
SIDE_DIFFUSE = 0.05
WARMING_FACTOR = 0.0633
TIME_STEP = 0.5

SUB = 8
AXES = ("grp", "gx", "gy")
VMEM_LIMIT = 48 * 1024 * 1024

F32 = jnp.float32


def vmem():
    return pl.BlockSpec(memory_space=pltpu.VMEM)


def hbm():
    return pl.BlockSpec(memory_space=pltpu.HBM)


def shape(*dims):
    return jax.ShapeDtypeStruct(dims, F32)


def turn(x, shift, axis):
    shift = shift % x.shape[axis]
    return x if shift == 0 else pltpu.roll(x, shift, axis)


def iota(x, axis):
    return lax.broadcasted_iota(jnp.int32, x, axis)


def pairing(sizes, axis, odd):
    size_g, size_x, size_y = sizes

    def partner(g, x, y):
        i, n = (x, size_x) if axis == "gx" else (y, size_y)
        j = i + 1 if i % 2 == odd else i - 1
        if 0 <= j < n:
            return (g, j, y) if axis == "gx" else (g, x, j)
        if axis == "gx":
            return (g, x, y ^ 1) if (y ^ 1) < size_y else (g, x, y)
        return (g, x ^ 1, y) if (x ^ 1) < size_x else (g, x, y)

    def index(g, x, y):
        return (g * size_x + x) * size_y + y

    return [
        (index(g, x, y), index(*partner(g, x, y)))
        for g in range(size_g)
        for x in range(size_x)
        for y in range(size_y)
    ]


def upward(sizes):
    size_g, size_x, size_y = sizes
    return [
        ((g * size_x + x) * size_y + y, (g * size_x + x) * size_y + (y + 1) % size_y)
        for g in range(size_g)
        for x in range(size_x)
        for y in range(size_y)
    ]


def from_others(value, count):
    return [
        lax.ppermute(value, "grp", [(i, (i + k) % count) for i in range(count)])
        for k in range(1, count)
    ]


def chunks(n, parts):
    step = -(-n // parts)
    return [(a, min(step, n - a)) for a in range(0, n, step)]


class Refs:
    def __init__(self, refs):
        self.refs = list(refs)

    def take(self, n):
        out, self.refs = self.refs[:n], self.refs[n:]
        return out


def pick(mine, others, k):
    value = mine
    for at, other in enumerate(others):
        value = jnp.where(k == at + 1, other, value)
    return value


def pack_sides(c, slot, left, right):
    lane = iota(c.shape, 1)
    left = jnp.where(lane == 2 * slot, turn(c, 2 * slot, 1), left)
    right = jnp.where(lane == 2 * slot, turn(c, 2 * slot + 1, 1), right)
    return left, right


def folds(slots, cells, width):
    return 4 * slots <= width and cells % (2 * SUB) == 0


def fold(v, slots):
    cells, width = v.shape
    if not folds(slots, cells, width):
        return v
    half = cells // 2
    return jnp.where(iota((half, width), 1) < width // 2, v[:half], turn(v[half:], width // 2, 1))


def unfold(v, slots, cells):
    width = v.shape[1]
    if not folds(slots, cells, width):
        return v
    return jnp.concatenate([v, turn(v, width // 2, 1)], axis=0)


def compact(rows, cells, count):
    return count == 2 and SUB == 2 * rows and cells >= 2 * SUB


def level_base(rows, cells, count):
    if count != 2:
        return SUB
    return cells // 2 + SUB if compact(rows, cells, count) else cells


def message_shapes(tracers, rows, cells, width, count):
    height = level_base(rows, cells, count) + tracers * rows + (SUB - rows)
    height += -height % SUB
    if count == 2:
        return [shape(height, width)]
    return [shape(cells, width), shape(height, width), shape(height, width)]


def write_levels(last, first, t, rows, base, msgs, g):
    here = pl.ds(base + t * rows, rows)
    if len(msgs) == 1:
        msgs[0][here, :] = jnp.where(g == 0, last[SUB - rows :], first[:rows])
    else:
        msgs[1][here, :] = last[SUB - rows :]
        msgs[2][here, :] = first[:rows]


def in_strip(rows, count, width, member):
    at_row = lax.rem(iota((SUB, width), 0), rows)
    strip = rows // count
    return (at_row >= member * strip) & (at_row < (member + 1) * strip)


def write_pigment(rows, count, p_ref, msg, g):
    cells, width = p_ref.shape
    if not compact(rows, cells, count):
        msg[pl.ds(0, cells), :] = p_ref[...]
        return
    levels, strip = cells // rows, rows // count
    for r in range(strip):
        msg[pl.ds(r, levels, stride=strip), :] = jnp.where(
            g == 0, p_ref[pl.ds(strip + r, levels, stride=rows), :], p_ref[pl.ds(r, levels, stride=rows), :]
        )
    blocks = [p_ref[pl.ds(at, SUB), :] for at in range(0, cells, SUB)]
    inner = blocks[1]
    for block in blocks[2:-1]:
        inner = inner + block
    inner = jnp.zeros_like(inner) if len(blocks) == 2 else inner
    near = jnp.where(g == 0, blocks[-1], blocks[0])
    rest = inner + jnp.where(g == 0, blocks[0], blocks[-1])
    rest = rest + turn(rest, rows, 0)
    msg[pl.ds(cells // 2, SUB), :] = jnp.where(in_strip(rows, count, width, g), near, turn(rest, strip, 0))


def read_pigment(rows, count, msg, other_s, g):
    cells, width = other_s.shape
    if not compact(rows, cells, count):
        return msg[pl.ds(0, cells), :]
    levels, strip = cells // rows, rows // count
    for s in range(count):
        for r in range(strip):
            other_s[pl.ds(s * strip + r, levels, stride=rows), :] = jnp.where(
                g == s, msg[pl.ds(r, levels, stride=strip), :], 0.0
            )
    edge = msg[pl.ds(cells // 2, SUB), :]
    theirs = in_strip(rows, count, width, 1 - g)
    first = other_s[pl.ds(0, SUB), :]
    rest = jnp.where(iota((SUB, width), 0) < rows, turn(edge, strip, 0), 0.0)
    other_s[pl.ds(0, SUB), :] = jnp.where(theirs, jnp.where(g == 0, edge, rest), first)
    last = other_s[pl.ds(cells - SUB, SUB), :]
    other_s[pl.ds(cells - SUB, SUB), :] = jnp.where(theirs & (g == 1), edge, last)
    return other_s[...]


def raw_window(rows, count, strip_cells, member):
    if count != 2:
        return 0, strip_cells
    height = strip_cells // 2 + 2 * (rows // count)
    return member * (strip_cells - height), height


def first_kernel(out_ref):
    out_ref[...] = jnp.zeros(out_ref.shape, F32)


def raw_kernel(rows, count, first_ref, pig_in, *refs):
    *fields, raw_ref, out_ref, pig_out = refs
    g = lax.axis_index("grp")
    pig_out[...] = pig_in[...]
    strip_cells = raw_ref.shape[1]
    low, height = raw_window(rows, count, strip_cells, 0)
    high, _ = raw_window(rows, count, strip_cells, 1)
    for at, field in enumerate(fields):
        raw_ref[at] = field[...]
        lower_part, upper_part = field[pl.ds(low, height), :], field[pl.ds(high, height), :]
        out_ref[pl.ds(at * height, height), :] = jnp.where(g == 0, upper_part, lower_part)


def tile(v, cells):
    width = v.shape[1]
    return jnp.broadcast_to(v[None], (cells // SUB, SUB, width)).reshape(cells, width)


def prep_kernel(rows, count, pig_ref, c_ref, p_ref, *msgs):
    g = lax.axis_index("grp")
    tracers, cells, width = c_ref.shape
    base = level_base(rows, cells, count)
    weights = pig_ref[...]
    pigment = jnp.zeros((cells, width), F32)
    for t in range(tracers):
        c = c_ref[t]
        pigment = pigment + tile(jnp.broadcast_to(weights[:, t : t + 1], (SUB, width)), cells) * c
        write_levels(c[cells - SUB :], c[:SUB], t, rows, base, msgs, g)
    p_ref[...] = pigment
    write_pigment(rows, count, p_ref, msgs[0], g)


def halves(v):
    high = v.astype(jnp.bfloat16)
    return high, (v - high.astype(F32)).astype(jnp.bfloat16)


def dot(a, b, **kw):
    return jnp.dot(a, b, preferred_element_type=F32, **kw)


def spread_rates(rates, tracers):
    exact = functools.partial(dot, precision=lax.Precision.HIGHEST)
    depth = tracers * SUB
    spread = jnp.where(iota((depth, tracers), 0) // SUB == iota((depth, tracers), 1), 1.0, 0.0)
    spread_t = jnp.where(iota((tracers, depth), 1) // SUB == iota((tracers, depth), 0), 1.0, 0.0)
    weights = exact(exact(spread, rates), spread_t)
    return jnp.where(
        lax.rem(iota((depth, depth), 0), SUB) == lax.rem(iota((depth, depth), 1), SUB), weights, 0.0
    )


def mix(weights, c_ref, mix_ref):
    tracers, cells, width = c_ref.shape
    w_high, w_low = halves(weights)
    for b in range(cells // SUB):
        here = pl.ds(b * SUB, SUB)
        c_high, c_low = halves(c_ref[:, here, :].reshape(tracers * SUB, width))
        mixed = dot(w_high, c_high) + (dot(w_high, c_low) + dot(w_low, c_high))
        mix_ref[:, here, :] = mixed.reshape(tracers, SUB, width)


def put_rows(msg_ya, msg_yb, slot, first, last):
    y_even = lax.rem(lax.axis_index("gy"), 2) == 0
    msg_ya[slot] = jnp.where(y_even, last, first)
    msg_yb[slot] = jnp.where(y_even, first, last)


def pack(rows, c_ref, p_ref, msg_xa, msg_xb, msg_ya, msg_yb):
    tracers, cells, _ = c_ref.shape
    levels = cells // rows
    x_even = lax.rem(lax.axis_index("gx"), 2) == 0
    left = right = jnp.zeros(c_ref.shape[1:], F32)
    left, right = pack_sides(p_ref[...], tracers + 2, left, right)
    for t in range(tracers):
        left, right = pack_sides(c_ref[t], t, left, right)
    msg_xa[...] = jnp.where(x_even, right, left)
    msg_xb[...] = jnp.where(x_even, left, right)
    first, last = pl.ds(0, levels, stride=rows), pl.ds(rows - 1, levels, stride=rows)
    for t in range(tracers):
        put_rows(msg_ya, msg_yb, t, c_ref[t, first, :], c_ref[t, last, :])
    if msg_ya.shape[0] > tracers:
        put_rows(msg_ya, msg_yb, tracers, p_ref[first, :], p_ref[last, :])


def pack_kernel(rows, *refs):
    refs = Refs(refs)
    photo_ref, sat_ref, pig_ref, depth_in, solar_in, c_ref, rates_ref, p_ref = refs.take(8)
    msg_xa, msg_xb, msg_ya, msg_yb, w_ref, mix_ref, tiles_ref, depth_ref, solar_ref = refs.take(9)
    tracers, cells, width = c_ref.shape
    for r in range(0, SUB, rows):
        depth_ref[pl.ds(r, rows), :] = depth_in[...]
        solar_ref[pl.ds(r, rows), :] = solar_in[...]
    for at, param in enumerate((photo_ref, sat_ref, pig_ref)):
        values = param[...]
        for t in range(tracers):
            tiles_ref[at, t] = jnp.broadcast_to(values[:, t : t + 1], (SUB, width))
    pack(rows, c_ref, p_ref, msg_xa, msg_xb, msg_ya, msg_yb)
    levels = cells // rows
    level = lax.axis_index("grp") * levels + iota((levels, width), 0)
    wet_first = jnp.where(level < depth_in[pl.ds(0, 1), :], 1.0, 0.0)
    wet_last = jnp.where(level < depth_in[pl.ds(rows - 1, 1), :], 1.0, 0.0)
    put_rows(msg_ya, msg_yb, tracers + 1, wet_first, wet_last)
    weights = spread_rates(rates_ref[...], tracers)
    w_ref[...] = weights
    mix(weights, c_ref, mix_ref)


def ocean_kernel(rows, count, tracers, first_step, *refs):
    refs = Refs(refs)
    depth_ref, solar_ref = refs.take(2)
    in_xa, in_xb = refs.take(2)
    p_own, *p_others = refs.take(count)
    if first_step:
        own_fields, *other_fields = refs.take(count)
    else:
        fields = refs.take(5)
    band_ref, msg_xa, msg_xb, speed_ref = refs.take(4)
    full_out = refs.take(5 if first_step else 4)
    p_full, p_other_s = refs.take(2)
    if first_step:
        fields = refs.take(5)
        other_s = refs.take(5 * (count - 1))
    face_s, par_s, wet_s = refs.take(3)
    g = lax.axis_index("grp")
    cells, width = in_xa.shape
    levels = cells // rows
    total = count * cells
    all_levels = total // rows
    strip = rows // count

    pigments = [read_pigment(rows, count, o, p_other_s, g) for o in p_others]
    for b in range(count):
        k = lax.rem(g - b + count, count)
        p_full[pl.ds(b * cells, cells), :] = pick(p_own[...], pigments, k)
    if first_step:
        strip_cells = all_levels * strip
        for at in range(5):
            for k in range(count - 1):
                other = other_s[5 * k + at]
                low, height = raw_window(rows, count, strip_cells, 0)
                value = other_fields[k][pl.ds(at * height, height), :]
                if count != 2:
                    other[...] = value
                    continue
                high, _ = raw_window(rows, count, strip_cells, 1)
                other[...] = jnp.zeros((strip_cells, width), F32)
                other[pl.ds(low, height), :] = jnp.where(g == 0, value, 0.0)
                kept = jnp.where(iota(value.shape, 0) < low + height - high, other[pl.ds(high, height), :], 0.0)
                other[pl.ds(high, height), :] = jnp.where(g == 1, value, kept)
            for s in range(count):
                k = lax.rem(g - s + count, count)
                for r in range(strip):
                    here = pl.ds(r, all_levels, stride=strip)
                    fields[at][pl.ds(s * strip + r, all_levels, stride=rows), :] = pick(
                        own_fields[at, here, :], [other_s[5 * j + at][here, :] for j in range(count - 1)], k
                    )

    row = iota((total, width), 0)
    wet = jnp.where(row // rows < tile(depth_ref[...], total), 1.0, 0.0)
    att = WATER_ATTEN + PIGMENT_ATTEN * p_full[...]
    summed = att
    step = rows
    while step < total:
        summed = summed + jnp.where(row >= step, turn(summed, step, 0), 0.0)
        step *= 2
    top = tile(solar_ref[...], total) * jnp.exp(att - summed)
    par = top * jnp.exp(-0.5 * att)
    east, north, temp, sal, mixing = [f[...] for f in fields]
    temp = temp + WARMING_UPTAKE * (top * (1.0 - jnp.exp(-att))) * wet

    def below(v):
        return turn(v, -rows, 0)

    density = SALT_EXPANSION * sal - WARM_EXPANSION * temp
    face = 0.5 * (mixing + below(mixing)) + CONVECT_MIX / (1.0 + jnp.exp(below(density) - density))
    face = jnp.where(row < total - rows, face * below(wet), 0.0)

    def stir(v):
        flux = face * (below(v) - v)
        return v + flux - turn(flux, rows, 0)

    for at, v in enumerate((east, north, temp, sal)):
        full_out[at][...] = stir(v)
    if first_step:
        full_out[4][...] = mixing
    face_s[...] = face
    par_s[...] = par
    wet_s[...] = wet

    band = pl.ds(pl.multiple_of(g * cells, SUB), cells)
    above = pl.ds(pl.multiple_of(lax.max(g * cells - SUB, 0), SUB), SUB)
    face_band = face_s[band, :]
    lifted = turn(jnp.concatenate([face_s[above, :], face_band], axis=0), rows, 0)[SUB:]
    lifted = jnp.where((iota((cells, width), 0) < rows) & (g == 0), 0.0, lifted)
    u = full_out[0][band, :]
    wet_band = wet_s[band, :]
    band_ref[0] = u
    band_ref[1] = full_out[1][band, :]
    band_ref[2] = full_out[2][band, :]
    band_ref[3] = face_band
    band_ref[4] = lifted
    band_ref[5] = par_s[band, :]
    band_ref[6] = wet_band

    x_even = lax.rem(lax.axis_index("gx"), 2) == 0
    xa, xb = in_xa[...], in_xb[...]
    left, right = jnp.where(x_even, xb, xa), jnp.where(x_even, xa, xb)
    left, right = pack_sides(wet_band, tracers + 1, left, right)
    _, right = pack_sides(u, tracers, left, right)
    msg_xa[...] = fold(jnp.where(x_even, right, left), tracers + 3)
    msg_xb[...] = fold(jnp.where(x_even, left, right), tracers + 3)
    speed_ref[pl.ds(0, levels), :] = band_ref[1, pl.ds(rows - 1, levels, stride=rows), :]
    speed_ref[pl.ds(levels, levels), :] = jnp.zeros((levels, width), F32)
    speed_ref[pl.ds(2 * levels, levels), :] = jnp.zeros((levels, width), F32)


def start_own_strip(rows, count, g, full, outs, strips, sems):
    strip = rows // count
    all_levels = full[0].shape[0] // rows
    copies = [pltpu.make_async_copy(strips[at], outs[at], sems.at[at]) for at in range(4)]
    for at in range(4):
        for r in range(strip):
            value = full[at][pl.ds(r, all_levels, stride=rows), :]
            for s in range(1, count):
                value = jnp.where(g == s, full[at][pl.ds(s * strip + r, all_levels, stride=rows), :], value)
            strips[at][pl.ds(r, all_levels, stride=strip), :] = value
        copies[at].start()
    return copies


def lower(opening, speed):
    return opening * (jnp.maximum(speed, 0.0) + SIDE_DIFFUSE)


def upper(opening, speed):
    return opening * (jnp.minimum(speed, 0.0) - SIDE_DIFFUSE)


def inner_kernel(rows, count, last_step, *refs):
    refs = Refs(refs)
    tiles_ref, c_ref, mix_ref, band_ref = refs.take(4)
    lev_in = refs.take(1 if count == 2 else 2)
    if last_step:
        full = refs.take(4)
    (part_ref,) = refs.take(1)
    if last_step:
        outs, strips = refs.take(4), refs.take(4)
        (sems,) = refs.take(1)
        copies = start_own_strip(rows, count, lax.axis_index("grp"), full, outs, strips, sems)
    else:
        (p_part,) = refs.take(1)
    tracers, cells, width = c_ref.shape
    base = level_base(rows, cells, count)
    lane = iota((cells, width), 1)
    at_row = lax.rem(iota((cells, width), 0), rows)
    u = band_ref[0]
    v = band_ref[1]
    wet = band_ref[6]

    def west(x):
        return turn(x, 1, 1)

    def east(x):
        return turn(x, -1, 1)

    def south(x):
        return turn(x, 1, 0)

    def north(x):
        return turn(x, -1, 0)

    open_w = jnp.where(lane == 0, 0.0, wet * west(wet))
    open_e = jnp.where(lane == width - 1, 0.0, wet * east(wet))
    open_s = jnp.where(at_row == 0, 0.0, wet * south(wet))
    open_n = jnp.where(at_row == rows - 1, 0.0, wet * north(wet))
    k_w = lower(open_w, west(u))
    k_e = -upper(open_e, u)
    k_s = lower(open_s, south(v))
    k_n = -upper(open_n, v)
    k_d = band_ref[3]
    k_u = band_ref[4]
    k_c = (upper(open_w, west(u)) - lower(open_e, u)) + (upper(open_s, south(v)) - lower(open_n, v))
    k_c = 1.0 + (k_c - k_d - k_u)
    par = band_ref[5]
    lit = TIME_STEP * wet
    warm = lit * jnp.exp(WARMING_FACTOR * (band_ref[2] - 20.0))
    lit = lit * par
    pigment = jnp.zeros((cells, width), F32)
    for t in range(tracers):
        c = c_ref[t]
        at = base + t * rows
        up8 = lev_in[0][pl.ds(at + rows - SUB, SUB), :]
        down8 = lev_in[-1][pl.ds(at, SUB), :]
        c_u = turn(jnp.concatenate([up8, c], axis=0), rows, 0)[SUB:]
        c_d = turn(jnp.concatenate([c, down8], axis=0), -rows, 0)[:cells]
        part = (
            (k_c + tile(tiles_ref[0, t], cells) * (lit / (par + tile(tiles_ref[1, t], cells)))) * c
            + (k_u * c_u + k_d * c_d)
            + (k_w * west(c) + k_e * east(c))
            + (k_s * south(c) + k_n * north(c))
            + warm * mix_ref[t]
        )
        part_ref[t] = part
        if not last_step:
            pigment = pigment + tile(tiles_ref[2, t], cells) * part
    if last_step:
        for copy in copies:
            copy.wait()
    else:
        p_part[...] = pigment


def x_halo(got_xa, got_xb, slots, cells):
    x_even = lax.rem(lax.axis_index("gx"), 2) == 0
    xa, xb = got_xa[...], got_xb[...]
    west = jnp.where(x_even, xb, xa)
    east = turn(jnp.where(x_even, xa, xb), -1, 1)
    return unfold(jnp.where(lax.rem(iota(xa.shape, 1), 2) == 0, west, east), slots, cells)


def spread_rows(rows, got_ya, got_yb, out_ref, slot):
    y_even = lax.rem(lax.axis_index("gy"), 2) == 0
    levels = got_ya.shape[1]
    ya, yb = got_ya[slot], got_yb[slot]
    out_ref[slot, pl.ds(0, levels, stride=rows), :] = jnp.where(y_even, yb, ya)
    out_ref[slot, pl.ds(rows - 1, levels, stride=rows), :] = jnp.where(y_even, ya, yb)


def side_factors(rows, sizes, halo, wet_out, speed, speed_s, band_ref, tracers):
    _, size_x, size_y = sizes
    x = lax.axis_index("gx")
    y = lax.axis_index("gy")
    u = band_ref[0]
    v = band_ref[1]
    wet = band_ref[6]
    cells, width = wet.shape
    speed_s[pl.ds(0, cells // rows, stride=rows), :] = speed[pl.ds(0, cells // rows), :]
    lane = iota((cells, width), 1)
    at_row = lax.rem(iota((cells, width), 0), rows)
    at_w, at_e, at_s, at_n = lane == 0, lane == width - 1, at_row == 0, at_row == rows - 1
    wet_x = wet * turn(halo, -2 * (tracers + 1), 1)
    wet_y = wet * wet_out
    open_w = jnp.where(at_w & (x > 0), wet_x, 0.0)
    open_e = jnp.where(at_e & (x < size_x - 1), wet_x, 0.0)
    open_s = jnp.where(at_s & (y > 0), wet_y, 0.0)
    open_n = jnp.where(at_n & (y < size_y - 1), wet_y, 0.0)
    u_w = turn(halo, -2 * tracers, 1)
    v_s = jnp.where(at_s, speed_s[...], 0.0)
    k_x = lower(open_w, u_w) - upper(open_e, u)
    k_y = lower(open_s, v_s) - upper(open_n, v)
    k_c = (upper(open_w, u_w) - lower(open_e, u)) + (upper(open_s, v_s) - lower(open_n, v))
    return k_x, k_y, k_c


def sideways(rows, factors, halo, outer, c, slot):
    k_x, k_y, k_c = factors
    at_row = lax.rem(iota(c.shape, 0), rows)
    edge = (at_row == 0) | (at_row == rows - 1)
    return (k_x * turn(halo, -2 * slot, 1) + k_c * c) + jnp.where(edge, k_y * outer, 0.0)


def early_kernel(rows, count, sizes, first_step, *refs):
    refs = Refs(refs)
    c_ref, band_ref, got_xa, got_xb, got_ya, got_yb = refs.take(6)
    (speed,) = refs.take(1)
    p_in, part_ref, p_part = refs.take(3)
    if not first_step:
        (wet_in,) = refs.take(1)
    k_ref, halo_ref, spread_s, wet_out, p_ref = refs.take(5)
    msgs, speed_s = refs.refs[:-1], refs.refs[-1]
    g = lax.axis_index("grp")
    tracers, cells, width = c_ref.shape
    base = level_base(rows, cells, count)
    halo = x_halo(got_xa, got_xb, tracers + 3, cells)
    halo_ref[...] = halo
    for slot in range(got_ya.shape[0]):
        spread_rows(rows, got_ya, got_yb, spread_s, slot)
    wet_out[...] = spread_s[tracers + 1] if first_step else wet_in[...]
    factors = side_factors(rows, sizes, halo, wet_out[...], speed, speed_s, band_ref, tracers)
    for at, k in enumerate(factors):
        k_ref[at] = k
    change = sideways(rows, factors, halo, spread_s[tracers], p_in[...], tracers + 2)
    p_ref[...] = p_part[...] + change
    write_pigment(rows, count, p_ref, msgs[0], g)

    def block(at, t):
        here = pl.ds(at, SUB)
        cut = [k[at : at + SUB] for k in factors]
        change = sideways(rows, cut, halo[at : at + SUB], spread_s[t, here, :], c_ref[t, here, :], t)
        return part_ref[t, here, :] + change

    for t in range(tracers):
        write_levels(block(cells - SUB, t), block(0, t), t, rows, base, msgs, g)


def step_kernel(rows, *refs):
    refs = Refs(refs)
    c_ref, part_ref, k_ref, halo_ref, spread_s, w_ref, p_ref = refs.take(7)
    out_ref, msg_xa, msg_xb, msg_ya, msg_yb, mix_ref = refs.take(6)
    tracers = c_ref.shape[0]
    factors = [k_ref[i] for i in range(3)]
    halo = halo_ref[...]
    for t in range(tracers):
        out_ref[t] = part_ref[t] + sideways(rows, factors, halo, spread_s[t], c_ref[t], t)
    pack(rows, out_ref, p_ref, msg_xa, msg_xb, msg_ya, msg_yb)
    mix(w_ref[...], out_ref, mix_ref)


def final_kernel(rows, sizes, first_step, *refs):
    refs = Refs(refs)
    c_ref, part_ref, band_ref, got_xa, got_xb, got_ya, got_yb = refs.take(7)
    (speed,) = refs.take(1)
    if not first_step:
        (wet_in,) = refs.take(1)
    out_hbm, spread_s, speed_s, new_s, sems = refs.take(5)
    tracers, cells, _ = c_ref.shape
    halo = x_halo(got_xa, got_xb, tracers + 3, cells)
    if first_step:
        spread_rows(rows, got_ya, got_yb, spread_s, tracers + 1)
    wet_out = spread_s[tracers + 1] if first_step else wet_in[...]
    factors = side_factors(rows, sizes, halo, wet_out, speed, speed_s, band_ref, tracers)
    copies = []
    for i, (a, n) in enumerate(chunks(tracers, sems.shape[0])):
        for t in range(a, a + n):
            spread_rows(rows, got_ya, got_yb, spread_s, t)
            new_s[t] = part_ref[t] + sideways(rows, factors, halo, spread_s[t], c_ref[t], t)
        copies.append(pltpu.make_async_copy(new_s.at[pl.ds(a, n)], out_hbm.at[pl.ds(a, n)], sems.at[i]))
        copies[-1].start()
    for copy in copies:
        copy.wait()


def call(kernel, ins, outs, in_specs=None, out_specs=None, scratch=(), flops=1 << 20, moved=1 << 20):
    return pl.pallas_call(
        kernel,
        in_specs=[vmem() for _ in ins] if in_specs is None else in_specs,
        out_specs=[vmem() for _ in outs] if out_specs is None else out_specs,
        out_shape=outs,
        scratch_shapes=list(scratch),
        compiler_params=pltpu.CompilerParams(vmem_limit_bytes=VMEM_LIMIT),
        cost_estimate=pl.CostEstimate(flops=flops, bytes_accessed=moved, transcendentals=0),
    )(*ins)


def per_device(
    sizes,
    zonal_boundary_speed,
    meridional_boundary_speed,
    potential_warmth,
    saltiness_field,
    quiescent_mixing_profile,
    substance_amounts,
    submerged_layer_number,
    solar_radiation,
    interaction_rates,
    photosynthetic_rates,
    saturation_irradiance,
    pigment_per_tracer,
):
    count = sizes[0]
    result_dimensions = zonal_boundary_speed.shape
    all_levels, _, strip, width = result_dimensions
    tracers, levels, rows, _ = substance_amounts.shape
    cells = levels * rows
    total = all_levels * rows
    strip_cells = all_levels * strip
    dma = pltpu.SemaphoreType.DMA
    column = pltpu.VMEM((total, width), F32)
    band_s = pltpu.VMEM((cells, width), F32)

    own = [
        f.reshape(strip_cells, width)
        for f in (
            zonal_boundary_speed,
            meridional_boundary_speed,
            potential_warmth,
            saltiness_field,
            quiescent_mixing_profile,
        )
    ]
    _, height = raw_window(rows, count, strip_cells, 0)
    params = [
        p.reshape(1, tracers) for p in (photosynthetic_rates, saturation_irradiance, pigment_per_tracer)
    ]
    (first,) = call(first_kernel, [], [shape(SUB, width)], flops=1 << 30)
    raw, window, pig = call(
        functools.partial(raw_kernel, rows, count),
        [first, params[2], *own],
        [shape(5, strip_cells, width), shape(5 * height, width), shape(1, tracers)],
    )
    raw_others = from_others(window, count)

    messages = message_shapes(tracers, rows, cells, width, count)
    cols = shape(cells, width)
    sent_cols = shape(cells // 2, width) if folds(tracers + 3, cells, width) else cols
    field = shape(tracers, cells, width)
    c = substance_amounts.reshape(tracers, cells, width)
    pigment, *msgs = call(
        functools.partial(prep_kernel, rows, count),
        [pig, c],
        [cols, *messages],
    )
    full = None
    for step in range(STEPS):
        first_step, last_step = step == 0, step == STEPS - 1
        p_others = from_others(msgs[0], count)
        if first_step:
            lines = shape(tracers + 2, levels, width)
            xa, xb, ya, yb, weights, mixed, tiles, depth, solar = call(
                functools.partial(pack_kernel, rows),
                [
                    *params,
                    submerged_layer_number,
                    solar_radiation,
                    c,
                    interaction_rates,
                    pigment,
                ],
                [
                    cols,
                    cols,
                    lines,
                    lines,
                    shape(tracers * SUB, tracers * SUB),
                    field,
                    shape(3, tracers, SUB, width),
                    jax.ShapeDtypeStruct((SUB, width), jnp.int32),
                    shape(SUB, width),
                ],
                flops=1<<24,
            )
        ya = lax.ppermute(ya, AXES, pairing(sizes, "gy", 0))
        yb = lax.ppermute(yb, AXES, pairing(sizes, "gy", 1))
        if count == 2:
            lev = p_others
        else:
            lev = [
                lax.ppermute(msgs[1], "grp", [(i, (i + 1) % count) for i in range(count)]),
                lax.ppermute(msgs[2], "grp", [((i + 1) % count, i) for i in range(count)]),
            ]
        band, xa, xb, speed, *full = call(
            functools.partial(ocean_kernel, rows, count, tracers, first_step),
            [depth, solar, xa, xb, pigment, *p_others, *([raw, *raw_others] if first_step else full)],
            [
                shape(7, cells, width),
                sent_cols,
                sent_cols,
                shape(3 * levels, width),
                *[shape(total, width)] * (5 if first_step else 4),
            ],
            scratch=[column, band_s]
            + [column] * (5 if first_step else 0)
            + [pltpu.VMEM((strip_cells, width), F32)] * (5 * (count - 1) if first_step else 0)
            + [column] * 3,
            flops=1<<32,
        )
        xa = lax.ppermute(xa, AXES, pairing(sizes, "gx", 0))
        xb = lax.ppermute(xb, AXES, pairing(sizes, "gx", 1))
        speed = lax.ppermute(speed, AXES, upward(sizes))
        part, *rest = call(
            functools.partial(inner_kernel, rows, count, last_step),
            [tiles, c, mixed, band, *lev, *(full if last_step else [])],
            [field] + ([shape(strip_cells, width)] * 4 if last_step else [cols]),
            out_specs=[vmem()] + ([hbm()] * 4 if last_step else [vmem()]),
            scratch=[pltpu.VMEM((strip_cells, width), F32)] * 4 + [dma((4,))] if last_step else [],
            flops=1<<10,
        )
        known = [] if first_step else [wet_out]
        if not last_step:
            k, halo, spread, wet_out, pigment_next, *msgs = call(
                functools.partial(early_kernel, rows, count, sizes, first_step),
                [c, band, xa, xb, ya, yb, speed, pigment, part, *rest, *known],
                [shape(3, cells, width), cols, shape(tracers + 2, cells, width), cols, cols, *messages],
                scratch=[band_s],
            )
            pigment = pigment_next
            lines = shape(tracers + (0 if step + 1 == STEPS - 1 else 1), levels, width)
            c, xa, xb, ya, yb, mixed = call(
                functools.partial(step_kernel, rows),
                [c, part, k, halo, spread, weights, pigment],
                [field, cols, cols, lines, lines, field],
                flops=1<<32,
            )
        else:
            ocean = rest
            (c,) = call(
                functools.partial(final_kernel, rows, sizes, first_step),
                [c, part, band, xa, xb, ya, yb, speed, *known],
                [field],
                out_specs=[hbm()],
                scratch=[
                    pltpu.VMEM((tracers + 2, cells, width), F32),
                    band_s,
                    pltpu.VMEM((tracers, cells, width), F32),
                    dma((5,)),
                ],
            )
    return tuple(f.reshape(result_dimensions) for f in ocean) + (c.reshape(substance_amounts.shape),)


def solution(mesh):
    ocean = P(None, "gy", "grp", "gx")
    tracer = P(None, "grp", "gy", "gx")
    surface = P("gy", "gx")
    sizes = tuple(mesh.shape[a] for a in AXES)
    return jax.shard_map(
        functools.partial(per_device, sizes),
        mesh=mesh,
        in_specs=(ocean,) * 5 + (tracer, surface, surface) + (P(),) * 4,
        out_specs=(ocean,) * 4 + (tracer,),
        check_vma=False,
    )
```

```python
import functools

import jax
import jax.numpy as jnp
from jax import lax
from jax.experimental import pallas as pl
from jax.experimental.pallas import tpu as pltpu
from jax.sharding import PartitionSpec as P

STEPS = 2

WATER_ATTEN = 0.01
PIGMENT_ATTEN = 0.05
WARMING_UPTAKE = 5.0
WARM_EXPANSION = 0.2
SALT_EXPANSION = 0.8
CONVECT_MIX = 0.15
SIDE_DIFFUSE = 0.05
WARMING_FACTOR = 0.0633
TIME_STEP = 0.5

SUB = 8
AXES = ("grp", "gx", "gy")
VMEM_LIMIT = 48 * 1024 * 1024

F32 = jnp.float32


def vmem():
    return pl.BlockSpec(memory_space=pltpu.VMEM)


def hbm():
    return pl.BlockSpec(memory_space=pltpu.HBM)


def shape(*dims):
    return jax.ShapeDtypeStruct(dims, F32)


def turn(x, shift, axis):
    shift = shift % x.shape[axis]
    return x if shift == 0 else pltpu.roll(x, shift, axis)


def iota(x, axis):
    return lax.broadcasted_iota(jnp.int32, x, axis)


def pairing(sizes, axis, odd):
    size_g, size_x, size_y = sizes

    def partner(g, x, y):
        i, n = (x, size_x) if axis == "gx" else (y, size_y)
        j = i + 1 if i % 2 == odd else i - 1
        if 0 <= j < n:
            return (g, j, y) if axis == "gx" else (g, x, j)
        if axis == "gx":
            return (g, x, y ^ 1) if (y ^ 1) < size_y else (g, x, y)
        return (g, x ^ 1, y) if (x ^ 1) < size_x else (g, x, y)

    def index(g, x, y):
        return (g * size_x + x) * size_y + y

    return [
        (index(g, x, y), index(*partner(g, x, y)))
        for g in range(size_g)
        for x in range(size_x)
        for y in range(size_y)
    ]


def upward(sizes):
    size_g, size_x, size_y = sizes
    return [
        ((g * size_x + x) * size_y + y, (g * size_x + x) * size_y + (y + 1) % size_y)
        for g in range(size_g)
        for x in range(size_x)
        for y in range(size_y)
    ]


def from_others(value, count):
    return [
        lax.ppermute(value, "grp", [(i, (i + k) % count) for i in range(count)])
        for k in range(1, count)
    ]


def chunks(n, parts):
    step = -(-n // parts)
    return [(a, min(step, n - a)) for a in range(0, n, step)]


class Refs:
    def __init__(self, refs):
        self.refs = list(refs)

    def take(self, n):
        out, self.refs = self.refs[:n], self.refs[n:]
        return out


def pick(mine, others, k):
    value = mine
    for at, other in enumerate(others):
        value = jnp.where(k == at + 1, other, value)
    return value


def folds(slots, cells, width):
    return 4 * slots < width and cells % (2 * SUB) == 0


def halves_of(cells, slots, width):
    if not folds(slots, cells, width):
        return [(slice(0, cells), 0)]
    return [(slice(0, cells // 2), 0), (slice(cells // 2, cells), width // 2)]


def pack_sides(c, slot, slots, left, right):
    cells, width = c.shape
    at = 2 * (slot + 1)
    lane = iota(left.shape, 1)
    for rows, base in halves_of(cells, slots, width):
        left = jnp.where(lane == base + at - 1, turn(c[rows], base + at - 1, 1), left)
        right = jnp.where(lane == base + at, turn(c[rows], base + at + 1, 1), right)
    return left, right


def sides_of(halo, slot, slots, cells):
    at = 2 * (slot + 1)
    width = halo.shape[1]
    turned = [turn(halo, -at - base, 1) for _, base in halves_of(cells, slots, width)]
    return turned[0] if len(turned) == 1 else jnp.concatenate(turned, axis=0)


def compact(rows, cells, count):
    return count == 2 and SUB == 2 * rows and cells >= 2 * SUB


def level_base(rows, cells, count, together):
    if not together:
        return SUB - rows
    return cells // 2 + SUB if compact(rows, cells, count) else cells


def message_shapes(tracers, rows, cells, width, count, together):
    height = level_base(rows, cells, count, together) + tracers * rows + (SUB - rows)
    height += -height % SUB
    if together:
        return [shape(height, width)]
    pigment = cells // 2 + SUB if compact(rows, cells, count) else cells
    return [shape(pigment, width)] + [shape(height, width)] * (1 if count == 2 else 2)


def write_levels(last, first, t, rows, base, msgs, g):
    here = pl.ds(base + t * rows, rows)
    if len(msgs) < 3:
        msgs[-1][here, :] = jnp.where(g == 0, last[SUB - rows :], first[:rows])
    else:
        msgs[1][here, :] = last[SUB - rows :]
        msgs[2][here, :] = first[:rows]


def in_strip(rows, count, width, member):
    at_row = lax.rem(iota((SUB, width), 0), rows)
    strip = rows // count
    return (at_row >= member * strip) & (at_row < (member + 1) * strip)


def write_pigment(rows, count, p_ref, msg, g):
    cells, width = p_ref.shape
    if not compact(rows, cells, count):
        msg[pl.ds(0, cells), :] = p_ref[...]
        return
    levels, strip = cells // rows, rows // count
    for r in range(strip):
        msg[pl.ds(r, levels, stride=strip), :] = jnp.where(
            g == 0, p_ref[pl.ds(strip + r, levels, stride=rows), :], p_ref[pl.ds(r, levels, stride=rows), :]
        )
    blocks = [p_ref[pl.ds(at, SUB), :] for at in range(0, cells, SUB)]
    inner = blocks[1]
    for block in blocks[2:-1]:
        inner = inner + block
    inner = jnp.zeros_like(inner) if len(blocks) == 2 else inner
    near = jnp.where(g == 0, blocks[-1], blocks[0])
    rest = inner + jnp.where(g == 0, blocks[0], blocks[-1])
    rest = rest + turn(rest, rows, 0)
    msg[pl.ds(cells // 2, SUB), :] = jnp.where(in_strip(rows, count, width, g), near, turn(rest, strip, 0))


def read_pigment(rows, count, msg, other_s, g):
    cells, width = other_s.shape
    if not compact(rows, cells, count):
        return msg[pl.ds(0, cells), :]
    levels, strip = cells // rows, rows // count
    for s in range(count):
        for r in range(strip):
            other_s[pl.ds(s * strip + r, levels, stride=rows), :] = jnp.where(
                g == s, msg[pl.ds(r, levels, stride=strip), :], 0.0
            )
    edge = msg[pl.ds(cells // 2, SUB), :]
    theirs = in_strip(rows, count, width, 1 - g)
    first = other_s[pl.ds(0, SUB), :]
    rest = jnp.where(iota((SUB, width), 0) < rows, turn(edge, strip, 0), 0.0)
    other_s[pl.ds(0, SUB), :] = jnp.where(theirs, jnp.where(g == 0, edge, rest), first)
    last = other_s[pl.ds(cells - SUB, SUB), :]
    other_s[pl.ds(cells - SUB, SUB), :] = jnp.where(theirs & (g == 1), edge, last)
    return other_s[...]


def raw_window(rows, count, strip_cells, member):
    if count != 2:
        return 0, strip_cells
    height = strip_cells // 2 + 2 * (rows // count)
    return member * (strip_cells - height), height


def first_kernel(out_ref):
    out_ref[...] = jnp.zeros(out_ref.shape, F32)


def raw_kernel(rows, count, first_ref, *refs):
    refs = Refs(refs)
    fields, small_in = refs.take(5), refs.take(6)
    raw_ref, out_ref = refs.take(2)
    g = lax.axis_index("grp")
    for small, small_out in zip(small_in, refs.take(6)):
        small_out[...] = small[...]
    strip_cells = raw_ref.shape[1]
    low, height = raw_window(rows, count, strip_cells, 0)
    high, _ = raw_window(rows, count, strip_cells, 1)
    for at, field in enumerate(fields):
        raw_ref[at] = field[...]
        lower_part, upper_part = field[pl.ds(low, height), :], field[pl.ds(high, height), :]
        out_ref[pl.ds(at * height, height), :] = jnp.where(g == 0, upper_part, lower_part)


def tile(v, cells):
    width = v.shape[1]
    return jnp.broadcast_to(v[None], (cells // SUB, SUB, width)).reshape(cells, width)


def prep_kernel(rows, count, pig_ref, c_ref, p_ref, *msgs):
    g = lax.axis_index("grp")
    tracers, cells, width = c_ref.shape
    base = level_base(rows, cells, count, False)
    weights = pig_ref[...]
    pigment = jnp.zeros((cells, width), F32)
    for t in range(tracers):
        c = c_ref[t]
        pigment = pigment + tile(jnp.broadcast_to(weights[:, t : t + 1], (SUB, width)), cells) * c
        write_levels(c[cells - SUB :], c[:SUB], t, rows, base, msgs, g)
    p_ref[...] = pigment
    write_pigment(rows, count, p_ref, msgs[0], g)


def halves(v):
    high = v.astype(jnp.bfloat16)
    return high, (v - high.astype(F32)).astype(jnp.bfloat16)


def dot(a, b, **kw):
    return jnp.dot(a, b, preferred_element_type=F32, **kw)


def spread_rates(rates, tracers):
    exact = functools.partial(dot, precision=lax.Precision.HIGHEST)
    depth = tracers * SUB
    spread = jnp.where(iota((depth, tracers), 0) // SUB == iota((depth, tracers), 1), 1.0, 0.0)
    spread_t = jnp.where(iota((tracers, depth), 1) // SUB == iota((tracers, depth), 0), 1.0, 0.0)
    weights = exact(exact(spread, rates), spread_t)
    return jnp.where(
        lax.rem(iota((depth, depth), 0), SUB) == lax.rem(iota((depth, depth), 1), SUB), weights, 0.0
    )


def mix(weights, c_ref, mix_ref):
    tracers, cells, width = c_ref.shape
    w_high, w_low = halves(weights)
    for b in range(cells // SUB):
        here = pl.ds(b * SUB, SUB)
        c_high, c_low = halves(c_ref[:, here, :].reshape(tracers * SUB, width))
        mixed = dot(w_high, c_high) + (dot(w_high, c_low) + dot(w_low, c_high))
        mix_ref[:, here, :] = mixed.reshape(tracers, SUB, width)


def put_rows(msg_ya, msg_yb, slot, first, last):
    y_even = lax.rem(lax.axis_index("gy"), 2) == 0
    msg_ya[slot] = jnp.where(y_even, last, first)
    msg_yb[slot] = jnp.where(y_even, first, last)


def pack(rows, c_ref, p_ref, msg_xa, msg_xb, msg_ya, msg_yb):
    tracers, cells, _ = c_ref.shape
    levels = cells // rows
    x_even = lax.rem(lax.axis_index("gx"), 2) == 0
    left = right = jnp.zeros(msg_xa.shape, F32)
    left, right = pack_sides(p_ref[...], tracers + 2, tracers + 3, left, right)
    for t in range(tracers):
        left, right = pack_sides(c_ref[t], t, tracers + 3, left, right)
    msg_xa[...] = jnp.where(x_even, right, left)
    msg_xb[...] = jnp.where(x_even, left, right)
    first, last = pl.ds(0, levels, stride=rows), pl.ds(rows - 1, levels, stride=rows)
    for t in range(tracers):
        put_rows(msg_ya, msg_yb, t, c_ref[t, first, :], c_ref[t, last, :])
    if msg_ya.shape[0] > tracers:
        put_rows(msg_ya, msg_yb, tracers, p_ref[first, :], p_ref[last, :])


def pack_kernel(rows, *refs):
    refs = Refs(refs)
    depth_in, solar_in, c_ref, p_ref = refs.take(4)
    msg_xa, msg_xb, msg_ya, msg_yb, depth_ref, solar_ref = refs.take(6)
    tracers, cells, width = c_ref.shape
    for r in range(0, SUB, rows):
        depth_ref[pl.ds(r, rows), :] = depth_in[...]
        solar_ref[pl.ds(r, rows), :] = solar_in[...]
    pack(rows, c_ref, p_ref, msg_xa, msg_xb, msg_ya, msg_yb)
    levels = cells // rows
    level = lax.axis_index("grp") * levels + iota((levels, width), 0)
    wet_first = jnp.where(level < depth_in[pl.ds(0, 1), :], 1.0, 0.0)
    wet_last = jnp.where(level < depth_in[pl.ds(rows - 1, 1), :], 1.0, 0.0)
    put_rows(msg_ya, msg_yb, tracers + 1, wet_first, wet_last)


def ocean_kernel(rows, count, tracers, first_step, *refs):
    refs = Refs(refs)
    depth_ref, solar_ref = refs.take(2)
    in_xa, in_xb = refs.take(2)
    p_own, *p_others = refs.take(count)
    if first_step:
        own_fields, *other_fields = refs.take(count)
    else:
        fields = refs.take(5)
    band_ref, msg_xa, msg_xb, speed_ref = refs.take(4)
    full_out = refs.take(5 if first_step else 4)
    p_full, p_other_s = refs.take(2)
    if first_step:
        fields = refs.take(5)
        other_s = refs.take(5 * (count - 1))
    face_s, par_s, wet_s = refs.take(3)
    g = lax.axis_index("grp")
    cells, width = p_own.shape
    levels = cells // rows
    total = count * cells
    all_levels = total // rows
    strip = rows // count

    pigments = [read_pigment(rows, count, o, p_other_s, g) for o in p_others]
    for b in range(count):
        k = lax.rem(g - b + count, count)
        p_full[pl.ds(b * cells, cells), :] = pick(p_own[...], pigments, k)
    if first_step:
        strip_cells = all_levels * strip
        for at in range(5):
            for k in range(count - 1):
                other = other_s[5 * k + at]
                low, height = raw_window(rows, count, strip_cells, 0)
                value = other_fields[k][pl.ds(at * height, height), :]
                if count != 2:
                    other[...] = value
                    continue
                high, _ = raw_window(rows, count, strip_cells, 1)
                other[...] = jnp.zeros((strip_cells, width), F32)
                other[pl.ds(low, height), :] = jnp.where(g == 0, value, 0.0)
                kept = jnp.where(iota(value.shape, 0) < low + height - high, other[pl.ds(high, height), :], 0.0)
                other[pl.ds(high, height), :] = jnp.where(g == 1, value, kept)
            for s in range(count):
                k = lax.rem(g - s + count, count)
                for r in range(strip):
                    here = pl.ds(r, all_levels, stride=strip)
                    fields[at][pl.ds(s * strip + r, all_levels, stride=rows), :] = pick(
                        own_fields[at, here, :], [other_s[5 * j + at][here, :] for j in range(count - 1)], k
                    )

    row = iota((total, width), 0)
    wet = jnp.where(row // rows < tile(depth_ref[...], total), 1.0, 0.0)
    att = WATER_ATTEN + PIGMENT_ATTEN * p_full[...]
    summed = att
    step = rows
    while step < total:
        summed = summed + jnp.where(row >= step, turn(summed, step, 0), 0.0)
        step *= 2
    top = tile(solar_ref[...], total) * jnp.exp(att - summed)
    par = top * jnp.exp(-0.5 * att)
    east, north, temp, sal, mixing = [f[...] for f in fields]
    temp = temp + WARMING_UPTAKE * (top * (1.0 - jnp.exp(-att))) * wet

    def below(v):
        return turn(v, -rows, 0)

    density = SALT_EXPANSION * sal - WARM_EXPANSION * temp
    face = 0.5 * (mixing + below(mixing)) + CONVECT_MIX / (1.0 + jnp.exp(below(density) - density))
    face = jnp.where(row < total - rows, face * below(wet), 0.0)

    def stir(v):
        flux = face * (below(v) - v)
        return v + flux - turn(flux, rows, 0)

    for at, v in enumerate((east, north, temp, sal)):
        full_out[at][...] = stir(v)
    if first_step:
        full_out[4][...] = mixing
    face_s[...] = face
    par_s[...] = par
    wet_s[...] = wet

    band = pl.ds(pl.multiple_of(g * cells, SUB), cells)
    above = pl.ds(pl.multiple_of(lax.max(g * cells - SUB, 0), SUB), SUB)
    face_band = face_s[band, :]
    lifted = turn(jnp.concatenate([face_s[above, :], face_band], axis=0), rows, 0)[SUB:]
    lifted = jnp.where((iota((cells, width), 0) < rows) & (g == 0), 0.0, lifted)
    u = full_out[0][band, :]
    wet_band = wet_s[band, :]
    band_ref[0] = u
    band_ref[1] = full_out[1][band, :]
    band_ref[2] = full_out[2][band, :]
    band_ref[3] = face_band
    band_ref[4] = lifted
    band_ref[5] = par_s[band, :]
    band_ref[6] = wet_band

    x_even = lax.rem(lax.axis_index("gx"), 2) == 0
    xa, xb = in_xa[...], in_xb[...]
    left, right = jnp.where(x_even, xb, xa), jnp.where(x_even, xa, xb)
    left, right = pack_sides(wet_band, tracers + 1, tracers + 3, left, right)
    _, right = pack_sides(u, tracers, tracers + 3, left, right)
    msg_xa[...] = jnp.where(x_even, right, left)
    msg_xb[...] = jnp.where(x_even, left, right)
    speed_ref[pl.ds(0, levels), :] = band_ref[1, pl.ds(rows - 1, levels, stride=rows), :]
    speed_ref[pl.ds(levels, levels), :] = jnp.zeros((levels, width), F32)
    speed_ref[pl.ds(2 * levels, levels), :] = jnp.zeros((levels, width), F32)


def start_own_strip(rows, count, g, full, outs, strips, sems):
    strip = rows // count
    all_levels = full[0].shape[0] // rows
    copies = [pltpu.make_async_copy(strips[at], outs[at], sems.at[at]) for at in range(4)]
    for at in range(4):
        for r in range(strip):
            value = full[at][pl.ds(r, all_levels, stride=rows), :]
            for s in range(1, count):
                value = jnp.where(g == s, full[at][pl.ds(s * strip + r, all_levels, stride=rows), :], value)
            strips[at][pl.ds(r, all_levels, stride=strip), :] = value
        copies[at].start()
    return copies


def lower(opening, speed):
    return opening * (jnp.maximum(speed, 0.0) + SIDE_DIFFUSE)


def upper(opening, speed):
    return opening * (jnp.minimum(speed, 0.0) - SIDE_DIFFUSE)


def inner_kernel(rows, count, first_step, last_step, *refs):
    refs = Refs(refs)
    if first_step:
        params, (rates_ref,) = refs.take(3), refs.take(1)
    else:
        tiles_ref, w_ref = refs.take(2)
    c_ref, band_ref = refs.take(2)
    lev_in = refs.take(1 if count == 2 else 2)
    if last_step:
        full = refs.take(4)
    (part_ref,) = refs.take(1)
    if last_step:
        outs = refs.take(4)
    else:
        (p_part,) = refs.take(1)
    if first_step:
        tiles_ref, w_ref = refs.take(2)
    if last_step:
        strips, (sems,) = refs.take(4), refs.take(1)
        copies = start_own_strip(rows, count, lax.axis_index("grp"), full, outs, strips, sems)
    (mix_ref,) = refs.take(1)
    tracers, cells, width = c_ref.shape
    if first_step:
        w_ref[...] = spread_rates(rates_ref[...], tracers)
        for at, param in enumerate(params):
            values = param[...]
            for t in range(tracers):
                tiles_ref[at, t] = jnp.broadcast_to(values[:, t : t + 1], (SUB, width))
    mix(w_ref[...], c_ref, mix_ref)
    base = level_base(rows, cells, count, False)
    lane = iota((cells, width), 1)
    at_row = lax.rem(iota((cells, width), 0), rows)
    u = band_ref[0]
    v = band_ref[1]
    wet = band_ref[6]

    def west(x):
        return turn(x, 1, 1)

    def east(x):
        return turn(x, -1, 1)

    def south(x):
        return turn(x, 1, 0)

    def north(x):
        return turn(x, -1, 0)

    open_w = jnp.where(lane == 0, 0.0, wet * west(wet))
    open_e = jnp.where(lane == width - 1, 0.0, wet * east(wet))
    open_s = jnp.where(at_row == 0, 0.0, wet * south(wet))
    open_n = jnp.where(at_row == rows - 1, 0.0, wet * north(wet))
    k_w = lower(open_w, west(u))
    k_e = -upper(open_e, u)
    k_s = lower(open_s, south(v))
    k_n = -upper(open_n, v)
    k_d = band_ref[3]
    k_u = band_ref[4]
    k_c = (upper(open_w, west(u)) - lower(open_e, u)) + (upper(open_s, south(v)) - lower(open_n, v))
    k_c = 1.0 + (k_c - k_d - k_u)
    par = band_ref[5]
    lit = TIME_STEP * wet
    warm = lit * jnp.exp(WARMING_FACTOR * (band_ref[2] - 20.0))
    lit = lit * par
    pigment = jnp.zeros((cells, width), F32)
    for t in range(tracers):
        c = c_ref[t]
        at = base + t * rows
        up8 = lev_in[0][pl.ds(at + rows - SUB, SUB), :]
        down8 = lev_in[-1][pl.ds(at, SUB), :]
        c_u = turn(jnp.concatenate([up8, c], axis=0), rows, 0)[SUB:]
        c_d = turn(jnp.concatenate([c, down8], axis=0), -rows, 0)[:cells]
        part = (
            (k_c + tile(tiles_ref[0, t], cells) * (lit / (par + tile(tiles_ref[1, t], cells)))) * c
            + (k_u * c_u + k_d * c_d)
            + (k_w * west(c) + k_e * east(c))
            + (k_s * south(c) + k_n * north(c))
            + warm * mix_ref[t]
        )
        part_ref[t] = part
        if not last_step:
            pigment = pigment + tile(tiles_ref[2, t], cells) * part
    if last_step:
        for copy in copies:
            copy.wait()
    else:
        p_part[...] = pigment


def x_halo(got_xa, got_xb):
    x_even = lax.rem(lax.axis_index("gx"), 2) == 0
    xa, xb = got_xa[...], got_xb[...]
    return jnp.where((lax.rem(iota(xa.shape, 1), 2) == 0) == x_even, xb, xa)


def spread_rows(rows, got_ya, got_yb, out_ref, slot):
    y_even = lax.rem(lax.axis_index("gy"), 2) == 0
    levels = got_ya.shape[1]
    ya, yb = got_ya[slot], got_yb[slot]
    out_ref[slot, pl.ds(0, levels, stride=rows), :] = jnp.where(y_even, yb, ya)
    out_ref[slot, pl.ds(rows - 1, levels, stride=rows), :] = jnp.where(y_even, ya, yb)


def side_factors(rows, sizes, halo_ref, wet_out, speed, speed_s, band_ref, tracers):
    _, size_x, size_y = sizes
    x = lax.axis_index("gx")
    y = lax.axis_index("gy")
    u = band_ref[0]
    v = band_ref[1]
    wet = band_ref[6]
    cells, width = wet.shape
    speed_s[pl.ds(0, cells // rows, stride=rows), :] = speed[pl.ds(0, cells // rows), :]
    lane = iota((cells, width), 1)
    at_row = lax.rem(iota((cells, width), 0), rows)
    at_w, at_e, at_s, at_n = lane == 0, lane == width - 1, at_row == 0, at_row == rows - 1
    wet_x = wet * sides_of(halo_ref[...], tracers + 1, tracers + 3, cells)
    wet_y = wet * wet_out
    open_w = jnp.where(at_w & (x > 0), wet_x, 0.0)
    open_e = jnp.where(at_e & (x < size_x - 1), wet_x, 0.0)
    open_s = jnp.where(at_s & (y > 0), wet_y, 0.0)
    open_n = jnp.where(at_n & (y < size_y - 1), wet_y, 0.0)
    u_w = sides_of(halo_ref[...], tracers, tracers + 3, cells)
    v_s = jnp.where(at_s, speed_s[...], 0.0)
    k_x = lower(open_w, u_w) - upper(open_e, u)
    k_y = lower(open_s, v_s) - upper(open_n, v)
    k_c = (upper(open_w, u_w) - lower(open_e, u)) + (upper(open_s, v_s) - lower(open_n, v))
    return k_x, k_y, k_c


def sideways(rows, factors, sides, outer, c):
    k_x, k_y, k_c = factors
    at_row = lax.rem(iota(c.shape, 0), rows)
    edge = (at_row == 0) | (at_row == rows - 1)
    return (k_x * sides + k_c * c) + jnp.where(edge, k_y * outer, 0.0)


def early_kernel(rows, count, sizes, first_step, *refs):
    refs = Refs(refs)
    c_ref, band_ref, got_xa, got_xb, got_ya, got_yb = refs.take(6)
    (speed,) = refs.take(1)
    p_in, part_ref, p_part = refs.take(3)
    if not first_step:
        (wet_in,) = refs.take(1)
    k_ref, halo_ref, spread_s, wet_out, p_ref = refs.take(5)
    msgs, speed_s = refs.refs[:-1], refs.refs[-1]
    g = lax.axis_index("grp")
    tracers, cells, width = c_ref.shape
    lev_base = level_base(rows, cells, count, False)
    halo_ref[...] = x_halo(got_xa, got_xb)
    for slot in range(got_ya.shape[0]):
        spread_rows(rows, got_ya, got_yb, spread_s, slot)
    wet_out[...] = spread_s[tracers + 1] if first_step else wet_in[...]
    factors = side_factors(rows, sizes, halo_ref, wet_out[...], speed, speed_s, band_ref, tracers)
    for at, k in enumerate(factors):
        k_ref[at] = k
    side = sides_of(halo_ref[...], tracers + 2, tracers + 3, cells)
    change = sideways(rows, factors, side, spread_s[tracers], p_in[...])
    p_ref[...] = p_part[...] + change
    write_pigment(rows, count, p_ref, msgs[0], g)

    def block(at, t):
        here = pl.ds(at, SUB)
        cut = [k[at : at + SUB] for k in factors]
        for part, base in halves_of(cells, tracers + 3, width):
            if part.start <= at < part.stop:
                side = turn(halo_ref[pl.ds(at - part.start, SUB), :], -2 * (t + 1) - base, 1)
        change = sideways(rows, cut, side, spread_s[t, here, :], c_ref[t, here, :])
        return part_ref[t, here, :] + change

    for t in range(tracers):
        write_levels(block(cells - SUB, t), block(0, t), t, rows, lev_base, msgs, g)


def step_kernel(rows, *refs):
    refs = Refs(refs)
    c_ref, part_ref, k_ref, halo_ref, spread_s, p_ref = refs.take(6)
    out_ref, msg_xa, msg_xb, msg_ya, msg_yb = refs.take(5)
    tracers = c_ref.shape[0]
    factors = [k_ref[i] for i in range(3)]
    for t in range(tracers):
        out_ref[t] = part_ref[t] + sideways(
                rows, factors, sides_of(halo_ref[...], t, tracers + 3, c_ref.shape[1]), spread_s[t], c_ref[t]
            )
    pack(rows, out_ref, p_ref, msg_xa, msg_xb, msg_ya, msg_yb)


def final_kernel(rows, sizes, first_step, *refs):
    refs = Refs(refs)
    c_ref, part_ref, band_ref, got_xa, got_xb, got_ya, got_yb = refs.take(7)
    (speed,) = refs.take(1)
    if not first_step:
        (wet_in,) = refs.take(1)
    out_hbm, spread_s, speed_s, halo_ref, new_s, sems = refs.take(6)
    tracers = c_ref.shape[0]
    halo_ref[...] = x_halo(got_xa, got_xb)
    if first_step:
        spread_rows(rows, got_ya, got_yb, spread_s, tracers + 1)
    wet_out = spread_s[tracers + 1] if first_step else wet_in[...]
    factors = side_factors(rows, sizes, halo_ref, wet_out, speed, speed_s, band_ref, tracers)
    copies = []
    for i, (a, n) in enumerate(chunks(tracers, sems.shape[0])):
        for t in range(a, a + n):
            spread_rows(rows, got_ya, got_yb, spread_s, t)
            new_s[t] = part_ref[t] + sideways(
                rows, factors, sides_of(halo_ref[...], t, tracers + 3, c_ref.shape[1]), spread_s[t], c_ref[t]
            )
        copies.append(pltpu.make_async_copy(new_s.at[pl.ds(a, n)], out_hbm.at[pl.ds(a, n)], sems.at[i]))
        copies[-1].start()
    for copy in copies:
        copy.wait()


def call(kernel, ins, outs, in_specs=None, out_specs=None, scratch=(), flops=1 << 20, moved=1 << 20):
    return pl.pallas_call(
        kernel,
        in_specs=[vmem() for _ in ins] if in_specs is None else in_specs,
        out_specs=[vmem() for _ in outs] if out_specs is None else out_specs,
        out_shape=outs,
        scratch_shapes=list(scratch),
        compiler_params=pltpu.CompilerParams(vmem_limit_bytes=VMEM_LIMIT),
        cost_estimate=pl.CostEstimate(flops=flops, bytes_accessed=moved, transcendentals=0),
    )(*ins)


def per_device(
    sizes,
    zonal_boundary_speed,
    meridional_boundary_speed,
    potential_warmth,
    saltiness_field,
    quiescent_mixing_profile,
    substance_amounts,
    submerged_layer_number,
    solar_radiation,
    interaction_rates,
    photosynthetic_rates,
    saturation_irradiance,
    pigment_per_tracer,
):
    count = sizes[0]
    result_dimensions = zonal_boundary_speed.shape
    all_levels, _, strip, width = result_dimensions
    tracers, levels, rows, _ = substance_amounts.shape
    cells = levels * rows
    total = all_levels * rows
    strip_cells = all_levels * strip
    dma = pltpu.SemaphoreType.DMA
    column = pltpu.VMEM((total, width), F32)
    band_s = pltpu.VMEM((cells, width), F32)

    own = [
        f.reshape(strip_cells, width)
        for f in (
            zonal_boundary_speed,
            meridional_boundary_speed,
            potential_warmth,
            saltiness_field,
            quiescent_mixing_profile,
        )
    ]
    _, height = raw_window(rows, count, strip_cells, 0)
    params = [
        p.reshape(1, tracers) for p in (photosynthetic_rates, saturation_irradiance, pigment_per_tracer)
    ]
    (first,) = call(first_kernel, [], [shape(SUB, width)], flops=1 << 30)
    small = [*params, interaction_rates, submerged_layer_number, solar_radiation]
    raw, window, *small = call(
        functools.partial(raw_kernel, rows, count),
        [first, *own, *small],
        [
            shape(5, strip_cells, width),
            shape(5 * height, width),
            *[jax.ShapeDtypeStruct(v.shape, v.dtype) for v in small],
        ],
    )
    *params, rates, layers, light = small
    raw_others = from_others(window, count)

    messages = message_shapes(tracers, rows, cells, width, count, False)
    cols = shape(cells, width)
    sent_cols = shape(cells // 2, width) if folds(tracers + 3, cells, width) else cols
    field = shape(tracers, cells, width)
    c = substance_amounts.reshape(tracers, cells, width)
    pigment, *msgs = call(
        functools.partial(prep_kernel, rows, count),
        [params[2], c],
        [cols, *message_shapes(tracers, rows, cells, width, count, False)],
    )
    full = None
    for step in range(STEPS):
        first_step, last_step = step == 0, step == STEPS - 1
        p_others = from_others(msgs[0], count)
        if first_step:
            lines = shape(tracers + 2, levels, width)
            xa, xb, ya, yb, depth, solar = call(
                functools.partial(pack_kernel, rows),
                [layers, light, c, pigment],
                [
                    sent_cols,
                    sent_cols,
                    lines,
                    lines,
                    jax.ShapeDtypeStruct((SUB, width), jnp.int32),
                    shape(SUB, width),
                ],
                flops=1 << 24,
            )
        ya = lax.ppermute(ya, AXES, pairing(sizes, "gy", 0))
        yb = lax.ppermute(yb, AXES, pairing(sizes, "gy", 1))
        if count == 2:
            lev = from_others(msgs[-1], count)
        else:
            lev = [
                lax.ppermute(msgs[1], "grp", [(i, (i + 1) % count) for i in range(count)]),
                lax.ppermute(msgs[2], "grp", [((i + 1) % count, i) for i in range(count)]),
            ]
        band, xa, xb, speed, *full = call(
            functools.partial(ocean_kernel, rows, count, tracers, first_step),
            [depth, solar, xa, xb, pigment, *p_others, *([raw, *raw_others] if first_step else full)],
            [
                shape(7, cells, width),
                sent_cols,
                sent_cols,
                shape(3 * levels, width),
                *[shape(total, width)] * (5 if first_step else 4),
            ],
            scratch=[column, band_s]
            + [column] * (5 if first_step else 0)
            + [pltpu.VMEM((strip_cells, width), F32)] * (5 * (count - 1) if first_step else 0)
            + [column] * 3,
            flops=1<<32,
        )
        xa = lax.ppermute(xa, AXES, pairing(sizes, "gx", 0))
        xb = lax.ppermute(xb, AXES, pairing(sizes, "gx", 1))
        speed = lax.ppermute(speed, AXES, upward(sizes))
        tables = [shape(3, tracers, SUB, width), shape(tracers * SUB, tracers * SUB)]
        part, *rest = call(
            functools.partial(inner_kernel, rows, count, first_step, last_step),
            [*([*params, rates] if first_step else known_rates), c, band, *lev, *(full if last_step else [])],
            [field]
            + ([shape(strip_cells, width)] * 4 if last_step else [cols])
            + (tables if first_step else []),
            out_specs=[vmem()]
            + ([hbm()] * 4 if last_step else [vmem()])
            + ([vmem()] * 2 if first_step else []),
            scratch=([pltpu.VMEM((strip_cells, width), F32)] * 4 + [dma((4,))] if last_step else [])
            + [pltpu.VMEM((tracers, cells, width), F32)],
            flops=1 << 10,
        )
        if first_step:
            *rest, tiles, weights = rest
            known_rates = [tiles, weights]
        known = [] if first_step else [wet_out]
        if not last_step:
            k, halo, spread, wet_out, pigment_next, *msgs = call(
                functools.partial(early_kernel, rows, count, sizes, first_step),
                [c, band, xa, xb, ya, yb, speed, pigment, part, *rest, *known],
                [shape(3, cells, width), sent_cols, shape(tracers + 2, cells, width), cols, cols, *messages],
                scratch=[band_s],
            )
            pigment = pigment_next
            lines = shape(tracers + (0 if step + 1 == STEPS - 1 else 1), levels, width)
            c, xa, xb, ya, yb = call(
                functools.partial(step_kernel, rows),
                [c, part, k, halo, spread, pigment],
                [field, sent_cols, sent_cols, lines, lines],
                flops=1<<32,
            )
        else:
            ocean = rest
            (c,) = call(
                functools.partial(final_kernel, rows, sizes, first_step),
                [c, part, band, xa, xb, ya, yb, speed, *known],
                [field],
                out_specs=[hbm()],
                scratch=[
                    pltpu.VMEM((tracers + 2, cells, width), F32),
                    band_s,
                    pltpu.VMEM(sent_cols.shape, F32),
                    pltpu.VMEM((tracers, cells, width), F32),
                    dma((5,)),
                ],
            )
    return tuple(f.reshape(result_dimensions) for f in ocean) + (c.reshape(substance_amounts.shape),)


def solution(mesh):
    ocean = P(None, "gy", "grp", "gx")
    tracer = P(None, "grp", "gy", "gx")
    surface = P("gy", "gx")
    sizes = tuple(mesh.shape[a] for a in AXES)
    return jax.shard_map(
        functools.partial(per_device, sizes),
        mesh=mesh,
        in_specs=(ocean,) * 5 + (tracer, surface, surface) + (P(),) * 4,
        out_specs=(ocean,) * 4 + (tracer,),
        check_vma=False,
    )
```

```python
import functools

import jax
import jax.numpy as jnp
from jax import lax
from jax.experimental import pallas as pl
from jax.experimental.pallas import tpu as pltpu
from jax.sharding import PartitionSpec as P

STEPS = 2

WATER_ATTEN = 0.01
PIGMENT_ATTEN = 0.05
WARMING_UPTAKE = 5.0
WARM_EXPANSION = 0.2
SALT_EXPANSION = 0.8
CONVECT_MIX = 0.15
SIDE_DIFFUSE = 0.05
WARMING_FACTOR = 0.0633
TIME_STEP = 0.5

SUB = 8
AXES = ("grp", "gx", "gy")
VMEM_LIMIT = 48 * 1024 * 1024

F32 = jnp.float32


def vmem():
    return pl.BlockSpec(memory_space=pltpu.VMEM)


def hbm():
    return pl.BlockSpec(memory_space=pltpu.HBM)


def shape(*dims):
    return jax.ShapeDtypeStruct(dims, F32)


def turn(x, shift, axis):
    shift = shift % x.shape[axis]
    return x if shift == 0 else pltpu.roll(x, shift, axis)


def iota(x, axis):
    return lax.broadcasted_iota(jnp.int32, x, axis)


def pairing(sizes, axis, odd):
    size_g, size_x, size_y = sizes

    def partner(g, x, y):
        i, n = (x, size_x) if axis == "gx" else (y, size_y)
        j = i + 1 if i % 2 == odd else i - 1
        if 0 <= j < n:
            return (g, j, y) if axis == "gx" else (g, x, j)
        if axis == "gx":
            return (g, x, y ^ 1) if (y ^ 1) < size_y else (g, x, y)
        return (g, x ^ 1, y) if (x ^ 1) < size_x else (g, x, y)

    def index(g, x, y):
        return (g * size_x + x) * size_y + y

    return [
        (index(g, x, y), index(*partner(g, x, y)))
        for g in range(size_g)
        for x in range(size_x)
        for y in range(size_y)
    ]


def upward(sizes):
    size_g, size_x, size_y = sizes
    return [
        ((g * size_x + x) * size_y + y, (g * size_x + x) * size_y + (y + 1) % size_y)
        for g in range(size_g)
        for x in range(size_x)
        for y in range(size_y)
    ]


def from_others(value, count):
    return [
        lax.ppermute(value, "grp", [(i, (i + k) % count) for i in range(count)])
        for k in range(1, count)
    ]


def chunks(n, parts):
    step = -(-n // parts)
    return [(a, min(step, n - a)) for a in range(0, n, step)]


class Refs:
    def __init__(self, refs):
        self.refs = list(refs)

    def take(self, n):
        out, self.refs = self.refs[:n], self.refs[n:]
        return out


def pick(mine, others, k):
    value = mine
    for at, other in enumerate(others):
        value = jnp.where(k == at + 1, other, value)
    return value


def folds(slots, cells, width):
    return 4 * slots < width and cells % (2 * SUB) == 0


def halves_of(cells, slots, width):
    if not folds(slots, cells, width):
        return [(slice(0, cells), 0)]
    return [(slice(0, cells // 2), 0), (slice(cells // 2, cells), width // 2)]


def pack_sides(c, slot, slots, left, right):
    cells, width = c.shape
    at = 2 * (slot + 1)
    lane = iota(left.shape, 1)
    for rows, base in halves_of(cells, slots, width):
        left = jnp.where(lane == base + at - 1, turn(c[rows], base + at - 1, 1), left)
        right = jnp.where(lane == base + at, turn(c[rows], base + at + 1, 1), right)
    return left, right


def sides_of(halo, slot, slots, cells):
    at = 2 * (slot + 1)
    width = halo.shape[1]
    turned = [turn(halo, -at - base, 1) for _, base in halves_of(cells, slots, width)]
    return turned[0] if len(turned) == 1 else jnp.concatenate(turned, axis=0)


def compact(rows, cells, count):
    return count == 2 and SUB == 2 * rows and cells >= 2 * SUB


def pigment_rows(rows, cells, count):
    return cells // 2 + SUB if compact(rows, cells, count) else cells


def level_shapes(tracers, rows, width, count):
    height = tracers * rows + 2 * (SUB - rows)
    height += -height % SUB
    return [shape(height, width)] * (1 if count == 2 else 2)


def write_levels(c, t, rows, levs, g):
    cells = c.shape[0]
    here = pl.ds(SUB - rows + t * rows, rows)
    if len(levs) == 1:
        levs[0][here, :] = jnp.where(g == 0, c[cells - rows :], c[:rows])
    else:
        levs[0][here, :] = c[cells - rows :]
        levs[1][here, :] = c[:rows]


def in_strip(rows, count, width, member):
    at_row = lax.rem(iota((SUB, width), 0), rows)
    strip = rows // count
    return (at_row >= member * strip) & (at_row < (member + 1) * strip)


def write_pigment(rows, count, p_ref, msg, g):
    cells, width = p_ref.shape
    if not compact(rows, cells, count):
        msg[pl.ds(0, cells), :] = p_ref[...]
        return
    levels, strip = cells // rows, rows // count
    for r in range(strip):
        msg[pl.ds(r, levels, stride=strip), :] = jnp.where(
            g == 0, p_ref[pl.ds(strip + r, levels, stride=rows), :], p_ref[pl.ds(r, levels, stride=rows), :]
        )
    blocks = [p_ref[pl.ds(at, SUB), :] for at in range(0, cells, SUB)]
    inner = blocks[1]
    for block in blocks[2:-1]:
        inner = inner + block
    inner = jnp.zeros_like(inner) if len(blocks) == 2 else inner
    near = jnp.where(g == 0, blocks[-1], blocks[0])
    rest = inner + jnp.where(g == 0, blocks[0], blocks[-1])
    rest = rest + turn(rest, rows, 0)
    msg[pl.ds(cells // 2, SUB), :] = jnp.where(in_strip(rows, count, width, g), near, turn(rest, strip, 0))


def read_pigment(rows, count, msg, other_s, g):
    cells, width = other_s.shape
    if not compact(rows, cells, count):
        return msg[pl.ds(0, cells), :]
    levels, strip = cells // rows, rows // count
    for s in range(count):
        for r in range(strip):
            other_s[pl.ds(s * strip + r, levels, stride=rows), :] = jnp.where(
                g == s, msg[pl.ds(r, levels, stride=strip), :], 0.0
            )
    edge = msg[pl.ds(cells // 2, SUB), :]
    theirs = in_strip(rows, count, width, 1 - g)
    first = other_s[pl.ds(0, SUB), :]
    rest = jnp.where(iota((SUB, width), 0) < rows, turn(edge, strip, 0), 0.0)
    other_s[pl.ds(0, SUB), :] = jnp.where(theirs, jnp.where(g == 0, edge, rest), first)
    last = other_s[pl.ds(cells - SUB, SUB), :]
    other_s[pl.ds(cells - SUB, SUB), :] = jnp.where(theirs & (g == 1), edge, last)
    return other_s[...]


def raw_window(rows, count, strip_cells, member):
    if count != 2:
        return 0, strip_cells
    height = strip_cells // 2 + 2 * (rows // count)
    return member * (strip_cells - height), height


def first_kernel(out_ref):
    out_ref[...] = jnp.zeros(out_ref.shape, F32)


def raw_kernel(rows, count, first_ref, *refs):
    refs = Refs(refs)
    fields, small_in = refs.take(5), refs.take(6)
    raw_ref, out_ref = refs.take(2)
    g = lax.axis_index("grp")
    for small, small_out in zip(small_in, refs.take(6)):
        small_out[...] = small[...]
    strip_cells = raw_ref.shape[1]
    low, height = raw_window(rows, count, strip_cells, 0)
    high, _ = raw_window(rows, count, strip_cells, 1)
    for at, field in enumerate(fields):
        raw_ref[at] = field[...]
        lower_part, upper_part = field[pl.ds(low, height), :], field[pl.ds(high, height), :]
        out_ref[pl.ds(at * height, height), :] = jnp.where(g == 0, upper_part, lower_part)


def tile(v, cells):
    width = v.shape[1]
    return jnp.broadcast_to(v[None], (cells // SUB, SUB, width)).reshape(cells, width)


def prep_kernel(rows, count, pig_ref, c_ref, p_ref, p_msg):
    g = lax.axis_index("grp")
    tracers, cells, width = c_ref.shape
    weights = pig_ref[...]
    pigment = jnp.zeros((cells, width), F32)
    for t in range(tracers):
        c = c_ref[t]
        pigment = pigment + tile(jnp.broadcast_to(weights[:, t : t + 1], (SUB, width)), cells) * c
    p_ref[...] = pigment
    write_pigment(rows, count, p_ref, p_msg, g)


def halves(v):
    high = v.astype(jnp.bfloat16)
    return high, (v - high.astype(F32)).astype(jnp.bfloat16)


def dot(a, b, **kw):
    return jnp.dot(a, b, preferred_element_type=F32, **kw)


def spread_rates(rates, tracers):
    exact = functools.partial(dot, precision=lax.Precision.HIGHEST)
    depth = tracers * SUB
    spread = jnp.where(iota((depth, tracers), 0) // SUB == iota((depth, tracers), 1), 1.0, 0.0)
    spread_t = jnp.where(iota((tracers, depth), 1) // SUB == iota((tracers, depth), 0), 1.0, 0.0)
    weights = exact(exact(spread, rates), spread_t)
    return jnp.where(
        lax.rem(iota((depth, depth), 0), SUB) == lax.rem(iota((depth, depth), 1), SUB), weights, 0.0
    )


def mix(weights, c_ref, mix_ref):
    tracers, cells, width = c_ref.shape
    w_high, w_low = halves(weights)
    for b in range(cells // SUB):
        here = pl.ds(b * SUB, SUB)
        c_high, c_low = halves(c_ref[:, here, :].reshape(tracers * SUB, width))
        mixed = dot(w_high, c_high) + (dot(w_high, c_low) + dot(w_low, c_high))
        mix_ref[:, here, :] = mixed.reshape(tracers, SUB, width)


def put_rows(msg_ya, msg_yb, slot, first, last):
    y_even = lax.rem(lax.axis_index("gy"), 2) == 0
    msg_ya[slot] = jnp.where(y_even, last, first)
    msg_yb[slot] = jnp.where(y_even, first, last)


def pack(rows, c_ref, p_ref, msg_xa, msg_xb, msg_ya, msg_yb, levs):
    tracers, cells, _ = c_ref.shape
    levels = cells // rows
    x_even = lax.rem(lax.axis_index("gx"), 2) == 0
    left = right = jnp.zeros(msg_xa.shape, F32)
    left, right = pack_sides(p_ref[...], tracers + 2, tracers + 3, left, right)
    g = lax.axis_index("grp")
    for t in range(tracers):
        left, right = pack_sides(c_ref[t], t, tracers + 3, left, right)
        write_levels(c_ref[t], t, rows, levs, g)
    msg_xa[...] = jnp.where(x_even, right, left)
    msg_xb[...] = jnp.where(x_even, left, right)
    first, last = pl.ds(0, levels, stride=rows), pl.ds(rows - 1, levels, stride=rows)
    for t in range(tracers):
        put_rows(msg_ya, msg_yb, t, c_ref[t, first, :], c_ref[t, last, :])
    if msg_ya.shape[0] > tracers:
        put_rows(msg_ya, msg_yb, tracers, p_ref[first, :], p_ref[last, :])


def pack_kernel(rows, *refs):
    refs = Refs(refs)
    depth_in, solar_in, c_ref, p_ref = refs.take(4)
    msg_xa, msg_xb, msg_ya, msg_yb, depth_ref, solar_ref = refs.take(6)
    levs = refs.refs
    tracers, cells, width = c_ref.shape
    for r in range(0, SUB, rows):
        depth_ref[pl.ds(r, rows), :] = depth_in[...]
        solar_ref[pl.ds(r, rows), :] = solar_in[...]
    pack(rows, c_ref, p_ref, msg_xa, msg_xb, msg_ya, msg_yb, levs)
    levels = cells // rows
    level = lax.axis_index("grp") * levels + iota((levels, width), 0)
    wet_first = jnp.where(level < depth_in[pl.ds(0, 1), :], 1.0, 0.0)
    wet_last = jnp.where(level < depth_in[pl.ds(rows - 1, 1), :], 1.0, 0.0)
    put_rows(msg_ya, msg_yb, tracers + 1, wet_first, wet_last)


def ocean_kernel(rows, count, tracers, first_step, *refs):
    refs = Refs(refs)
    depth_ref, solar_ref = refs.take(2)
    in_xa, in_xb = refs.take(2)
    p_own, *p_others = refs.take(count)
    if first_step:
        own_fields, *other_fields = refs.take(count)
    else:
        fields = refs.take(5)
    band_ref, msg_xa, msg_xb, speed_ref = refs.take(4)
    full_out = refs.take(5 if first_step else 4)
    p_full, p_other_s = refs.take(2)
    if first_step:
        fields = refs.take(5)
        other_s = refs.take(5 * (count - 1))
    face_s, par_s, wet_s = refs.take(3)
    g = lax.axis_index("grp")
    cells, width = p_own.shape
    levels = cells // rows
    total = count * cells
    all_levels = total // rows
    strip = rows // count

    pigments = [read_pigment(rows, count, o, p_other_s, g) for o in p_others]
    for b in range(count):
        k = lax.rem(g - b + count, count)
        p_full[pl.ds(b * cells, cells), :] = pick(p_own[...], pigments, k)
    if first_step:
        strip_cells = all_levels * strip
        for at in range(5):
            for k in range(count - 1):
                other = other_s[5 * k + at]
                low, height = raw_window(rows, count, strip_cells, 0)
                value = other_fields[k][pl.ds(at * height, height), :]
                if count != 2:
                    other[...] = value
                    continue
                high, _ = raw_window(rows, count, strip_cells, 1)
                other[...] = jnp.zeros((strip_cells, width), F32)
                other[pl.ds(low, height), :] = jnp.where(g == 0, value, 0.0)
                kept = jnp.where(iota(value.shape, 0) < low + height - high, other[pl.ds(high, height), :], 0.0)
                other[pl.ds(high, height), :] = jnp.where(g == 1, value, kept)
            for s in range(count):
                k = lax.rem(g - s + count, count)
                for r in range(strip):
                    here = pl.ds(r, all_levels, stride=strip)
                    fields[at][pl.ds(s * strip + r, all_levels, stride=rows), :] = pick(
                        own_fields[at, here, :], [other_s[5 * j + at][here, :] for j in range(count - 1)], k
                    )

    row = iota((total, width), 0)
    wet = jnp.where(row // rows < tile(depth_ref[...], total), 1.0, 0.0)
    att = WATER_ATTEN + PIGMENT_ATTEN * p_full[...]
    summed = att
    step = rows
    while step < total:
        summed = summed + jnp.where(row >= step, turn(summed, step, 0), 0.0)
        step *= 2
    top = tile(solar_ref[...], total) * jnp.exp(att - summed)
    par = top * jnp.exp(-0.5 * att)
    east, north, temp, sal, mixing = [f[...] for f in fields]
    temp = temp + WARMING_UPTAKE * (top * (1.0 - jnp.exp(-att))) * wet

    def below(v):
        return turn(v, -rows, 0)

    density = SALT_EXPANSION * sal - WARM_EXPANSION * temp
    face = 0.5 * (mixing + below(mixing)) + CONVECT_MIX / (1.0 + jnp.exp(below(density) - density))
    face = jnp.where(row < total - rows, face * below(wet), 0.0)

    def stir(v):
        flux = face * (below(v) - v)
        return v + flux - turn(flux, rows, 0)

    for at, v in enumerate((east, north, temp, sal)):
        full_out[at][...] = stir(v)
    if first_step:
        full_out[4][...] = mixing
    face_s[...] = face
    par_s[...] = par
    wet_s[...] = wet

    band = pl.ds(pl.multiple_of(g * cells, SUB), cells)
    above = pl.ds(pl.multiple_of(lax.max(g * cells - SUB, 0), SUB), SUB)
    face_band = face_s[band, :]
    lifted = turn(jnp.concatenate([face_s[above, :], face_band], axis=0), rows, 0)[SUB:]
    lifted = jnp.where((iota((cells, width), 0) < rows) & (g == 0), 0.0, lifted)
    u = full_out[0][band, :]
    wet_band = wet_s[band, :]
    band_ref[0] = u
    band_ref[1] = full_out[1][band, :]
    band_ref[2] = full_out[2][band, :]
    band_ref[3] = face_band
    band_ref[4] = lifted
    band_ref[5] = par_s[band, :]
    band_ref[6] = wet_band

    x_even = lax.rem(lax.axis_index("gx"), 2) == 0
    xa, xb = in_xa[...], in_xb[...]
    left, right = jnp.where(x_even, xb, xa), jnp.where(x_even, xa, xb)
    left, right = pack_sides(wet_band, tracers + 1, tracers + 3, left, right)
    _, right = pack_sides(u, tracers, tracers + 3, left, right)
    msg_xa[...] = jnp.where(x_even, right, left)
    msg_xb[...] = jnp.where(x_even, left, right)
    speed_ref[pl.ds(0, levels), :] = band_ref[1, pl.ds(rows - 1, levels, stride=rows), :]
    speed_ref[pl.ds(levels, levels), :] = jnp.zeros((levels, width), F32)
    speed_ref[pl.ds(2 * levels, levels), :] = jnp.zeros((levels, width), F32)


def start_own_strip(rows, count, g, full, outs, strips, sems):
    strip = rows // count
    all_levels = full[0].shape[0] // rows
    copies = [pltpu.make_async_copy(strips[at], outs[at], sems.at[at]) for at in range(4)]
    for at in range(4):
        for r in range(strip):
            value = full[at][pl.ds(r, all_levels, stride=rows), :]
            for s in range(1, count):
                value = jnp.where(g == s, full[at][pl.ds(s * strip + r, all_levels, stride=rows), :], value)
            strips[at][pl.ds(r, all_levels, stride=strip), :] = value
        copies[at].start()
    return copies


def lower(opening, speed):
    return opening * (jnp.maximum(speed, 0.0) + SIDE_DIFFUSE)


def upper(opening, speed):
    return opening * (jnp.minimum(speed, 0.0) - SIDE_DIFFUSE)


def inner_kernel(rows, count, first_step, last_step, *refs):
    refs = Refs(refs)
    if first_step:
        params, (rates_ref,) = refs.take(3), refs.take(1)
    else:
        tiles_ref, w_ref = refs.take(2)
    c_ref, band_ref = refs.take(2)
    lev_in = refs.take(1 if count == 2 else 2)
    if last_step:
        full = refs.take(4)
    (part_ref,) = refs.take(1)
    if last_step:
        outs = refs.take(4)
    else:
        (p_part,) = refs.take(1)
    if first_step:
        tiles_ref, w_ref = refs.take(2)
    if last_step:
        strips, (sems,) = refs.take(4), refs.take(1)
        copies = start_own_strip(rows, count, lax.axis_index("grp"), full, outs, strips, sems)
    (mix_ref,) = refs.take(1)
    tracers, cells, width = c_ref.shape
    if first_step:
        w_ref[...] = spread_rates(rates_ref[...], tracers)
        for at, param in enumerate(params):
            values = param[...]
            for t in range(tracers):
                tiles_ref[at, t] = jnp.broadcast_to(values[:, t : t + 1], (SUB, width))
    mix(w_ref[...], c_ref, mix_ref)
    lane = iota((cells, width), 1)
    at_row = lax.rem(iota((cells, width), 0), rows)
    u = band_ref[0]
    v = band_ref[1]
    wet = band_ref[6]

    def west(x):
        return turn(x, 1, 1)

    def east(x):
        return turn(x, -1, 1)

    def south(x):
        return turn(x, 1, 0)

    def north(x):
        return turn(x, -1, 0)

    open_w = jnp.where(lane == 0, 0.0, wet * west(wet))
    open_e = jnp.where(lane == width - 1, 0.0, wet * east(wet))
    open_s = jnp.where(at_row == 0, 0.0, wet * south(wet))
    open_n = jnp.where(at_row == rows - 1, 0.0, wet * north(wet))
    k_w = lower(open_w, west(u))
    k_e = -upper(open_e, u)
    k_s = lower(open_s, south(v))
    k_n = -upper(open_n, v)
    k_d = band_ref[3]
    k_u = band_ref[4]
    k_c = (upper(open_w, west(u)) - lower(open_e, u)) + (upper(open_s, south(v)) - lower(open_n, v))
    k_c = 1.0 + (k_c - k_d - k_u)
    par = band_ref[5]
    lit = TIME_STEP * wet
    warm = lit * jnp.exp(WARMING_FACTOR * (band_ref[2] - 20.0))
    lit = lit * par
    pigment = jnp.zeros((cells, width), F32)
    for t in range(tracers):
        c = c_ref[t]
        at = SUB - rows + t * rows
        up8 = lev_in[0][pl.ds(at + rows - SUB, SUB), :]
        down8 = lev_in[-1][pl.ds(at, SUB), :]
        c_u = turn(jnp.concatenate([up8, c], axis=0), rows, 0)[SUB:]
        c_d = turn(jnp.concatenate([c, down8], axis=0), -rows, 0)[:cells]
        part = (
            (k_c + tile(tiles_ref[0, t], cells) * (lit / (par + tile(tiles_ref[1, t], cells)))) * c
            + (k_u * c_u + k_d * c_d)
            + (k_w * west(c) + k_e * east(c))
            + (k_s * south(c) + k_n * north(c))
            + warm * mix_ref[t]
        )
        part_ref[t] = part
        if not last_step:
            pigment = pigment + tile(tiles_ref[2, t], cells) * part
    if last_step:
        for copy in copies:
            copy.wait()
    else:
        p_part[...] = pigment


def x_halo(got_xa, got_xb):
    x_even = lax.rem(lax.axis_index("gx"), 2) == 0
    xa, xb = got_xa[...], got_xb[...]
    return jnp.where((lax.rem(iota(xa.shape, 1), 2) == 0) == x_even, xb, xa)


def spread_rows(rows, got_ya, got_yb, out_ref, slot):
    y_even = lax.rem(lax.axis_index("gy"), 2) == 0
    levels = got_ya.shape[1]
    ya, yb = got_ya[slot], got_yb[slot]
    out_ref[slot, pl.ds(0, levels, stride=rows), :] = jnp.where(y_even, yb, ya)
    out_ref[slot, pl.ds(rows - 1, levels, stride=rows), :] = jnp.where(y_even, ya, yb)


def side_factors(rows, sizes, halo_ref, wet_out, speed, speed_s, band_ref, tracers):
    _, size_x, size_y = sizes
    x = lax.axis_index("gx")
    y = lax.axis_index("gy")
    u = band_ref[0]
    v = band_ref[1]
    wet = band_ref[6]
    cells, width = wet.shape
    speed_s[pl.ds(0, cells // rows, stride=rows), :] = speed[pl.ds(0, cells // rows), :]
    lane = iota((cells, width), 1)
    at_row = lax.rem(iota((cells, width), 0), rows)
    at_w, at_e, at_s, at_n = lane == 0, lane == width - 1, at_row == 0, at_row == rows - 1
    wet_x = wet * sides_of(halo_ref[...], tracers + 1, tracers + 3, cells)
    wet_y = wet * wet_out
    open_w = jnp.where(at_w & (x > 0), wet_x, 0.0)
    open_e = jnp.where(at_e & (x < size_x - 1), wet_x, 0.0)
    open_s = jnp.where(at_s & (y > 0), wet_y, 0.0)
    open_n = jnp.where(at_n & (y < size_y - 1), wet_y, 0.0)
    u_w = sides_of(halo_ref[...], tracers, tracers + 3, cells)
    v_s = jnp.where(at_s, speed_s[...], 0.0)
    k_x = lower(open_w, u_w) - upper(open_e, u)
    k_y = lower(open_s, v_s) - upper(open_n, v)
    k_c = (upper(open_w, u_w) - lower(open_e, u)) + (upper(open_s, v_s) - lower(open_n, v))
    return k_x, k_y, k_c


def sideways(rows, factors, sides, outer, c):
    k_x, k_y, k_c = factors
    at_row = lax.rem(iota(c.shape, 0), rows)
    edge = (at_row == 0) | (at_row == rows - 1)
    return (k_x * sides + k_c * c) + jnp.where(edge, k_y * outer, 0.0)


def early_kernel(rows, count, sizes, first_step, *refs):
    refs = Refs(refs)
    c_ref, band_ref, got_xa, got_xb, got_ya, got_yb = refs.take(6)
    (speed,) = refs.take(1)
    p_in, part_ref, p_part = refs.take(3)
    if not first_step:
        (wet_in,) = refs.take(1)
    k_ref, halo_ref, spread_s, wet_out, p_ref, p_msg, speed_s = refs.take(7)
    g = lax.axis_index("grp")
    tracers, cells, width = c_ref.shape
    halo_ref[...] = x_halo(got_xa, got_xb)
    for slot in range(got_ya.shape[0]):
        spread_rows(rows, got_ya, got_yb, spread_s, slot)
    wet_out[...] = spread_s[tracers + 1] if first_step else wet_in[...]
    factors = side_factors(rows, sizes, halo_ref, wet_out[...], speed, speed_s, band_ref, tracers)
    for at, k in enumerate(factors):
        k_ref[at] = k
    side = sides_of(halo_ref[...], tracers + 2, tracers + 3, cells)
    change = sideways(rows, factors, side, spread_s[tracers], p_in[...])
    p_ref[...] = p_part[...] + change
    write_pigment(rows, count, p_ref, p_msg, g)


def step_kernel(rows, *refs):
    refs = Refs(refs)
    c_ref, part_ref, k_ref, halo_ref, spread_s, p_ref = refs.take(6)
    out_ref, msg_xa, msg_xb, msg_ya, msg_yb = refs.take(5)
    tracers = c_ref.shape[0]
    factors = [k_ref[i] for i in range(3)]
    for t in range(tracers):
        out_ref[t] = part_ref[t] + sideways(
                rows, factors, sides_of(halo_ref[...], t, tracers + 3, c_ref.shape[1]), spread_s[t], c_ref[t]
            )
    pack(rows, out_ref, p_ref, msg_xa, msg_xb, msg_ya, msg_yb, refs.refs)


def final_kernel(rows, sizes, first_step, *refs):
    refs = Refs(refs)
    c_ref, part_ref, band_ref, got_xa, got_xb, got_ya, got_yb = refs.take(7)
    (speed,) = refs.take(1)
    if not first_step:
        (wet_in,) = refs.take(1)
    out_hbm, spread_s, speed_s, halo_ref, new_s, sems = refs.take(6)
    tracers = c_ref.shape[0]
    halo_ref[...] = x_halo(got_xa, got_xb)
    if first_step:
        spread_rows(rows, got_ya, got_yb, spread_s, tracers + 1)
    wet_out = spread_s[tracers + 1] if first_step else wet_in[...]
    factors = side_factors(rows, sizes, halo_ref, wet_out, speed, speed_s, band_ref, tracers)
    copies = []
    for i, (a, n) in enumerate(chunks(tracers, sems.shape[0])):
        for t in range(a, a + n):
            spread_rows(rows, got_ya, got_yb, spread_s, t)
            new_s[t] = part_ref[t] + sideways(
                rows, factors, sides_of(halo_ref[...], t, tracers + 3, c_ref.shape[1]), spread_s[t], c_ref[t]
            )
        copies.append(pltpu.make_async_copy(new_s.at[pl.ds(a, n)], out_hbm.at[pl.ds(a, n)], sems.at[i]))
        copies[-1].start()
    for copy in copies:
        copy.wait()


def call(kernel, ins, outs, in_specs=None, out_specs=None, scratch=(), flops=1 << 20, moved=1 << 20):
    return pl.pallas_call(
        kernel,
        in_specs=[vmem() for _ in ins] if in_specs is None else in_specs,
        out_specs=[vmem() for _ in outs] if out_specs is None else out_specs,
        out_shape=outs,
        scratch_shapes=list(scratch),
        compiler_params=pltpu.CompilerParams(vmem_limit_bytes=VMEM_LIMIT),
        cost_estimate=pl.CostEstimate(flops=flops, bytes_accessed=moved, transcendentals=0),
    )(*ins)


def per_device(
    sizes,
    zonal_boundary_speed,
    meridional_boundary_speed,
    potential_warmth,
    saltiness_field,
    quiescent_mixing_profile,
    substance_amounts,
    submerged_layer_number,
    solar_radiation,
    interaction_rates,
    photosynthetic_rates,
    saturation_irradiance,
    pigment_per_tracer,
):
    count = sizes[0]
    result_dimensions = zonal_boundary_speed.shape
    all_levels, _, strip, width = result_dimensions
    tracers, levels, rows, _ = substance_amounts.shape
    cells = levels * rows
    total = all_levels * rows
    strip_cells = all_levels * strip
    dma = pltpu.SemaphoreType.DMA
    column = pltpu.VMEM((total, width), F32)
    band_s = pltpu.VMEM((cells, width), F32)

    own = [
        f.reshape(strip_cells, width)
        for f in (
            zonal_boundary_speed,
            meridional_boundary_speed,
            potential_warmth,
            saltiness_field,
            quiescent_mixing_profile,
        )
    ]
    _, height = raw_window(rows, count, strip_cells, 0)
    params = [
        p.reshape(1, tracers) for p in (photosynthetic_rates, saturation_irradiance, pigment_per_tracer)
    ]
    (first,) = call(first_kernel, [], [shape(SUB, width)], flops=1 << 30)
    small = [*params, interaction_rates, submerged_layer_number, solar_radiation]
    raw, window, *small = call(
        functools.partial(raw_kernel, rows, count),
        [first, *own, *small],
        [
            shape(5, strip_cells, width),
            shape(5 * height, width),
            *[jax.ShapeDtypeStruct(v.shape, v.dtype) for v in small],
        ],
    )
    *params, rates, layers, light = small
    raw_others = from_others(window, count)

    sent_pigment = shape(pigment_rows(rows, cells, count), width)
    sent_levels = level_shapes(tracers, rows, width, count)
    cols = shape(cells, width)
    sent_cols = shape(cells // 2, width) if folds(tracers + 3, cells, width) else cols
    field = shape(tracers, cells, width)
    c = substance_amounts.reshape(tracers, cells, width)
    pigment, p_msg = call(
        functools.partial(prep_kernel, rows, count),
        [params[2], c],
        [cols, sent_pigment],
    )
    full = None
    for step in range(STEPS):
        first_step, last_step = step == 0, step == STEPS - 1
        p_others = from_others(p_msg, count)
        if first_step:
            lines = shape(tracers + 2, levels, width)
            xa, xb, ya, yb, depth, solar, *levs = call(
                functools.partial(pack_kernel, rows),
                [layers, light, c, pigment],
                [
                    sent_cols,
                    sent_cols,
                    lines,
                    lines,
                    jax.ShapeDtypeStruct((SUB, width), jnp.int32),
                    shape(SUB, width),
                    *sent_levels,
                ],
                flops=1 << 24,
            )
        ya = lax.ppermute(ya, AXES, pairing(sizes, "gy", 0))
        yb = lax.ppermute(yb, AXES, pairing(sizes, "gy", 1))
        if count == 2:
            lev = from_others(levs[0], count)
        else:
            lev = [
                lax.ppermute(levs[0], "grp", [(i, (i + 1) % count) for i in range(count)]),
                lax.ppermute(levs[1], "grp", [((i + 1) % count, i) for i in range(count)]),
            ]
        band, xa, xb, speed, *full = call(
            functools.partial(ocean_kernel, rows, count, tracers, first_step),
            [depth, solar, xa, xb, pigment, *p_others, *([raw, *raw_others] if first_step else full)],
            [
                shape(7, cells, width),
                sent_cols,
                sent_cols,
                shape(3 * levels, width),
                *[shape(total, width)] * (5 if first_step else 4),
            ],
            scratch=[column, band_s]
            + [column] * (5 if first_step else 0)
            + [pltpu.VMEM((strip_cells, width), F32)] * (5 * (count - 1) if first_step else 0)
            + [column] * 3,
            flops=1<<32,
        )
        xa = lax.ppermute(xa, AXES, pairing(sizes, "gx", 0))
        xb = lax.ppermute(xb, AXES, pairing(sizes, "gx", 1))
        speed = lax.ppermute(speed, AXES, upward(sizes))
        tables = [shape(3, tracers, SUB, width), shape(tracers * SUB, tracers * SUB)]
        part, *rest = call(
            functools.partial(inner_kernel, rows, count, first_step, last_step),
            [*([*params, rates] if first_step else known_rates), c, band, *lev, *(full if last_step else [])],
            [field]
            + ([shape(strip_cells, width)] * 4 if last_step else [cols])
            + (tables if first_step else []),
            out_specs=[vmem()]
            + ([hbm()] * 4 if last_step else [vmem()])
            + ([vmem()] * 2 if first_step else []),
            scratch=([pltpu.VMEM((strip_cells, width), F32)] * 4 + [dma((4,))] if last_step else [])
            + [pltpu.VMEM((tracers, cells, width), F32)],
            flops=1 << 10,
        )
        if first_step:
            *rest, tiles, weights = rest
            known_rates = [tiles, weights]
        known = [] if first_step else [wet_out]
        if not last_step:
            k, halo, spread, wet_out, pigment_next, p_msg = call(
                functools.partial(early_kernel, rows, count, sizes, first_step),
                [c, band, xa, xb, ya, yb, speed, pigment, part, *rest, *known],
                [shape(3, cells, width), sent_cols, shape(tracers + 2, cells, width), cols, cols, sent_pigment],
                scratch=[band_s],
            )
            pigment = pigment_next
            lines = shape(tracers + (0 if step + 1 == STEPS - 1 else 1), levels, width)
            c, xa, xb, ya, yb, *levs = call(
                functools.partial(step_kernel, rows),
                [c, part, k, halo, spread, pigment],
                [field, sent_cols, sent_cols, lines, lines, *sent_levels],
                flops=1<<32,
            )
        else:
            ocean = rest
            (c,) = call(
                functools.partial(final_kernel, rows, sizes, first_step),
                [c, part, band, xa, xb, ya, yb, speed, *known],
                [field],
                out_specs=[hbm()],
                scratch=[
                    pltpu.VMEM((tracers + 2, cells, width), F32),
                    band_s,
                    pltpu.VMEM(sent_cols.shape, F32),
                    pltpu.VMEM((tracers, cells, width), F32),
                    dma((5,)),
                ],
            )
    return tuple(f.reshape(result_dimensions) for f in ocean) + (c.reshape(substance_amounts.shape),)


def solution(mesh):
    ocean = P(None, "gy", "grp", "gx")
    tracer = P(None, "grp", "gy", "gx")
    surface = P("gy", "gx")
    sizes = tuple(mesh.shape[a] for a in AXES)
    return jax.shard_map(
        functools.partial(per_device, sizes),
        mesh=mesh,
        in_specs=(ocean,) * 5 + (tracer, surface, surface) + (P(),) * 4,
        out_specs=(ocean,) * 4 + (tracer,),
        check_vma=False,
    )
```

```python
import functools

import jax
import jax.numpy as jnp
from jax import lax
from jax.experimental import pallas as pl
from jax.experimental.pallas import tpu as pltpu
from jax.sharding import PartitionSpec as P

STEPS = 2

WATER_ATTEN = 0.01
PIGMENT_ATTEN = 0.05
WARMING_UPTAKE = 5.0
WARM_EXPANSION = 0.2
SALT_EXPANSION = 0.8
CONVECT_MIX = 0.15
SIDE_DIFFUSE = 0.05
WARMING_FACTOR = 0.0633
TIME_STEP = 0.5

SUB = 8
AXES = ("grp", "gx", "gy")
VMEM_LIMIT = 48 * 1024 * 1024

F32 = jnp.float32


def vmem():
    return pl.BlockSpec(memory_space=pltpu.VMEM)


def hbm():
    return pl.BlockSpec(memory_space=pltpu.HBM)


def shape(*dims):
    return jax.ShapeDtypeStruct(dims, F32)


def turn(x, shift, axis):
    shift = shift % x.shape[axis]
    return x if shift == 0 else pltpu.roll(x, shift, axis)


def iota(x, axis):
    return lax.broadcasted_iota(jnp.int32, x, axis)


def pairing(sizes, axis, odd):
    size_g, size_x, size_y = sizes

    def partner(g, x, y):
        i, n = (x, size_x) if axis == "gx" else (y, size_y)
        j = i + 1 if i % 2 == odd else i - 1
        if 0 <= j < n:
            return (g, j, y) if axis == "gx" else (g, x, j)
        if axis == "gx":
            return (g, x, y ^ 1) if (y ^ 1) < size_y else (g, x, y)
        return (g, x ^ 1, y) if (x ^ 1) < size_x else (g, x, y)

    def index(g, x, y):
        return (g * size_x + x) * size_y + y

    return [
        (index(g, x, y), index(*partner(g, x, y)))
        for g in range(size_g)
        for x in range(size_x)
        for y in range(size_y)
    ]


def upward(sizes):
    size_g, size_x, size_y = sizes
    return [
        ((g * size_x + x) * size_y + y, (g * size_x + x) * size_y + (y + 1) % size_y)
        for g in range(size_g)
        for x in range(size_x)
        for y in range(size_y)
    ]


def from_others(value, count):
    return [
        lax.ppermute(value, "grp", [(i, (i + k) % count) for i in range(count)])
        for k in range(1, count)
    ]


def chunks(n, parts):
    step = -(-n // parts)
    return [(a, min(step, n - a)) for a in range(0, n, step)]


class Refs:
    def __init__(self, refs):
        self.refs = list(refs)

    def take(self, n):
        out, self.refs = self.refs[:n], self.refs[n:]
        return out


def pick(mine, others, k):
    value = mine
    for at, other in enumerate(others):
        value = jnp.where(k == at + 1, other, value)
    return value


def folds(slots, cells, width):
    return 4 * slots < width and cells % (2 * SUB) == 0


def halves_of(cells, slots, width):
    if not folds(slots, cells, width):
        return [(slice(0, cells), 0)]
    return [(slice(0, cells // 2), 0), (slice(cells // 2, cells), width // 2)]


def pack_sides(c, slot, slots, left, right):
    cells, width = c.shape
    at = 2 * (slot + 1)
    lane = iota(left.shape, 1)
    for rows, base in halves_of(cells, slots, width):
        left = jnp.where(lane == base + at - 1, turn(c[rows], base + at - 1, 1), left)
        right = jnp.where(lane == base + at, turn(c[rows], base + at + 1, 1), right)
    return left, right


def sides_of(halo, slot, slots, cells):
    at = 2 * (slot + 1)
    width = halo.shape[1]
    turned = [turn(halo, -at - base, 1) for _, base in halves_of(cells, slots, width)]
    return turned[0] if len(turned) == 1 else jnp.concatenate(turned, axis=0)


def compact(rows, cells, count):
    return count == 2 and SUB == 2 * rows and cells >= 2 * SUB


def pigment_rows(rows, cells, count):
    return cells // 2 + SUB if compact(rows, cells, count) else cells


def level_shapes(tracers, rows, width, count):
    height = tracers * rows + 2 * (SUB - rows)
    height += -height % SUB
    return [shape(height, width)] * (1 if count == 2 else 2)


def write_levels(c, t, rows, levs, g):
    cells = c.shape[0]
    here = pl.ds(SUB - rows + t * rows, rows)
    if len(levs) == 1:
        levs[0][here, :] = jnp.where(g == 0, c[cells - rows :], c[:rows])
    else:
        levs[0][here, :] = c[cells - rows :]
        levs[1][here, :] = c[:rows]


def in_strip(rows, count, width, member):
    at_row = lax.rem(iota((SUB, width), 0), rows)
    strip = rows // count
    return (at_row >= member * strip) & (at_row < (member + 1) * strip)


def write_pigment(rows, count, p_ref, msg, g):
    cells, width = p_ref.shape
    if not compact(rows, cells, count):
        msg[pl.ds(0, cells), :] = p_ref[...]
        return
    levels, strip = cells // rows, rows // count
    for r in range(strip):
        msg[pl.ds(r, levels, stride=strip), :] = jnp.where(
            g == 0, p_ref[pl.ds(strip + r, levels, stride=rows), :], p_ref[pl.ds(r, levels, stride=rows), :]
        )
    blocks = [p_ref[pl.ds(at, SUB), :] for at in range(0, cells, SUB)]
    inner = blocks[1]
    for block in blocks[2:-1]:
        inner = inner + block
    inner = jnp.zeros_like(inner) if len(blocks) == 2 else inner
    near = jnp.where(g == 0, blocks[-1], blocks[0])
    rest = inner + jnp.where(g == 0, blocks[0], blocks[-1])
    rest = rest + turn(rest, rows, 0)
    msg[pl.ds(cells // 2, SUB), :] = jnp.where(in_strip(rows, count, width, g), near, turn(rest, strip, 0))


def read_pigment(rows, count, msg, other_s, g):
    cells, width = other_s.shape
    if not compact(rows, cells, count):
        return msg[pl.ds(0, cells), :]
    levels, strip = cells // rows, rows // count
    for s in range(count):
        for r in range(strip):
            other_s[pl.ds(s * strip + r, levels, stride=rows), :] = jnp.where(
                g == s, msg[pl.ds(r, levels, stride=strip), :], 0.0
            )
    edge = msg[pl.ds(cells // 2, SUB), :]
    theirs = in_strip(rows, count, width, 1 - g)
    first = other_s[pl.ds(0, SUB), :]
    rest = jnp.where(iota((SUB, width), 0) < rows, turn(edge, strip, 0), 0.0)
    other_s[pl.ds(0, SUB), :] = jnp.where(theirs, jnp.where(g == 0, edge, rest), first)
    last = other_s[pl.ds(cells - SUB, SUB), :]
    other_s[pl.ds(cells - SUB, SUB), :] = jnp.where(theirs & (g == 1), edge, last)
    return other_s[...]


def raw_window(rows, count, strip_cells, member):
    if count != 2:
        return 0, strip_cells
    height = strip_cells // 2 + 2 * (rows // count)
    return member * (strip_cells - height), height


def first_kernel(out_ref):
    out_ref[...] = jnp.zeros(out_ref.shape, F32)


def raw_kernel(rows, count, first_ref, *refs):
    refs = Refs(refs)
    fields, small_in = refs.take(5), refs.take(6)
    raw_ref, out_ref = refs.take(2)
    g = lax.axis_index("grp")
    for small, small_out in zip(small_in, refs.take(6)):
        small_out[...] = small[...]
    strip_cells = raw_ref.shape[1]
    low, height = raw_window(rows, count, strip_cells, 0)
    high, _ = raw_window(rows, count, strip_cells, 1)
    for at, field in enumerate(fields):
        raw_ref[at] = field[...]
        lower_part, upper_part = field[pl.ds(low, height), :], field[pl.ds(high, height), :]
        out_ref[pl.ds(at * height, height), :] = jnp.where(g == 0, upper_part, lower_part)


def tile(v, cells):
    width = v.shape[1]
    return jnp.broadcast_to(v[None], (cells // SUB, SUB, width)).reshape(cells, width)


def prep_kernel(rows, count, pig_ref, c_ref, p_ref, p_msg):
    g = lax.axis_index("grp")
    tracers, cells, width = c_ref.shape
    weights = pig_ref[...]
    pigment = jnp.zeros((cells, width), F32)
    for t in range(tracers):
        c = c_ref[t]
        pigment = pigment + tile(jnp.broadcast_to(weights[:, t : t + 1], (SUB, width)), cells) * c
    p_ref[...] = pigment
    write_pigment(rows, count, p_ref, p_msg, g)


def halves(v):
    high = v.astype(jnp.bfloat16)
    return high, (v - high.astype(F32)).astype(jnp.bfloat16)


def dot(a, b, **kw):
    return jnp.dot(a, b, preferred_element_type=F32, **kw)


def spread_rates(rates, tracers):
    exact = functools.partial(dot, precision=lax.Precision.HIGHEST)
    depth = tracers * SUB
    spread = jnp.where(iota((depth, tracers), 0) // SUB == iota((depth, tracers), 1), 1.0, 0.0)
    spread_t = jnp.where(iota((tracers, depth), 1) // SUB == iota((tracers, depth), 0), 1.0, 0.0)
    weights = exact(exact(spread, rates), spread_t)
    return jnp.where(
        lax.rem(iota((depth, depth), 0), SUB) == lax.rem(iota((depth, depth), 1), SUB), weights, 0.0
    )


def mix(weights, c_ref, mix_ref):
    tracers, cells, width = c_ref.shape
    w_high, w_low = halves(weights)
    for b in range(cells // SUB):
        here = pl.ds(b * SUB, SUB)
        c_high, c_low = halves(c_ref[:, here, :].reshape(tracers * SUB, width))
        mixed = dot(w_high, c_high) + (dot(w_high, c_low) + dot(w_low, c_high))
        mix_ref[:, here, :] = mixed.reshape(tracers, SUB, width)


def put_rows(msg_ya, msg_yb, slot, first, last):
    y_even = lax.rem(lax.axis_index("gy"), 2) == 0
    msg_ya[slot] = jnp.where(y_even, last, first)
    msg_yb[slot] = jnp.where(y_even, first, last)


def pack(rows, c_ref, p_ref, msg_xa, msg_xb, msg_ya, msg_yb, levs):
    tracers, cells, _ = c_ref.shape
    levels = cells // rows
    x_even = lax.rem(lax.axis_index("gx"), 2) == 0
    left = right = jnp.zeros(msg_xa.shape, F32)
    left, right = pack_sides(p_ref[...], tracers + 2, tracers + 3, left, right)
    g = lax.axis_index("grp")
    for t in range(tracers):
        left, right = pack_sides(c_ref[t], t, tracers + 3, left, right)
        write_levels(c_ref[t], t, rows, levs, g)
    msg_xa[...] = jnp.where(x_even, right, left)
    msg_xb[...] = jnp.where(x_even, left, right)
    first, last = pl.ds(0, levels, stride=rows), pl.ds(rows - 1, levels, stride=rows)
    for t in range(tracers):
        put_rows(msg_ya, msg_yb, t, c_ref[t, first, :], c_ref[t, last, :])
    if msg_ya.shape[0] > tracers:
        put_rows(msg_ya, msg_yb, tracers, p_ref[first, :], p_ref[last, :])


def pack_kernel(rows, *refs):
    refs = Refs(refs)
    depth_in, solar_in, c_ref, p_ref = refs.take(4)
    msg_xa, msg_xb, msg_ya, msg_yb, depth_ref, solar_ref = refs.take(6)
    levs = refs.refs
    tracers, cells, width = c_ref.shape
    for r in range(0, SUB, rows):
        depth_ref[pl.ds(r, rows), :] = depth_in[...]
        solar_ref[pl.ds(r, rows), :] = solar_in[...]
    pack(rows, c_ref, p_ref, msg_xa, msg_xb, msg_ya, msg_yb, levs)
    levels = cells // rows
    level = lax.axis_index("grp") * levels + iota((levels, width), 0)
    wet_first = jnp.where(level < depth_in[pl.ds(0, 1), :], 1.0, 0.0)
    wet_last = jnp.where(level < depth_in[pl.ds(rows - 1, 1), :], 1.0, 0.0)
    put_rows(msg_ya, msg_yb, tracers + 1, wet_first, wet_last)


def ocean_kernel(rows, count, tracers, first_step, *refs):
    refs = Refs(refs)
    depth_ref, solar_ref = refs.take(2)
    in_xa, in_xb = refs.take(2)
    p_own, *p_others = refs.take(count)
    if first_step:
        own_fields, *other_fields = refs.take(count)
    else:
        fields = refs.take(5)
    band_ref, msg_xa, msg_xb, speed_ref = refs.take(4)
    full_out = refs.take(5 if first_step else 4)
    (p_other_s,) = refs.take(1)
    if first_step:
        fields = refs.take(5)
        other_s = refs.take(5 * (count - 1))
    g = lax.axis_index("grp")
    cells, width = p_own.shape
    levels = cells // rows
    total = count * cells
    all_levels = total // rows
    strip = rows // count

    pigments = [read_pigment(rows, count, o, p_other_s, g) for o in p_others]
    bands = [pick(p_own[...], pigments, lax.rem(g - b + count, count)) for b in range(count)]
    pigment = jnp.concatenate(bands, axis=0)
    if first_step:
        strip_cells = all_levels * strip
        for at in range(5):
            for k in range(count - 1):
                other = other_s[5 * k + at]
                low, height = raw_window(rows, count, strip_cells, 0)
                value = other_fields[k][pl.ds(at * height, height), :]
                if count != 2:
                    other[...] = value
                    continue
                high, _ = raw_window(rows, count, strip_cells, 1)
                other[...] = jnp.zeros((strip_cells, width), F32)
                other[pl.ds(low, height), :] = jnp.where(g == 0, value, 0.0)
                kept = jnp.where(iota(value.shape, 0) < low + height - high, other[pl.ds(high, height), :], 0.0)
                other[pl.ds(high, height), :] = jnp.where(g == 1, value, kept)
            for s in range(count):
                k = lax.rem(g - s + count, count)
                for r in range(strip):
                    here = pl.ds(r, all_levels, stride=strip)
                    fields[at][pl.ds(s * strip + r, all_levels, stride=rows), :] = pick(
                        own_fields[at, here, :], [other_s[5 * j + at][here, :] for j in range(count - 1)], k
                    )

    row = iota((total, width), 0)
    wet = jnp.where(row // rows < tile(depth_ref[...], total), 1.0, 0.0)
    att = WATER_ATTEN + PIGMENT_ATTEN * pigment
    summed = att
    step = rows
    while step < total:
        summed = summed + jnp.where(row >= step, turn(summed, step, 0), 0.0)
        step *= 2
    top = tile(solar_ref[...], total) * jnp.exp(att - summed)
    par = top * jnp.exp(-0.5 * att)
    east, north, temp, sal, mixing = [f[...] for f in fields]
    temp = temp + WARMING_UPTAKE * (top * (1.0 - jnp.exp(-att))) * wet

    def below(v):
        return turn(v, -rows, 0)

    density = SALT_EXPANSION * sal - WARM_EXPANSION * temp
    face = 0.5 * (mixing + below(mixing)) + CONVECT_MIX / (1.0 + jnp.exp(below(density) - density))
    face = jnp.where(row < total - rows, face * below(wet), 0.0)

    def stir(v):
        flux = face * (below(v) - v)
        return v + flux - turn(flux, rows, 0)

    mixed = [stir(v) for v in (east, north, temp, sal)]

    def band_of(v):
        value = v[:cells]
        for b in range(1, count):
            value = jnp.where(g == b, v[b * cells : (b + 1) * cells], value)
        return value

    u = band_of(mixed[0])
    wet_band = band_of(wet)
    band_ref[0] = u
    band_ref[1] = band_of(mixed[1])
    speed_ref[pl.ds(0, levels), :] = band_ref[1, pl.ds(rows - 1, levels, stride=rows), :]
    speed_ref[pl.ds(levels, levels), :] = jnp.zeros((levels, width), F32)
    speed_ref[pl.ds(2 * levels, levels), :] = jnp.zeros((levels, width), F32)

    x_even = lax.rem(lax.axis_index("gx"), 2) == 0
    xa, xb = in_xa[...], in_xb[...]
    left, right = jnp.where(x_even, xb, xa), jnp.where(x_even, xa, xb)
    left, right = pack_sides(wet_band, tracers + 1, tracers + 3, left, right)
    _, right = pack_sides(u, tracers, tracers + 3, left, right)
    msg_xa[...] = jnp.where(x_even, right, left)
    msg_xb[...] = jnp.where(x_even, left, right)
    band_ref[2] = band_of(mixed[2])
    band_ref[3] = band_of(face)
    band_ref[4] = band_of(turn(face, rows, 0))
    band_ref[5] = band_of(par)
    band_ref[6] = wet_band
    for at, v in enumerate(mixed):
        full_out[at][...] = v
    if first_step:
        full_out[4][...] = mixing


def start_own_strip(rows, count, g, full, outs, strips, sems):
    strip = rows // count
    all_levels = full[0].shape[0] // rows
    copies = [pltpu.make_async_copy(strips[at], outs[at], sems.at[at]) for at in range(4)]
    for at in range(4):
        for r in range(strip):
            value = full[at][pl.ds(r, all_levels, stride=rows), :]
            for s in range(1, count):
                value = jnp.where(g == s, full[at][pl.ds(s * strip + r, all_levels, stride=rows), :], value)
            strips[at][pl.ds(r, all_levels, stride=strip), :] = value
        copies[at].start()
    return copies


def lower(opening, speed):
    return opening * (jnp.maximum(speed, 0.0) + SIDE_DIFFUSE)


def upper(opening, speed):
    return opening * (jnp.minimum(speed, 0.0) - SIDE_DIFFUSE)


def inner_kernel(rows, count, first_step, last_step, *refs):
    refs = Refs(refs)
    if first_step:
        params, (rates_ref,) = refs.take(3), refs.take(1)
    else:
        tiles_ref, w_ref = refs.take(2)
    c_ref, band_ref = refs.take(2)
    lev_in = refs.take(1 if count == 2 else 2)
    if last_step:
        full = refs.take(4)
    (part_ref,) = refs.take(1)
    if last_step:
        outs = refs.take(4)
    else:
        (p_part,) = refs.take(1)
    if first_step:
        tiles_ref, w_ref = refs.take(2)
    if last_step:
        strips, (sems,) = refs.take(4), refs.take(1)
        copies = start_own_strip(rows, count, lax.axis_index("grp"), full, outs, strips, sems)
    (mix_ref,) = refs.take(1)
    tracers, cells, width = c_ref.shape
    if first_step:
        w_ref[...] = spread_rates(rates_ref[...], tracers)
        for at, param in enumerate(params):
            values = param[...]
            for t in range(tracers):
                tiles_ref[at, t] = jnp.broadcast_to(values[:, t : t + 1], (SUB, width))
    mix(w_ref[...], c_ref, mix_ref)
    lane = iota((cells, width), 1)
    at_row = lax.rem(iota((cells, width), 0), rows)
    u = band_ref[0]
    v = band_ref[1]
    wet = band_ref[6]

    def west(x):
        return turn(x, 1, 1)

    def east(x):
        return turn(x, -1, 1)

    def south(x):
        return turn(x, 1, 0)

    def north(x):
        return turn(x, -1, 0)

    open_w = jnp.where(lane == 0, 0.0, wet * west(wet))
    open_e = jnp.where(lane == width - 1, 0.0, wet * east(wet))
    open_s = jnp.where(at_row == 0, 0.0, wet * south(wet))
    open_n = jnp.where(at_row == rows - 1, 0.0, wet * north(wet))
    k_w = lower(open_w, west(u))
    k_e = -upper(open_e, u)
    k_s = lower(open_s, south(v))
    k_n = -upper(open_n, v)
    k_d = band_ref[3]
    k_u = band_ref[4]
    k_c = (upper(open_w, west(u)) - lower(open_e, u)) + (upper(open_s, south(v)) - lower(open_n, v))
    k_c = 1.0 + (k_c - k_d - k_u)
    par = band_ref[5]
    lit = TIME_STEP * wet
    warm = lit * jnp.exp(WARMING_FACTOR * (band_ref[2] - 20.0))
    lit = lit * par
    pigment = jnp.zeros((cells, width), F32)
    for t in range(tracers):
        c = c_ref[t]
        at = SUB - rows + t * rows
        up8 = lev_in[0][pl.ds(at + rows - SUB, SUB), :]
        down8 = lev_in[-1][pl.ds(at, SUB), :]
        c_u = turn(jnp.concatenate([up8, c], axis=0), rows, 0)[SUB:]
        c_d = turn(jnp.concatenate([c, down8], axis=0), -rows, 0)[:cells]
        part = (
            (k_c + tile(tiles_ref[0, t], cells) * (lit / (par + tile(tiles_ref[1, t], cells)))) * c
            + (k_u * c_u + k_d * c_d)
            + (k_w * west(c) + k_e * east(c))
            + (k_s * south(c) + k_n * north(c))
            + warm * mix_ref[t]
        )
        part_ref[t] = part
        if not last_step:
            pigment = pigment + tile(tiles_ref[2, t], cells) * part
    if last_step:
        for copy in copies:
            copy.wait()
    else:
        p_part[...] = pigment


def x_halo(got_xa, got_xb):
    x_even = lax.rem(lax.axis_index("gx"), 2) == 0
    xa, xb = got_xa[...], got_xb[...]
    return jnp.where((lax.rem(iota(xa.shape, 1), 2) == 0) == x_even, xb, xa)


def spread_rows(rows, got_ya, got_yb, out_ref, slot):
    y_even = lax.rem(lax.axis_index("gy"), 2) == 0
    levels = got_ya.shape[1]
    ya, yb = got_ya[slot], got_yb[slot]
    out_ref[slot, pl.ds(0, levels, stride=rows), :] = jnp.where(y_even, yb, ya)
    out_ref[slot, pl.ds(rows - 1, levels, stride=rows), :] = jnp.where(y_even, ya, yb)


def side_factors(rows, sizes, halo_ref, wet_out, speed, speed_s, band_ref, tracers):
    _, size_x, size_y = sizes
    x = lax.axis_index("gx")
    y = lax.axis_index("gy")
    u = band_ref[0]
    v = band_ref[1]
    wet = band_ref[6]
    cells, width = wet.shape
    speed_s[pl.ds(0, cells // rows, stride=rows), :] = speed[pl.ds(0, cells // rows), :]
    lane = iota((cells, width), 1)
    at_row = lax.rem(iota((cells, width), 0), rows)
    at_w, at_e, at_s, at_n = lane == 0, lane == width - 1, at_row == 0, at_row == rows - 1
    wet_x = wet * sides_of(halo_ref[...], tracers + 1, tracers + 3, cells)
    wet_y = wet * wet_out
    open_w = jnp.where(at_w & (x > 0), wet_x, 0.0)
    open_e = jnp.where(at_e & (x < size_x - 1), wet_x, 0.0)
    open_s = jnp.where(at_s & (y > 0), wet_y, 0.0)
    open_n = jnp.where(at_n & (y < size_y - 1), wet_y, 0.0)
    u_w = sides_of(halo_ref[...], tracers, tracers + 3, cells)
    v_s = jnp.where(at_s, speed_s[...], 0.0)
    k_x = lower(open_w, u_w) - upper(open_e, u)
    k_y = lower(open_s, v_s) - upper(open_n, v)
    k_c = (upper(open_w, u_w) - lower(open_e, u)) + (upper(open_s, v_s) - lower(open_n, v))
    return k_x, k_y, k_c


def sideways(rows, factors, sides, outer, c):
    k_x, k_y, k_c = factors
    at_row = lax.rem(iota(c.shape, 0), rows)
    edge = (at_row == 0) | (at_row == rows - 1)
    return (k_x * sides + k_c * c) + jnp.where(edge, k_y * outer, 0.0)


def early_kernel(rows, count, sizes, first_step, *refs):
    refs = Refs(refs)
    c_ref, band_ref, got_xa, got_xb, got_ya, got_yb = refs.take(6)
    (speed,) = refs.take(1)
    p_in, part_ref, p_part = refs.take(3)
    if not first_step:
        (wet_in,) = refs.take(1)
    k_ref, halo_ref, spread_s, wet_out, p_ref, p_msg, speed_s = refs.take(7)
    g = lax.axis_index("grp")
    tracers, cells, width = c_ref.shape
    halo_ref[...] = x_halo(got_xa, got_xb)
    for slot in range(got_ya.shape[0]):
        spread_rows(rows, got_ya, got_yb, spread_s, slot)
    wet_out[...] = spread_s[tracers + 1] if first_step else wet_in[...]
    factors = side_factors(rows, sizes, halo_ref, wet_out[...], speed, speed_s, band_ref, tracers)
    for at, k in enumerate(factors):
        k_ref[at] = k
    side = sides_of(halo_ref[...], tracers + 2, tracers + 3, cells)
    change = sideways(rows, factors, side, spread_s[tracers], p_in[...])
    p_ref[...] = p_part[...] + change
    write_pigment(rows, count, p_ref, p_msg, g)


def step_kernel(rows, *refs):
    refs = Refs(refs)
    c_ref, part_ref, k_ref, halo_ref, spread_s, p_ref = refs.take(6)
    out_ref, msg_xa, msg_xb, msg_ya, msg_yb = refs.take(5)
    tracers = c_ref.shape[0]
    factors = [k_ref[i] for i in range(3)]
    for t in range(tracers):
        out_ref[t] = part_ref[t] + sideways(
                rows, factors, sides_of(halo_ref[...], t, tracers + 3, c_ref.shape[1]), spread_s[t], c_ref[t]
            )
    pack(rows, out_ref, p_ref, msg_xa, msg_xb, msg_ya, msg_yb, refs.refs)


def final_kernel(rows, sizes, first_step, *refs):
    refs = Refs(refs)
    c_ref, part_ref, band_ref, got_xa, got_xb, got_ya, got_yb = refs.take(7)
    (speed,) = refs.take(1)
    if not first_step:
        (wet_in,) = refs.take(1)
    out_hbm, spread_s, speed_s, halo_ref, new_s, sems = refs.take(6)
    tracers = c_ref.shape[0]
    halo_ref[...] = x_halo(got_xa, got_xb)
    if first_step:
        spread_rows(rows, got_ya, got_yb, spread_s, tracers + 1)
    wet_out = spread_s[tracers + 1] if first_step else wet_in[...]
    factors = side_factors(rows, sizes, halo_ref, wet_out, speed, speed_s, band_ref, tracers)
    copies = []
    for i, (a, n) in enumerate(chunks(tracers, sems.shape[0])):
        for t in range(a, a + n):
            spread_rows(rows, got_ya, got_yb, spread_s, t)
            new_s[t] = part_ref[t] + sideways(
                rows, factors, sides_of(halo_ref[...], t, tracers + 3, c_ref.shape[1]), spread_s[t], c_ref[t]
            )
        copies.append(pltpu.make_async_copy(new_s.at[pl.ds(a, n)], out_hbm.at[pl.ds(a, n)], sems.at[i]))
        copies[-1].start()
    for copy in copies:
        copy.wait()


def call(kernel, ins, outs, in_specs=None, out_specs=None, scratch=(), flops=1 << 20, moved=1 << 20):
    return pl.pallas_call(
        kernel,
        in_specs=[vmem() for _ in ins] if in_specs is None else in_specs,
        out_specs=[vmem() for _ in outs] if out_specs is None else out_specs,
        out_shape=outs,
        scratch_shapes=list(scratch),
        compiler_params=pltpu.CompilerParams(vmem_limit_bytes=VMEM_LIMIT),
        cost_estimate=pl.CostEstimate(flops=flops, bytes_accessed=moved, transcendentals=0),
    )(*ins)


def per_device(
    sizes,
    zonal_boundary_speed,
    meridional_boundary_speed,
    potential_warmth,
    saltiness_field,
    quiescent_mixing_profile,
    substance_amounts,
    submerged_layer_number,
    solar_radiation,
    interaction_rates,
    photosynthetic_rates,
    saturation_irradiance,
    pigment_per_tracer,
):
    count = sizes[0]
    result_dimensions = zonal_boundary_speed.shape
    all_levels, _, strip, width = result_dimensions
    tracers, levels, rows, _ = substance_amounts.shape
    cells = levels * rows
    total = all_levels * rows
    strip_cells = all_levels * strip
    dma = pltpu.SemaphoreType.DMA
    column = pltpu.VMEM((total, width), F32)
    band_s = pltpu.VMEM((cells, width), F32)

    own = [
        f.reshape(strip_cells, width)
        for f in (
            zonal_boundary_speed,
            meridional_boundary_speed,
            potential_warmth,
            saltiness_field,
            quiescent_mixing_profile,
        )
    ]
    _, height = raw_window(rows, count, strip_cells, 0)
    params = [
        p.reshape(1, tracers) for p in (photosynthetic_rates, saturation_irradiance, pigment_per_tracer)
    ]
    (first,) = call(first_kernel, [], [shape(SUB, width)], flops=1 << 30)
    small = [*params, interaction_rates, submerged_layer_number, solar_radiation]
    raw, window, *small = call(
        functools.partial(raw_kernel, rows, count),
        [first, *own, *small],
        [
            shape(5, strip_cells, width),
            shape(5 * height, width),
            *[jax.ShapeDtypeStruct(v.shape, v.dtype) for v in small],
        ],
    )
    *params, rates, layers, light = small
    raw_others = from_others(window, count)

    sent_pigment = shape(pigment_rows(rows, cells, count), width)
    sent_levels = level_shapes(tracers, rows, width, count)
    cols = shape(cells, width)
    sent_cols = shape(cells // 2, width) if folds(tracers + 3, cells, width) else cols
    field = shape(tracers, cells, width)
    c = substance_amounts.reshape(tracers, cells, width)
    pigment, p_msg = call(
        functools.partial(prep_kernel, rows, count),
        [params[2], c],
        [cols, sent_pigment],
    )
    full = None
    for step in range(STEPS):
        first_step, last_step = step == 0, step == STEPS - 1
        p_others = from_others(p_msg, count)
        if first_step:
            lines = shape(tracers + 2, levels, width)
            xa, xb, ya, yb, depth, solar, *levs = call(
                functools.partial(pack_kernel, rows),
                [layers, light, c, pigment],
                [
                    sent_cols,
                    sent_cols,
                    lines,
                    lines,
                    jax.ShapeDtypeStruct((SUB, width), jnp.int32),
                    shape(SUB, width),
                    *sent_levels,
                ],
                flops=1 << 24,
            )
        ya = lax.ppermute(ya, AXES, pairing(sizes, "gy", 0))
        yb = lax.ppermute(yb, AXES, pairing(sizes, "gy", 1))
        if count == 2:
            lev = from_others(levs[0], count)
        else:
            lev = [
                lax.ppermute(levs[0], "grp", [(i, (i + 1) % count) for i in range(count)]),
                lax.ppermute(levs[1], "grp", [((i + 1) % count, i) for i in range(count)]),
            ]
        band, xa, xb, speed, *full = call(
            functools.partial(ocean_kernel, rows, count, tracers, first_step),
            [depth, solar, xa, xb, pigment, *p_others, *([raw, *raw_others] if first_step else full)],
            [
                shape(7, cells, width),
                sent_cols,
                sent_cols,
                shape(3 * levels, width),
                *[shape(total, width)] * (5 if first_step else 4),
            ],
            scratch=[band_s]
            + [column] * (5 if first_step else 0)
            + [pltpu.VMEM((strip_cells, width), F32)] * (5 * (count - 1) if first_step else 0),
            flops=1<<32,
        )
        xa = lax.ppermute(xa, AXES, pairing(sizes, "gx", 0))
        xb = lax.ppermute(xb, AXES, pairing(sizes, "gx", 1))
        speed = lax.ppermute(speed, AXES, upward(sizes))
        tables = [shape(3, tracers, SUB, width), shape(tracers * SUB, tracers * SUB)]
        part, *rest = call(
            functools.partial(inner_kernel, rows, count, first_step, last_step),
            [*([*params, rates] if first_step else known_rates), c, band, *lev, *(full if last_step else [])],
            [field]
            + ([shape(strip_cells, width)] * 4 if last_step else [cols])
            + (tables if first_step else []),
            out_specs=[vmem()]
            + ([hbm()] * 4 if last_step else [vmem()])
            + ([vmem()] * 2 if first_step else []),
            scratch=([pltpu.VMEM((strip_cells, width), F32)] * 4 + [dma((4,))] if last_step else [])
            + [pltpu.VMEM((tracers, cells, width), F32)],
            flops=1 << 10,
        )
        if first_step:
            *rest, tiles, weights = rest
            known_rates = [tiles, weights]
        known = [] if first_step else [wet_out]
        if not last_step:
            k, halo, spread, wet_out, pigment_next, p_msg = call(
                functools.partial(early_kernel, rows, count, sizes, first_step),
                [c, band, xa, xb, ya, yb, speed, pigment, part, *rest, *known],
                [shape(3, cells, width), sent_cols, shape(tracers + 2, cells, width), cols, cols, sent_pigment],
                scratch=[band_s],
            )
            pigment = pigment_next
            lines = shape(tracers + (0 if step + 1 == STEPS - 1 else 1), levels, width)
            c, xa, xb, ya, yb, *levs = call(
                functools.partial(step_kernel, rows),
                [c, part, k, halo, spread, pigment],
                [field, sent_cols, sent_cols, lines, lines, *sent_levels],
                flops=1<<32,
            )
        else:
            ocean = rest
            (c,) = call(
                functools.partial(final_kernel, rows, sizes, first_step),
                [c, part, band, xa, xb, ya, yb, speed, *known],
                [field],
                out_specs=[hbm()],
                scratch=[
                    pltpu.VMEM((tracers + 2, cells, width), F32),
                    band_s,
                    pltpu.VMEM(sent_cols.shape, F32),
                    pltpu.VMEM((tracers, cells, width), F32),
                    dma((5,)),
                ],
            )
    return tuple(f.reshape(result_dimensions) for f in ocean) + (c.reshape(substance_amounts.shape),)


def solution(mesh):
    ocean = P(None, "gy", "grp", "gx")
    tracer = P(None, "grp", "gy", "gx")
    surface = P("gy", "gx")
    sizes = tuple(mesh.shape[a] for a in AXES)
    return jax.shard_map(
        functools.partial(per_device, sizes),
        mesh=mesh,
        in_specs=(ocean,) * 5 + (tracer, surface, surface) + (P(),) * 4,
        out_specs=(ocean,) * 4 + (tracer,),
        check_vma=False,
    )
```

```python
import functools

import jax
import jax.numpy as jnp
from jax import lax
from jax.experimental import pallas as pl
from jax.experimental.pallas import tpu as pltpu
from jax.sharding import PartitionSpec as P

STEPS = 2

WATER_ATTEN = 0.01
PIGMENT_ATTEN = 0.05
WARMING_UPTAKE = 5.0
WARM_EXPANSION = 0.2
SALT_EXPANSION = 0.8
CONVECT_MIX = 0.15
SIDE_DIFFUSE = 0.05
WARMING_FACTOR = 0.0633
TIME_STEP = 0.5

SUB = 8
AXES = ("grp", "gx", "gy")
VMEM_LIMIT = 48 * 1024 * 1024

F32 = jnp.float32


def vmem():
    return pl.BlockSpec(memory_space=pltpu.VMEM)


def hbm():
    return pl.BlockSpec(memory_space=pltpu.HBM)


def shape(*dims):
    return jax.ShapeDtypeStruct(dims, F32)


def turn(x, shift, axis):
    shift = shift % x.shape[axis]
    return x if shift == 0 else pltpu.roll(x, shift, axis)


def iota(x, axis):
    return lax.broadcasted_iota(jnp.int32, x, axis)


def pairing(sizes, axis, odd):
    size_g, size_x, size_y = sizes

    def partner(g, x, y):
        i, n = (x, size_x) if axis == "gx" else (y, size_y)
        j = i + 1 if i % 2 == odd else i - 1
        if 0 <= j < n:
            return (g, j, y) if axis == "gx" else (g, x, j)
        if axis == "gx":
            return (g, x, y ^ 1) if (y ^ 1) < size_y else (g, x, y)
        return (g, x ^ 1, y) if (x ^ 1) < size_x else (g, x, y)

    def index(g, x, y):
        return (g * size_x + x) * size_y + y

    return [
        (index(g, x, y), index(*partner(g, x, y)))
        for g in range(size_g)
        for x in range(size_x)
        for y in range(size_y)
    ]


def upward(sizes):
    size_g, size_x, size_y = sizes
    return [
        ((g * size_x + x) * size_y + y, (g * size_x + x) * size_y + (y + 1) % size_y)
        for g in range(size_g)
        for x in range(size_x)
        for y in range(size_y)
    ]


def from_others(value, count):
    return [
        lax.ppermute(value, "grp", [(i, (i + k) % count) for i in range(count)])
        for k in range(1, count)
    ]


def chunks(n, parts):
    step = -(-n // parts)
    return [(a, min(step, n - a)) for a in range(0, n, step)]


class Refs:
    def __init__(self, refs):
        self.refs = list(refs)

    def take(self, n):
        out, self.refs = self.refs[:n], self.refs[n:]
        return out


def pick(mine, others, k):
    value = mine
    for at, other in enumerate(others):
        value = jnp.where(k == at + 1, other, value)
    return value


def folds(slots, cells, width):
    return 4 * slots < width and cells % (2 * SUB) == 0


def halves_of(cells, slots, width):
    if not folds(slots, cells, width):
        return [(slice(0, cells), 0)]
    return [(slice(0, cells // 2), 0), (slice(cells // 2, cells), width // 2)]


def pack_sides(c, slot, slots, left, right):
    cells, width = c.shape
    at = 2 * (slot + 1)
    lane = iota(left.shape, 1)
    for rows, base in halves_of(cells, slots, width):
        left = jnp.where(lane == base + at - 1, turn(c[rows], base + at - 1, 1), left)
        right = jnp.where(lane == base + at, turn(c[rows], base + at + 1, 1), right)
    return left, right


def sides_of(halo, slot, slots, cells):
    at = 2 * (slot + 1)
    width = halo.shape[1]
    turned = [turn(halo, -at - base, 1) for _, base in halves_of(cells, slots, width)]
    return turned[0] if len(turned) == 1 else jnp.concatenate(turned, axis=0)


def compact(rows, cells, count):
    return count == 2 and SUB == 2 * rows and cells >= 2 * SUB


def pigment_rows(rows, cells, count):
    return cells // 2 + SUB if compact(rows, cells, count) else cells


def level_shapes(tracers, rows, width, count):
    height = tracers * rows + 2 * (SUB - rows)
    height += -height % SUB
    return [shape(height, width)] * (1 if count == 2 else 2)


def write_levels(c, t, rows, levs, g):
    cells = c.shape[0]
    here = pl.ds(SUB - rows + t * rows, rows)
    if len(levs) == 1:
        levs[0][here, :] = jnp.where(g == 0, c[cells - rows :], c[:rows])
    else:
        levs[0][here, :] = c[cells - rows :]
        levs[1][here, :] = c[:rows]


def in_strip(rows, count, width, member):
    at_row = lax.rem(iota((SUB, width), 0), rows)
    strip = rows // count
    return (at_row >= member * strip) & (at_row < (member + 1) * strip)


def write_pigment(rows, count, p_ref, msg, g):
    cells, width = p_ref.shape
    if not compact(rows, cells, count):
        msg[pl.ds(0, cells), :] = p_ref[...]
        return
    levels, strip = cells // rows, rows // count
    for r in range(strip):
        msg[pl.ds(r, levels, stride=strip), :] = jnp.where(
            g == 0, p_ref[pl.ds(strip + r, levels, stride=rows), :], p_ref[pl.ds(r, levels, stride=rows), :]
        )
    blocks = [p_ref[pl.ds(at, SUB), :] for at in range(0, cells, SUB)]
    inner = blocks[1]
    for block in blocks[2:-1]:
        inner = inner + block
    inner = jnp.zeros_like(inner) if len(blocks) == 2 else inner
    near = jnp.where(g == 0, blocks[-1], blocks[0])
    rest = inner + jnp.where(g == 0, blocks[0], blocks[-1])
    rest = rest + turn(rest, rows, 0)
    msg[pl.ds(cells // 2, SUB), :] = jnp.where(in_strip(rows, count, width, g), near, turn(rest, strip, 0))


def read_pigment(rows, count, msg, other_s, g):
    cells, width = other_s.shape
    if not compact(rows, cells, count):
        return msg[pl.ds(0, cells), :]
    levels, strip = cells // rows, rows // count
    for s in range(count):
        for r in range(strip):
            other_s[pl.ds(s * strip + r, levels, stride=rows), :] = jnp.where(
                g == s, msg[pl.ds(r, levels, stride=strip), :], 0.0
            )
    edge = msg[pl.ds(cells // 2, SUB), :]
    theirs = in_strip(rows, count, width, 1 - g)
    first = other_s[pl.ds(0, SUB), :]
    rest = jnp.where(iota((SUB, width), 0) < rows, turn(edge, strip, 0), 0.0)
    other_s[pl.ds(0, SUB), :] = jnp.where(theirs, jnp.where(g == 0, edge, rest), first)
    last = other_s[pl.ds(cells - SUB, SUB), :]
    other_s[pl.ds(cells - SUB, SUB), :] = jnp.where(theirs & (g == 1), edge, last)
    return other_s[...]


def raw_window(rows, count, strip_cells, member):
    if count != 2:
        return 0, strip_cells
    height = strip_cells // 2 + 2 * (rows // count)
    return member * (strip_cells - height), height


def first_kernel(out_ref):
    out_ref[...] = jnp.zeros(out_ref.shape, F32)


def raw_kernel(rows, count, first_ref, *refs):
    refs = Refs(refs)
    fields, small_in = refs.take(5), refs.take(6)
    raw_ref, out_ref = refs.take(2)
    g = lax.axis_index("grp")
    for small, small_out in zip(small_in, refs.take(6)):
        small_out[...] = small[...]
    strip_cells = raw_ref.shape[1]
    low, height = raw_window(rows, count, strip_cells, 0)
    high, _ = raw_window(rows, count, strip_cells, 1)
    for at, field in enumerate(fields):
        raw_ref[at] = field[...]
        lower_part, upper_part = field[pl.ds(low, height), :], field[pl.ds(high, height), :]
        out_ref[pl.ds(at * height, height), :] = jnp.where(g == 0, upper_part, lower_part)


def tile(v, cells):
    width = v.shape[1]
    return jnp.broadcast_to(v[None], (cells // SUB, SUB, width)).reshape(cells, width)


def prep_kernel(rows, count, pig_ref, c_ref, p_ref, p_msg):
    g = lax.axis_index("grp")
    tracers, cells, width = c_ref.shape
    weights = pig_ref[...]
    pigment = jnp.zeros((cells, width), F32)
    for t in range(tracers):
        c = c_ref[t]
        pigment = pigment + tile(jnp.broadcast_to(weights[:, t : t + 1], (SUB, width)), cells) * c
    p_ref[...] = pigment
    write_pigment(rows, count, p_ref, p_msg, g)


def halves(v):
    high = v.astype(jnp.bfloat16)
    return high, (v - high.astype(F32)).astype(jnp.bfloat16)


def dot(a, b, **kw):
    return jnp.dot(a, b, preferred_element_type=F32, **kw)


def spread_rates(rates, tracers):
    exact = functools.partial(dot, precision=lax.Precision.HIGHEST)
    depth = tracers * SUB
    spread = jnp.where(iota((depth, tracers), 0) // SUB == iota((depth, tracers), 1), 1.0, 0.0)
    spread_t = jnp.where(iota((tracers, depth), 1) // SUB == iota((tracers, depth), 0), 1.0, 0.0)
    weights = exact(exact(spread, rates), spread_t)
    return jnp.where(
        lax.rem(iota((depth, depth), 0), SUB) == lax.rem(iota((depth, depth), 1), SUB), weights, 0.0
    )


def mix(weights, c_ref, mix_ref):
    tracers, cells, width = c_ref.shape
    w_high, w_low = halves(weights)
    for b in range(cells // SUB):
        here = pl.ds(b * SUB, SUB)
        c_high, c_low = halves(c_ref[:, here, :].reshape(tracers * SUB, width))
        mixed = dot(w_high, c_high) + (dot(w_high, c_low) + dot(w_low, c_high))
        mix_ref[:, here, :] = mixed.reshape(tracers, SUB, width)


def put_rows(msg_ya, msg_yb, slot, first, last):
    y_even = lax.rem(lax.axis_index("gy"), 2) == 0
    msg_ya[slot] = jnp.where(y_even, last, first)
    msg_yb[slot] = jnp.where(y_even, first, last)


def pack(rows, c_ref, p_ref, msg_xa, msg_xb, msg_ya, msg_yb, levs):
    tracers, cells, _ = c_ref.shape
    levels = cells // rows
    x_even = lax.rem(lax.axis_index("gx"), 2) == 0
    left = right = jnp.zeros(msg_xa.shape, F32)
    left, right = pack_sides(p_ref[...], tracers + 2, tracers + 3, left, right)
    g = lax.axis_index("grp")
    for t in range(tracers):
        left, right = pack_sides(c_ref[t], t, tracers + 3, left, right)
        write_levels(c_ref[t], t, rows, levs, g)
    msg_xa[...] = jnp.where(x_even, right, left)
    msg_xb[...] = jnp.where(x_even, left, right)
    first, last = pl.ds(0, levels, stride=rows), pl.ds(rows - 1, levels, stride=rows)
    for t in range(tracers):
        put_rows(msg_ya, msg_yb, t, c_ref[t, first, :], c_ref[t, last, :])
    if msg_ya.shape[0] > tracers:
        put_rows(msg_ya, msg_yb, tracers, p_ref[first, :], p_ref[last, :])


def pack_kernel(rows, *refs):
    refs = Refs(refs)
    depth_in, solar_in, c_ref, p_ref = refs.take(4)
    msg_xa, msg_xb, msg_ya, msg_yb, depth_ref, solar_ref = refs.take(6)
    levs = refs.refs
    tracers, cells, width = c_ref.shape
    for r in range(0, SUB, rows):
        depth_ref[pl.ds(r, rows), :] = depth_in[...]
        solar_ref[pl.ds(r, rows), :] = solar_in[...]
    pack(rows, c_ref, p_ref, msg_xa, msg_xb, msg_ya, msg_yb, levs)
    levels = cells // rows
    level = lax.axis_index("grp") * levels + iota((levels, width), 0)
    wet_first = jnp.where(level < depth_in[pl.ds(0, 1), :], 1.0, 0.0)
    wet_last = jnp.where(level < depth_in[pl.ds(rows - 1, 1), :], 1.0, 0.0)
    put_rows(msg_ya, msg_yb, tracers + 1, wet_first, wet_last)


def ocean_kernel(rows, count, tracers, first_step, *refs):
    refs = Refs(refs)
    depth_ref, solar_ref = refs.take(2)
    in_xa, in_xb = refs.take(2)
    p_own, *p_others = refs.take(count)
    if first_step:
        own_fields, *other_fields = refs.take(count)
    else:
        fields = refs.take(5)
    band_ref, msg_xa, msg_xb, speed_ref = refs.take(4)
    full_out = refs.take(5 if first_step else 4)
    p_full, p_other_s = refs.take(2)
    if first_step:
        fields = refs.take(5)
        other_s = refs.take(5 * (count - 1))
    face_s, par_s, wet_s = refs.take(3)
    g = lax.axis_index("grp")
    cells, width = p_own.shape
    levels = cells // rows
    total = count * cells
    all_levels = total // rows
    strip = rows // count

    pigments = [read_pigment(rows, count, o, p_other_s, g) for o in p_others]
    for b in range(count):
        k = lax.rem(g - b + count, count)
        p_full[pl.ds(b * cells, cells), :] = pick(p_own[...], pigments, k)
    if first_step:
        strip_cells = all_levels * strip
        for at in range(5):
            for k in range(count - 1):
                other = other_s[5 * k + at]
                low, height = raw_window(rows, count, strip_cells, 0)
                value = other_fields[k][pl.ds(at * height, height), :]
                if count != 2:
                    other[...] = value
                    continue
                high, _ = raw_window(rows, count, strip_cells, 1)
                other[...] = jnp.zeros((strip_cells, width), F32)
                other[pl.ds(low, height), :] = jnp.where(g == 0, value, 0.0)
                kept = jnp.where(iota(value.shape, 0) < low + height - high, other[pl.ds(high, height), :], 0.0)
                other[pl.ds(high, height), :] = jnp.where(g == 1, value, kept)
            for s in range(count):
                k = lax.rem(g - s + count, count)
                for r in range(strip):
                    here = pl.ds(r, all_levels, stride=strip)
                    fields[at][pl.ds(s * strip + r, all_levels, stride=rows), :] = pick(
                        own_fields[at, here, :], [other_s[5 * j + at][here, :] for j in range(count - 1)], k
                    )

    row = iota((total, width), 0)
    wet = jnp.where(row // rows < tile(depth_ref[...], total), 1.0, 0.0)
    att = WATER_ATTEN + PIGMENT_ATTEN * p_full[...]
    summed = att
    step = rows
    while step < total:
        summed = summed + jnp.where(row >= step, turn(summed, step, 0), 0.0)
        step *= 2
    top = tile(solar_ref[...], total) * jnp.exp(att - summed)
    par = top * jnp.exp(-0.5 * att)
    east, north, temp, sal, mixing = [f[...] for f in fields]
    temp = temp + WARMING_UPTAKE * (top * (1.0 - jnp.exp(-att))) * wet

    def below(v):
        return turn(v, -rows, 0)

    density = SALT_EXPANSION * sal - WARM_EXPANSION * temp
    face = 0.5 * (mixing + below(mixing)) + CONVECT_MIX / (1.0 + jnp.exp(below(density) - density))
    face = jnp.where(row < total - rows, face * below(wet), 0.0)

    def stir(v):
        flux = face * (below(v) - v)
        return v + flux - turn(flux, rows, 0)

    for at, v in enumerate((east, north, temp, sal)):
        full_out[at][...] = stir(v)
    if first_step:
        full_out[4][...] = mixing
    face_s[...] = face
    par_s[...] = par
    wet_s[...] = wet

    band = pl.ds(pl.multiple_of(g * cells, SUB), cells)
    above = pl.ds(pl.multiple_of(lax.max(g * cells - SUB, 0), SUB), SUB)
    face_band = face_s[band, :]
    lifted = turn(jnp.concatenate([face_s[above, :], face_band], axis=0), rows, 0)[SUB:]
    lifted = jnp.where((iota((cells, width), 0) < rows) & (g == 0), 0.0, lifted)
    u = full_out[0][band, :]
    wet_band = wet_s[band, :]
    band_ref[0] = u
    band_ref[1] = full_out[1][band, :]
    band_ref[2] = full_out[2][band, :]
    band_ref[3] = face_band
    band_ref[4] = lifted
    band_ref[5] = par_s[band, :]
    band_ref[6] = wet_band

    x_even = lax.rem(lax.axis_index("gx"), 2) == 0
    xa, xb = in_xa[...], in_xb[...]
    left, right = jnp.where(x_even, xb, xa), jnp.where(x_even, xa, xb)
    left, right = pack_sides(wet_band, tracers + 1, tracers + 3, left, right)
    _, right = pack_sides(u, tracers, tracers + 3, left, right)
    msg_xa[...] = jnp.where(x_even, right, left)
    msg_xb[...] = jnp.where(x_even, left, right)
    speed_ref[pl.ds(0, levels), :] = band_ref[1, pl.ds(rows - 1, levels, stride=rows), :]
    speed_ref[pl.ds(levels, levels), :] = jnp.zeros((levels, width), F32)
    speed_ref[pl.ds(2 * levels, levels), :] = jnp.zeros((levels, width), F32)


def start_own_strip(rows, count, g, full, outs, strips, sems):
    strip = rows // count
    all_levels = full[0].shape[0] // rows
    copies = [pltpu.make_async_copy(strips[at], outs[at], sems.at[at]) for at in range(4)]
    for at in range(4):
        for r in range(strip):
            value = full[at][pl.ds(r, all_levels, stride=rows), :]
            for s in range(1, count):
                value = jnp.where(g == s, full[at][pl.ds(s * strip + r, all_levels, stride=rows), :], value)
            strips[at][pl.ds(r, all_levels, stride=strip), :] = value
        copies[at].start()
    return copies


def lower(opening, speed):
    return opening * (jnp.maximum(speed, 0.0) + SIDE_DIFFUSE)


def upper(opening, speed):
    return opening * (jnp.minimum(speed, 0.0) - SIDE_DIFFUSE)


def inner_kernel(rows, count, first_step, last_step, *refs):
    refs = Refs(refs)
    if first_step:
        params, (rates_ref,) = refs.take(3), refs.take(1)
    else:
        tiles_ref, w_ref = refs.take(2)
    c_ref, band_ref, _ = refs.take(3)
    lev_in = refs.take(1 if count == 2 else 2)
    if last_step:
        full = refs.take(4)
    (part_ref,) = refs.take(1)
    if last_step:
        outs = refs.take(4)
    else:
        (p_part,) = refs.take(1)
    if first_step:
        tiles_ref, w_ref = refs.take(2)
    if last_step:
        strips, (sems,) = refs.take(4), refs.take(1)
        copies = start_own_strip(rows, count, lax.axis_index("grp"), full, outs, strips, sems)
    (mix_ref,) = refs.take(1)
    tracers, cells, width = c_ref.shape
    if first_step:
        w_ref[...] = spread_rates(rates_ref[...], tracers)
        for at, param in enumerate(params):
            values = param[...]
            for t in range(tracers):
                tiles_ref[at, t] = jnp.broadcast_to(values[:, t : t + 1], (SUB, width))
    mix(w_ref[...], c_ref, mix_ref)
    lane = iota((cells, width), 1)
    at_row = lax.rem(iota((cells, width), 0), rows)
    u = band_ref[0]
    v = band_ref[1]
    wet = band_ref[6]

    def west(x):
        return turn(x, 1, 1)

    def east(x):
        return turn(x, -1, 1)

    def south(x):
        return turn(x, 1, 0)

    def north(x):
        return turn(x, -1, 0)

    open_w = jnp.where(lane == 0, 0.0, wet * west(wet))
    open_e = jnp.where(lane == width - 1, 0.0, wet * east(wet))
    open_s = jnp.where(at_row == 0, 0.0, wet * south(wet))
    open_n = jnp.where(at_row == rows - 1, 0.0, wet * north(wet))
    k_w = lower(open_w, west(u))
    k_e = -upper(open_e, u)
    k_s = lower(open_s, south(v))
    k_n = -upper(open_n, v)
    k_d = band_ref[3]
    k_u = band_ref[4]
    k_c = (upper(open_w, west(u)) - lower(open_e, u)) + (upper(open_s, south(v)) - lower(open_n, v))
    k_c = 1.0 + (k_c - k_d - k_u)
    par = band_ref[5]
    lit = TIME_STEP * wet
    warm = lit * jnp.exp(WARMING_FACTOR * (band_ref[2] - 20.0))
    lit = lit * par
    pigment = jnp.zeros((cells, width), F32)
    for t in range(tracers):
        c = c_ref[t]
        at = SUB - rows + t * rows
        up8 = lev_in[0][pl.ds(at + rows - SUB, SUB), :]
        down8 = lev_in[-1][pl.ds(at, SUB), :]
        c_u = turn(jnp.concatenate([up8, c], axis=0), rows, 0)[SUB:]
        c_d = turn(jnp.concatenate([c, down8], axis=0), -rows, 0)[:cells]
        part = (
            (k_c + tile(tiles_ref[0, t], cells) * (lit / (par + tile(tiles_ref[1, t], cells)))) * c
            + (k_u * c_u + k_d * c_d)
            + (k_w * west(c) + k_e * east(c))
            + (k_s * south(c) + k_n * north(c))
            + warm * mix_ref[t]
        )
        part_ref[t] = part
        if not last_step:
            pigment = pigment + tile(tiles_ref[2, t], cells) * part
    if last_step:
        for copy in copies:
            copy.wait()
    else:
        p_part[...] = pigment


def x_halo(got_xa, got_xb):
    x_even = lax.rem(lax.axis_index("gx"), 2) == 0
    xa, xb = got_xa[...], got_xb[...]
    return jnp.where((lax.rem(iota(xa.shape, 1), 2) == 0) == x_even, xb, xa)


def spread_rows(rows, got_ya, got_yb, out_ref, slot):
    y_even = lax.rem(lax.axis_index("gy"), 2) == 0
    levels = got_ya.shape[1]
    ya, yb = got_ya[slot], got_yb[slot]
    out_ref[slot, pl.ds(0, levels, stride=rows), :] = jnp.where(y_even, yb, ya)
    out_ref[slot, pl.ds(rows - 1, levels, stride=rows), :] = jnp.where(y_even, ya, yb)


def side_factors(rows, sizes, halo_ref, wet_out, speed, speed_s, band_ref, tracers):
    _, size_x, size_y = sizes
    x = lax.axis_index("gx")
    y = lax.axis_index("gy")
    u = band_ref[0]
    v = band_ref[1]
    wet = band_ref[6]
    cells, width = wet.shape
    speed_s[pl.ds(0, cells // rows, stride=rows), :] = speed[pl.ds(0, cells // rows), :]
    lane = iota((cells, width), 1)
    at_row = lax.rem(iota((cells, width), 0), rows)
    at_w, at_e, at_s, at_n = lane == 0, lane == width - 1, at_row == 0, at_row == rows - 1
    wet_x = wet * sides_of(halo_ref[...], tracers + 1, tracers + 3, cells)
    wet_y = wet * wet_out
    open_w = jnp.where(at_w & (x > 0), wet_x, 0.0)
    open_e = jnp.where(at_e & (x < size_x - 1), wet_x, 0.0)
    open_s = jnp.where(at_s & (y > 0), wet_y, 0.0)
    open_n = jnp.where(at_n & (y < size_y - 1), wet_y, 0.0)
    u_w = sides_of(halo_ref[...], tracers, tracers + 3, cells)
    v_s = jnp.where(at_s, speed_s[...], 0.0)
    k_x = lower(open_w, u_w) - upper(open_e, u)
    k_y = lower(open_s, v_s) - upper(open_n, v)
    k_c = (upper(open_w, u_w) - lower(open_e, u)) + (upper(open_s, v_s) - lower(open_n, v))
    return k_x, k_y, k_c


def sideways(rows, factors, sides, outer, c):
    k_x, k_y, k_c = factors
    at_row = lax.rem(iota(c.shape, 0), rows)
    edge = (at_row == 0) | (at_row == rows - 1)
    return (k_x * sides + k_c * c) + jnp.where(edge, k_y * outer, 0.0)


def early_kernel(rows, count, sizes, first_step, *refs):
    refs = Refs(refs)
    c_ref, band_ref, got_xa, got_xb, got_ya, got_yb = refs.take(6)
    (speed,) = refs.take(1)
    p_in, part_ref, p_part = refs.take(3)
    if not first_step:
        (wet_in,) = refs.take(1)
    k_ref, halo_ref, spread_s, wet_out, p_ref, p_msg, speed_s = refs.take(7)
    g = lax.axis_index("grp")
    tracers, cells, width = c_ref.shape
    halo_ref[...] = x_halo(got_xa, got_xb)
    for slot in range(got_ya.shape[0]):
        spread_rows(rows, got_ya, got_yb, spread_s, slot)
    wet_out[...] = spread_s[tracers + 1] if first_step else wet_in[...]
    factors = side_factors(rows, sizes, halo_ref, wet_out[...], speed, speed_s, band_ref, tracers)
    for at, k in enumerate(factors):
        k_ref[at] = k
    side = sides_of(halo_ref[...], tracers + 2, tracers + 3, cells)
    change = sideways(rows, factors, side, spread_s[tracers], p_in[...])
    p_ref[...] = p_part[...] + change
    write_pigment(rows, count, p_ref, p_msg, g)


def step_kernel(rows, *refs):
    refs = Refs(refs)
    c_ref, part_ref, k_ref, halo_ref, spread_s, p_ref = refs.take(6)
    out_ref, msg_xa, msg_xb, msg_ya, msg_yb = refs.take(5)
    tracers = c_ref.shape[0]
    factors = [k_ref[i] for i in range(3)]
    for t in range(tracers):
        out_ref[t] = part_ref[t] + sideways(
                rows, factors, sides_of(halo_ref[...], t, tracers + 3, c_ref.shape[1]), spread_s[t], c_ref[t]
            )
    pack(rows, out_ref, p_ref, msg_xa, msg_xb, msg_ya, msg_yb, refs.refs)


def final_kernel(rows, sizes, first_step, *refs):
    refs = Refs(refs)
    c_ref, part_ref, band_ref, got_xa, got_xb, got_ya, got_yb = refs.take(7)
    (speed,) = refs.take(1)
    if not first_step:
        (wet_in,) = refs.take(1)
    out_hbm, spread_s, speed_s, halo_ref, new_s, sems = refs.take(6)
    tracers = c_ref.shape[0]
    halo_ref[...] = x_halo(got_xa, got_xb)
    if first_step:
        spread_rows(rows, got_ya, got_yb, spread_s, tracers + 1)
    wet_out = spread_s[tracers + 1] if first_step else wet_in[...]
    factors = side_factors(rows, sizes, halo_ref, wet_out, speed, speed_s, band_ref, tracers)
    copies = []
    for i, (a, n) in enumerate(chunks(tracers, sems.shape[0])):
        for t in range(a, a + n):
            spread_rows(rows, got_ya, got_yb, spread_s, t)
            new_s[t] = part_ref[t] + sideways(
                rows, factors, sides_of(halo_ref[...], t, tracers + 3, c_ref.shape[1]), spread_s[t], c_ref[t]
            )
        copies.append(pltpu.make_async_copy(new_s.at[pl.ds(a, n)], out_hbm.at[pl.ds(a, n)], sems.at[i]))
        copies[-1].start()
    for copy in copies:
        copy.wait()


def call(kernel, ins, outs, in_specs=None, out_specs=None, scratch=(), flops=1 << 20, moved=1 << 20):
    return pl.pallas_call(
        kernel,
        in_specs=[vmem() for _ in ins] if in_specs is None else in_specs,
        out_specs=[vmem() for _ in outs] if out_specs is None else out_specs,
        out_shape=outs,
        scratch_shapes=list(scratch),
        compiler_params=pltpu.CompilerParams(vmem_limit_bytes=VMEM_LIMIT),
        cost_estimate=pl.CostEstimate(flops=flops, bytes_accessed=moved, transcendentals=0),
    )(*ins)


def per_device(
    sizes,
    zonal_boundary_speed,
    meridional_boundary_speed,
    potential_warmth,
    saltiness_field,
    quiescent_mixing_profile,
    substance_amounts,
    submerged_layer_number,
    solar_radiation,
    interaction_rates,
    photosynthetic_rates,
    saturation_irradiance,
    pigment_per_tracer,
):
    count = sizes[0]
    result_dimensions = zonal_boundary_speed.shape
    all_levels, _, strip, width = result_dimensions
    tracers, levels, rows, _ = substance_amounts.shape
    cells = levels * rows
    total = all_levels * rows
    strip_cells = all_levels * strip
    dma = pltpu.SemaphoreType.DMA
    column = pltpu.VMEM((total, width), F32)
    band_s = pltpu.VMEM((cells, width), F32)

    own = [
        f.reshape(strip_cells, width)
        for f in (
            zonal_boundary_speed,
            meridional_boundary_speed,
            potential_warmth,
            saltiness_field,
            quiescent_mixing_profile,
        )
    ]
    _, height = raw_window(rows, count, strip_cells, 0)
    params = [
        p.reshape(1, tracers) for p in (photosynthetic_rates, saturation_irradiance, pigment_per_tracer)
    ]
    (first,) = call(first_kernel, [], [shape(SUB, width)], flops=1 << 30)
    small = [*params, interaction_rates, submerged_layer_number, solar_radiation]
    raw, window, *small = call(
        functools.partial(raw_kernel, rows, count),
        [first, *own, *small],
        [
            shape(5, strip_cells, width),
            shape(5 * height, width),
            *[jax.ShapeDtypeStruct(v.shape, v.dtype) for v in small],
        ],
    )
    *params, rates, layers, light = small
    raw_others = from_others(window, count)

    sent_pigment = shape(pigment_rows(rows, cells, count), width)
    sent_levels = level_shapes(tracers, rows, width, count)
    cols = shape(cells, width)
    sent_cols = shape(cells // 2, width) if folds(tracers + 3, cells, width) else cols
    field = shape(tracers, cells, width)
    c = substance_amounts.reshape(tracers, cells, width)
    pigment, p_msg = call(
        functools.partial(prep_kernel, rows, count),
        [params[2], c],
        [cols, sent_pigment],
    )
    full = None
    for step in range(STEPS):
        first_step, last_step = step == 0, step == STEPS - 1
        p_others = from_others(p_msg, count)
        if first_step:
            lines = shape(tracers + 2, levels, width)
            xa, xb, ya, yb, depth, solar, *levs = call(
                functools.partial(pack_kernel, rows),
                [layers, light, c, pigment],
                [
                    sent_cols,
                    sent_cols,
                    lines,
                    lines,
                    jax.ShapeDtypeStruct((SUB, width), jnp.int32),
                    shape(SUB, width),
                    *sent_levels,
                ],
                flops=1 << 24,
            )
        ya = lax.ppermute(ya, AXES, pairing(sizes, "gy", 0))
        yb = lax.ppermute(yb, AXES, pairing(sizes, "gy", 1))
        if count == 2:
            lev = from_others(levs[0], count)
        else:
            lev = [
                lax.ppermute(levs[0], "grp", [(i, (i + 1) % count) for i in range(count)]),
                lax.ppermute(levs[1], "grp", [((i + 1) % count, i) for i in range(count)]),
            ]
        band, xa, xb, speed, *full = call(
            functools.partial(ocean_kernel, rows, count, tracers, first_step),
            [depth, solar, xa, xb, pigment, *p_others, *([raw, *raw_others] if first_step else full)],
            [
                shape(7, cells, width),
                sent_cols,
                sent_cols,
                shape(3 * levels, width),
                *[shape(total, width)] * (5 if first_step else 4),
            ],
            scratch=[column, band_s]
            + [column] * (5 if first_step else 0)
            + [pltpu.VMEM((strip_cells, width), F32)] * (5 * (count - 1) if first_step else 0)
            + [column] * 3,
            flops=1<<32,
        )
        xa = lax.ppermute(xa, AXES, pairing(sizes, "gx", 0))
        xb = lax.ppermute(xb, AXES, pairing(sizes, "gx", 1))
        speed = lax.ppermute(speed, AXES, upward(sizes))
        tables = [shape(3, tracers, SUB, width), shape(tracers * SUB, tracers * SUB)]
        part, *rest = call(
            functools.partial(inner_kernel, rows, count, first_step, last_step),
            [*([*params, rates] if first_step else known_rates), c, band, ya, *lev, *(full if last_step else [])],
            [field]
            + ([shape(strip_cells, width)] * 4 if last_step else [cols])
            + (tables if first_step else []),
            out_specs=[vmem()]
            + ([hbm()] * 4 if last_step else [vmem()])
            + ([vmem()] * 2 if first_step else []),
            scratch=([pltpu.VMEM((strip_cells, width), F32)] * 4 + [dma((4,))] if last_step else [])
            + [pltpu.VMEM((tracers, cells, width), F32)],
            flops=1 << 10,
        )
        if first_step:
            *rest, tiles, weights = rest
            known_rates = [tiles, weights]
        known = [] if first_step else [wet_out]
        if not last_step:
            k, halo, spread, wet_out, pigment_next, p_msg = call(
                functools.partial(early_kernel, rows, count, sizes, first_step),
                [c, band, xa, xb, ya, yb, speed, pigment, part, *rest, *known],
                [shape(3, cells, width), sent_cols, shape(tracers + 2, cells, width), cols, cols, sent_pigment],
                scratch=[band_s],
            )
            pigment = pigment_next
            lines = shape(tracers + (0 if step + 1 == STEPS - 1 else 1), levels, width)
            c, xa, xb, ya, yb, *levs = call(
                functools.partial(step_kernel, rows),
                [c, part, k, halo, spread, pigment],
                [field, sent_cols, sent_cols, lines, lines, *sent_levels],
                flops=1<<32,
            )
        else:
            ocean = rest
            (c,) = call(
                functools.partial(final_kernel, rows, sizes, first_step),
                [c, part, band, xa, xb, ya, yb, speed, *known],
                [field],
                out_specs=[hbm()],
                scratch=[
                    pltpu.VMEM((tracers + 2, cells, width), F32),
                    band_s,
                    pltpu.VMEM(sent_cols.shape, F32),
                    pltpu.VMEM((tracers, cells, width), F32),
                    dma((5,)),
                ],
            )
    return tuple(f.reshape(result_dimensions) for f in ocean) + (c.reshape(substance_amounts.shape),)


def solution(mesh):
    ocean = P(None, "gy", "grp", "gx")
    tracer = P(None, "grp", "gy", "gx")
    surface = P("gy", "gx")
    sizes = tuple(mesh.shape[a] for a in AXES)
    return jax.shard_map(
        functools.partial(per_device, sizes),
        mesh=mesh,
        in_specs=(ocean,) * 5 + (tracer, surface, surface) + (P(),) * 4,
        out_specs=(ocean,) * 4 + (tracer,),
        check_vma=False,
    )
```

```python
import functools

import jax
import jax.numpy as jnp
from jax import lax
from jax.experimental import pallas as pl
from jax.experimental.pallas import tpu as pltpu
from jax.sharding import PartitionSpec as P

STEPS = 2

WATER_ATTEN = 0.01
PIGMENT_ATTEN = 0.05
WARMING_UPTAKE = 5.0
WARM_EXPANSION = 0.2
SALT_EXPANSION = 0.8
CONVECT_MIX = 0.15
SIDE_DIFFUSE = 0.05
WARMING_FACTOR = 0.0633
TIME_STEP = 0.5

SUB = 8
AXES = ("grp", "gx", "gy")
VMEM_LIMIT = 48 * 1024 * 1024

F32 = jnp.float32


def vmem():
    return pl.BlockSpec(memory_space=pltpu.VMEM)


def hbm():
    return pl.BlockSpec(memory_space=pltpu.HBM)


def shape(*dims):
    return jax.ShapeDtypeStruct(dims, F32)


def turn(x, shift, axis):
    shift = shift % x.shape[axis]
    return x if shift == 0 else pltpu.roll(x, shift, axis)


def iota(x, axis):
    return lax.broadcasted_iota(jnp.int32, x, axis)


def pairing(sizes, axis, odd):
    size_g, size_x, size_y = sizes

    def partner(g, x, y):
        i, n = (x, size_x) if axis == "gx" else (y, size_y)
        j = i + 1 if i % 2 == odd else i - 1
        if 0 <= j < n:
            return (g, j, y) if axis == "gx" else (g, x, j)
        if axis == "gx":
            return (g, x, y ^ 1) if (y ^ 1) < size_y else (g, x, y)
        return (g, x ^ 1, y) if (x ^ 1) < size_x else (g, x, y)

    def index(g, x, y):
        return (g * size_x + x) * size_y + y

    return [
        (index(g, x, y), index(*partner(g, x, y)))
        for g in range(size_g)
        for x in range(size_x)
        for y in range(size_y)
    ]


def upward(sizes):
    size_g, size_x, size_y = sizes
    return [
        ((g * size_x + x) * size_y + y, (g * size_x + x) * size_y + (y + 1) % size_y)
        for g in range(size_g)
        for x in range(size_x)
        for y in range(size_y)
    ]


def from_others(value, count):
    return [
        lax.ppermute(value, "grp", [(i, (i + k) % count) for i in range(count)])
        for k in range(1, count)
    ]


def chunks(n, parts):
    step = -(-n // parts)
    return [(a, min(step, n - a)) for a in range(0, n, step)]


class Refs:
    def __init__(self, refs):
        self.refs = list(refs)

    def take(self, n):
        out, self.refs = self.refs[:n], self.refs[n:]
        return out


def pick(mine, others, k):
    value = mine
    for at, other in enumerate(others):
        value = jnp.where(k == at + 1, other, value)
    return value


def folds(slots, cells, width):
    return 4 * slots < width and cells % (2 * SUB) == 0


def halves_of(cells, slots, width):
    if not folds(slots, cells, width):
        return [(slice(0, cells), 0)]
    return [(slice(0, cells // 2), 0), (slice(cells // 2, cells), width // 2)]


def pack_sides(c, slot, slots, left, right):
    cells, width = c.shape
    at = 2 * (slot + 1)
    lane = iota(left.shape, 1)
    for rows, base in halves_of(cells, slots, width):
        left = jnp.where(lane == base + at - 1, turn(c[rows], base + at - 1, 1), left)
        right = jnp.where(lane == base + at, turn(c[rows], base + at + 1, 1), right)
    return left, right


def sides_of(halo, slot, slots, cells):
    at = 2 * (slot + 1)
    width = halo.shape[1]
    turned = [turn(halo, -at - base, 1) for _, base in halves_of(cells, slots, width)]
    return turned[0] if len(turned) == 1 else jnp.concatenate(turned, axis=0)


def compact(rows, cells, count):
    return count == 2 and SUB == 2 * rows and cells >= 2 * SUB


def pigment_rows(rows, cells, count):
    return cells // 2 + SUB if compact(rows, cells, count) else cells


def level_shapes(tracers, rows, width, count):
    height = tracers * rows + 2 * (SUB - rows)
    height += -height % SUB
    return [shape(height, width)] * (1 if count == 2 else 2)


def write_levels(c, t, rows, levs, g):
    cells = c.shape[0]
    here = pl.ds(SUB - rows + t * rows, rows)
    if len(levs) == 1:
        levs[0][here, :] = jnp.where(g == 0, c[cells - rows :], c[:rows])
    else:
        levs[0][here, :] = c[cells - rows :]
        levs[1][here, :] = c[:rows]


def in_strip(rows, count, width, member):
    at_row = lax.rem(iota((SUB, width), 0), rows)
    strip = rows // count
    return (at_row >= member * strip) & (at_row < (member + 1) * strip)


def write_pigment(rows, count, p_ref, msg, g):
    cells, width = p_ref.shape
    if not compact(rows, cells, count):
        msg[pl.ds(0, cells), :] = p_ref[...]
        return
    levels, strip = cells // rows, rows // count
    for r in range(strip):
        msg[pl.ds(r, levels, stride=strip), :] = jnp.where(
            g == 0, p_ref[pl.ds(strip + r, levels, stride=rows), :], p_ref[pl.ds(r, levels, stride=rows), :]
        )
    blocks = [p_ref[pl.ds(at, SUB), :] for at in range(0, cells, SUB)]
    inner = blocks[1]
    for block in blocks[2:-1]:
        inner = inner + block
    inner = jnp.zeros_like(inner) if len(blocks) == 2 else inner
    near = jnp.where(g == 0, blocks[-1], blocks[0])
    rest = inner + jnp.where(g == 0, blocks[0], blocks[-1])
    rest = rest + turn(rest, rows, 0)
    msg[pl.ds(cells // 2, SUB), :] = jnp.where(in_strip(rows, count, width, g), near, turn(rest, strip, 0))


def read_pigment(rows, count, msg, other_s, g):
    cells, width = other_s.shape
    if not compact(rows, cells, count):
        return msg[pl.ds(0, cells), :]
    levels, strip = cells // rows, rows // count
    for s in range(count):
        for r in range(strip):
            other_s[pl.ds(s * strip + r, levels, stride=rows), :] = jnp.where(
                g == s, msg[pl.ds(r, levels, stride=strip), :], 0.0
            )
    edge = msg[pl.ds(cells // 2, SUB), :]
    theirs = in_strip(rows, count, width, 1 - g)
    first = other_s[pl.ds(0, SUB), :]
    rest = jnp.where(iota((SUB, width), 0) < rows, turn(edge, strip, 0), 0.0)
    other_s[pl.ds(0, SUB), :] = jnp.where(theirs, jnp.where(g == 0, edge, rest), first)
    last = other_s[pl.ds(cells - SUB, SUB), :]
    other_s[pl.ds(cells - SUB, SUB), :] = jnp.where(theirs & (g == 1), edge, last)
    return other_s[...]


def raw_window(rows, count, strip_cells, member):
    if count != 2:
        return 0, strip_cells
    height = strip_cells // 2 + 2 * (rows // count)
    return member * (strip_cells - height), height


def first_kernel(out_ref):
    out_ref[...] = jnp.zeros(out_ref.shape, F32)


def raw_kernel(rows, count, first_ref, *refs):
    refs = Refs(refs)
    fields, small_in = refs.take(5), refs.take(6)
    raw_ref, out_ref = refs.take(2)
    g = lax.axis_index("grp")
    for small, small_out in zip(small_in, refs.take(6)):
        small_out[...] = small[...]
    strip_cells = raw_ref.shape[1]
    low, height = raw_window(rows, count, strip_cells, 0)
    high, _ = raw_window(rows, count, strip_cells, 1)
    for at, field in enumerate(fields):
        raw_ref[at] = field[...]
        lower_part, upper_part = field[pl.ds(low, height), :], field[pl.ds(high, height), :]
        out_ref[pl.ds(at * height, height), :] = jnp.where(g == 0, upper_part, lower_part)


def tile(v, cells):
    width = v.shape[1]
    return jnp.broadcast_to(v[None], (cells // SUB, SUB, width)).reshape(cells, width)


def prep_kernel(rows, count, pig_ref, c_ref, p_ref, p_msg):
    g = lax.axis_index("grp")
    tracers, cells, width = c_ref.shape
    weights = pig_ref[...]
    pigment = jnp.zeros((cells, width), F32)
    for t in range(tracers):
        c = c_ref[t]
        pigment = pigment + tile(jnp.broadcast_to(weights[:, t : t + 1], (SUB, width)), cells) * c
    p_ref[...] = pigment
    write_pigment(rows, count, p_ref, p_msg, g)


def halves(v):
    high = v.astype(jnp.bfloat16)
    return high, (v - high.astype(F32)).astype(jnp.bfloat16)


def dot(a, b, **kw):
    return jnp.dot(a, b, preferred_element_type=F32, **kw)


def spread_rates(rates, tracers):
    exact = functools.partial(dot, precision=lax.Precision.HIGHEST)
    depth = tracers * SUB
    spread = jnp.where(iota((depth, tracers), 0) // SUB == iota((depth, tracers), 1), 1.0, 0.0)
    spread_t = jnp.where(iota((tracers, depth), 1) // SUB == iota((tracers, depth), 0), 1.0, 0.0)
    weights = exact(exact(spread, rates), spread_t)
    return jnp.where(
        lax.rem(iota((depth, depth), 0), SUB) == lax.rem(iota((depth, depth), 1), SUB), weights, 0.0
    )


def mix(weights, c_ref, mix_ref):
    tracers, cells, width = c_ref.shape
    w_high, w_low = halves(weights)
    for b in range(cells // SUB):
        here = pl.ds(b * SUB, SUB)
        c_high, c_low = halves(c_ref[:, here, :].reshape(tracers * SUB, width))
        mixed = dot(w_high, c_high) + (dot(w_high, c_low) + dot(w_low, c_high))
        mix_ref[:, here, :] = mixed.reshape(tracers, SUB, width)


def put_rows(msg_ya, msg_yb, slot, first, last):
    y_even = lax.rem(lax.axis_index("gy"), 2) == 0
    msg_ya[slot] = jnp.where(y_even, last, first)
    msg_yb[slot] = jnp.where(y_even, first, last)


def pack(rows, c_ref, p_ref, msg_xa, msg_xb, msg_ya, msg_yb, levs):
    tracers, cells, _ = c_ref.shape
    levels = cells // rows
    x_even = lax.rem(lax.axis_index("gx"), 2) == 0
    left = right = jnp.zeros(msg_xa.shape, F32)
    left, right = pack_sides(p_ref[...], tracers + 2, tracers + 3, left, right)
    g = lax.axis_index("grp")
    for t in range(tracers):
        left, right = pack_sides(c_ref[t], t, tracers + 3, left, right)
        write_levels(c_ref[t], t, rows, levs, g)
    msg_xa[...] = jnp.where(x_even, right, left)
    msg_xb[...] = jnp.where(x_even, left, right)
    first, last = pl.ds(0, levels, stride=rows), pl.ds(rows - 1, levels, stride=rows)
    for t in range(tracers):
        put_rows(msg_ya, msg_yb, t, c_ref[t, first, :], c_ref[t, last, :])
    if msg_ya.shape[0] > tracers:
        put_rows(msg_ya, msg_yb, tracers, p_ref[first, :], p_ref[last, :])


def pack_kernel(rows, *refs):
    refs = Refs(refs)
    depth_in, solar_in, c_ref, p_ref = refs.take(4)
    msg_xa, msg_xb, msg_ya, msg_yb, depth_ref, solar_ref = refs.take(6)
    levs = refs.refs
    tracers, cells, width = c_ref.shape
    for r in range(0, SUB, rows):
        depth_ref[pl.ds(r, rows), :] = depth_in[...]
        solar_ref[pl.ds(r, rows), :] = solar_in[...]
    pack(rows, c_ref, p_ref, msg_xa, msg_xb, msg_ya, msg_yb, levs)
    levels = cells // rows
    level = lax.axis_index("grp") * levels + iota((levels, width), 0)
    wet_first = jnp.where(level < depth_in[pl.ds(0, 1), :], 1.0, 0.0)
    wet_last = jnp.where(level < depth_in[pl.ds(rows - 1, 1), :], 1.0, 0.0)
    put_rows(msg_ya, msg_yb, tracers + 1, wet_first, wet_last)


def ocean_kernel(rows, count, tracers, first_step, *refs):
    refs = Refs(refs)
    depth_ref, solar_ref = refs.take(2)
    in_xa, in_xb = refs.take(2)
    p_own, *p_others = refs.take(count)
    if first_step:
        own_fields, *other_fields = refs.take(count)
    else:
        fields = refs.take(5)
    band_ref, msg_xa, msg_xb, speed_ref = refs.take(4)
    full_out = refs.take(5 if first_step else 4)
    (p_other_s,) = refs.take(1)
    if first_step:
        fields = refs.take(5)
        other_s = refs.take(5 * (count - 1))
    g = lax.axis_index("grp")
    cells, width = p_own.shape
    levels = cells // rows
    total = count * cells
    all_levels = total // rows
    strip = rows // count

    pigments = [read_pigment(rows, count, o, p_other_s, g) for o in p_others]
    bands = [pick(p_own[...], pigments, lax.rem(g - b + count, count)) for b in range(count)]
    pigment = jnp.concatenate(bands, axis=0)
    if first_step:
        strip_cells = all_levels * strip
        for at in range(5):
            for k in range(count - 1):
                other = other_s[5 * k + at]
                low, height = raw_window(rows, count, strip_cells, 0)
                value = other_fields[k][pl.ds(at * height, height), :]
                if count != 2:
                    other[...] = value
                    continue
                high, _ = raw_window(rows, count, strip_cells, 1)
                other[...] = jnp.zeros((strip_cells, width), F32)
                other[pl.ds(low, height), :] = jnp.where(g == 0, value, 0.0)
                kept = jnp.where(iota(value.shape, 0) < low + height - high, other[pl.ds(high, height), :], 0.0)
                other[pl.ds(high, height), :] = jnp.where(g == 1, value, kept)
            for s in range(count):
                k = lax.rem(g - s + count, count)
                for r in range(strip):
                    here = pl.ds(r, all_levels, stride=strip)
                    fields[at][pl.ds(s * strip + r, all_levels, stride=rows), :] = pick(
                        own_fields[at, here, :], [other_s[5 * j + at][here, :] for j in range(count - 1)], k
                    )

    row = iota((total, width), 0)
    wet = jnp.where(row // rows < tile(depth_ref[...], total), 1.0, 0.0)
    att = WATER_ATTEN + PIGMENT_ATTEN * pigment
    summed = att
    step = rows
    while step < total:
        summed = summed + jnp.where(row >= step, turn(summed, step, 0), 0.0)
        step *= 2
    top = tile(solar_ref[...], total) * jnp.exp(att - summed)
    par = top * jnp.exp(-0.5 * att)
    east, north, temp, sal, mixing = [f[...] for f in fields]
    temp = temp + WARMING_UPTAKE * (top * (1.0 - jnp.exp(-att))) * wet

    def below(v):
        return turn(v, -rows, 0)

    density = SALT_EXPANSION * sal - WARM_EXPANSION * temp
    face = 0.5 * (mixing + below(mixing)) + CONVECT_MIX / (1.0 + jnp.exp(below(density) - density))
    face = jnp.where(row < total - rows, face * below(wet), 0.0)

    def stir(v):
        flux = face * (below(v) - v)
        return v + flux - turn(flux, rows, 0)

    mixed = [stir(v) for v in (east, north, temp, sal)]

    def band_of(v):
        value = v[:cells]
        for b in range(1, count):
            value = jnp.where(g == b, v[b * cells : (b + 1) * cells], value)
        return value

    u = band_of(mixed[0])
    wet_band = band_of(wet)
    band_ref[0] = u
    band_ref[1] = band_of(mixed[1])
    speed_ref[pl.ds(0, levels), :] = band_ref[1, pl.ds(rows - 1, levels, stride=rows), :]
    speed_ref[pl.ds(levels, levels), :] = jnp.zeros((levels, width), F32)
    speed_ref[pl.ds(2 * levels, levels), :] = jnp.zeros((levels, width), F32)

    x_even = lax.rem(lax.axis_index("gx"), 2) == 0
    xa, xb = in_xa[...], in_xb[...]
    left, right = jnp.where(x_even, xb, xa), jnp.where(x_even, xa, xb)
    left, right = pack_sides(wet_band, tracers + 1, tracers + 3, left, right)
    _, right = pack_sides(u, tracers, tracers + 3, left, right)
    msg_xa[...] = jnp.where(x_even, right, left)
    msg_xb[...] = jnp.where(x_even, left, right)
    band_ref[2] = band_of(mixed[2])
    band_ref[3] = band_of(face)
    band_ref[4] = band_of(turn(face, rows, 0))
    band_ref[5] = band_of(par)
    band_ref[6] = wet_band
    for at, v in enumerate(mixed):
        full_out[at][...] = v
    if first_step:
        full_out[4][...] = mixing


def start_own_strip(rows, count, g, full, outs, strips, sems):
    strip = rows // count
    all_levels = full[0].shape[0] // rows
    copies = [pltpu.make_async_copy(strips[at], outs[at], sems.at[at]) for at in range(4)]
    for at in range(4):
        for r in range(strip):
            value = full[at][pl.ds(r, all_levels, stride=rows), :]
            for s in range(1, count):
                value = jnp.where(g == s, full[at][pl.ds(s * strip + r, all_levels, stride=rows), :], value)
            strips[at][pl.ds(r, all_levels, stride=strip), :] = value
        copies[at].start()
    return copies


def lower(opening, speed):
    return opening * (jnp.maximum(speed, 0.0) + SIDE_DIFFUSE)


def upper(opening, speed):
    return opening * (jnp.minimum(speed, 0.0) - SIDE_DIFFUSE)


def inner_kernel(rows, count, first_step, last_step, *refs):
    refs = Refs(refs)
    if first_step:
        params, (rates_ref,) = refs.take(3), refs.take(1)
    else:
        tiles_ref, w_ref = refs.take(2)
    c_ref, band_ref, _ = refs.take(3)
    lev_in = refs.take(1 if count == 2 else 2)
    if last_step:
        full = refs.take(4)
    (part_ref,) = refs.take(1)
    if last_step:
        outs = refs.take(4)
    else:
        (p_part,) = refs.take(1)
    if first_step:
        tiles_ref, w_ref = refs.take(2)
    if last_step:
        strips, (sems,) = refs.take(4), refs.take(1)
        copies = start_own_strip(rows, count, lax.axis_index("grp"), full, outs, strips, sems)
    (mix_ref,) = refs.take(1)
    tracers, cells, width = c_ref.shape
    if first_step:
        w_ref[...] = spread_rates(rates_ref[...], tracers)
        for at, param in enumerate(params):
            values = param[...]
            for t in range(tracers):
                tiles_ref[at, t] = jnp.broadcast_to(values[:, t : t + 1], (SUB, width))
    mix(w_ref[...], c_ref, mix_ref)
    lane = iota((cells, width), 1)
    at_row = lax.rem(iota((cells, width), 0), rows)
    u = band_ref[0]
    v = band_ref[1]
    wet = band_ref[6]

    def west(x):
        return turn(x, 1, 1)

    def east(x):
        return turn(x, -1, 1)

    def south(x):
        return turn(x, 1, 0)

    def north(x):
        return turn(x, -1, 0)

    open_w = jnp.where(lane == 0, 0.0, wet * west(wet))
    open_e = jnp.where(lane == width - 1, 0.0, wet * east(wet))
    open_s = jnp.where(at_row == 0, 0.0, wet * south(wet))
    open_n = jnp.where(at_row == rows - 1, 0.0, wet * north(wet))
    k_w = lower(open_w, west(u))
    k_e = -upper(open_e, u)
    k_s = lower(open_s, south(v))
    k_n = -upper(open_n, v)
    k_d = band_ref[3]
    k_u = band_ref[4]
    k_c = (upper(open_w, west(u)) - lower(open_e, u)) + (upper(open_s, south(v)) - lower(open_n, v))
    k_c = 1.0 + (k_c - k_d - k_u)
    par = band_ref[5]
    lit = TIME_STEP * wet
    warm = lit * jnp.exp(WARMING_FACTOR * (band_ref[2] - 20.0))
    lit = lit * par
    pigment = jnp.zeros((cells, width), F32)
    for t in range(tracers):
        c = c_ref[t]
        at = SUB - rows + t * rows
        up8 = lev_in[0][pl.ds(at + rows - SUB, SUB), :]
        down8 = lev_in[-1][pl.ds(at, SUB), :]
        c_u = turn(jnp.concatenate([up8, c], axis=0), rows, 0)[SUB:]
        c_d = turn(jnp.concatenate([c, down8], axis=0), -rows, 0)[:cells]
        part = (
            (k_c + tile(tiles_ref[0, t], cells) * (lit / (par + tile(tiles_ref[1, t], cells)))) * c
            + (k_u * c_u + k_d * c_d)
            + (k_w * west(c) + k_e * east(c))
            + (k_s * south(c) + k_n * north(c))
            + warm * mix_ref[t]
        )
        part_ref[t] = part
        if not last_step:
            pigment = pigment + tile(tiles_ref[2, t], cells) * part
    if last_step:
        for copy in copies:
            copy.wait()
    else:
        p_part[...] = pigment


def x_halo(got_xa, got_xb):
    x_even = lax.rem(lax.axis_index("gx"), 2) == 0
    xa, xb = got_xa[...], got_xb[...]
    return jnp.where((lax.rem(iota(xa.shape, 1), 2) == 0) == x_even, xb, xa)


def spread_rows(rows, got_ya, got_yb, out_ref, slot):
    y_even = lax.rem(lax.axis_index("gy"), 2) == 0
    levels = got_ya.shape[1]
    ya, yb = got_ya[slot], got_yb[slot]
    out_ref[slot, pl.ds(0, levels, stride=rows), :] = jnp.where(y_even, yb, ya)
    out_ref[slot, pl.ds(rows - 1, levels, stride=rows), :] = jnp.where(y_even, ya, yb)


def side_factors(rows, sizes, halo_ref, wet_out, speed, speed_s, band_ref, tracers):
    _, size_x, size_y = sizes
    x = lax.axis_index("gx")
    y = lax.axis_index("gy")
    u = band_ref[0]
    v = band_ref[1]
    wet = band_ref[6]
    cells, width = wet.shape
    speed_s[pl.ds(0, cells // rows, stride=rows), :] = speed[pl.ds(0, cells // rows), :]
    lane = iota((cells, width), 1)
    at_row = lax.rem(iota((cells, width), 0), rows)
    at_w, at_e, at_s, at_n = lane == 0, lane == width - 1, at_row == 0, at_row == rows - 1
    wet_x = wet * sides_of(halo_ref[...], tracers + 1, tracers + 3, cells)
    wet_y = wet * wet_out
    open_w = jnp.where(at_w & (x > 0), wet_x, 0.0)
    open_e = jnp.where(at_e & (x < size_x - 1), wet_x, 0.0)
    open_s = jnp.where(at_s & (y > 0), wet_y, 0.0)
    open_n = jnp.where(at_n & (y < size_y - 1), wet_y, 0.0)
    u_w = sides_of(halo_ref[...], tracers, tracers + 3, cells)
    v_s = jnp.where(at_s, speed_s[...], 0.0)
    k_x = lower(open_w, u_w) - upper(open_e, u)
    k_y = lower(open_s, v_s) - upper(open_n, v)
    k_c = (upper(open_w, u_w) - lower(open_e, u)) + (upper(open_s, v_s) - lower(open_n, v))
    return k_x, k_y, k_c


def sideways(rows, factors, sides, outer, c):
    k_x, k_y, k_c = factors
    at_row = lax.rem(iota(c.shape, 0), rows)
    edge = (at_row == 0) | (at_row == rows - 1)
    return (k_x * sides + k_c * c) + jnp.where(edge, k_y * outer, 0.0)


def early_kernel(rows, count, sizes, first_step, *refs):
    refs = Refs(refs)
    c_ref, band_ref, got_xa, got_xb, got_ya, got_yb = refs.take(6)
    (speed,) = refs.take(1)
    p_in, part_ref, p_part = refs.take(3)
    if not first_step:
        (wet_in,) = refs.take(1)
    k_ref, halo_ref, spread_s, wet_out, p_ref, p_msg, speed_s = refs.take(7)
    g = lax.axis_index("grp")
    tracers, cells, width = c_ref.shape
    halo_ref[...] = x_halo(got_xa, got_xb)
    for slot in range(got_ya.shape[0]):
        spread_rows(rows, got_ya, got_yb, spread_s, slot)
    wet_out[...] = spread_s[tracers + 1] if first_step else wet_in[...]
    factors = side_factors(rows, sizes, halo_ref, wet_out[...], speed, speed_s, band_ref, tracers)
    for at, k in enumerate(factors):
        k_ref[at] = k
    side = sides_of(halo_ref[...], tracers + 2, tracers + 3, cells)
    change = sideways(rows, factors, side, spread_s[tracers], p_in[...])
    p_ref[...] = p_part[...] + change
    write_pigment(rows, count, p_ref, p_msg, g)


def step_kernel(rows, *refs):
    refs = Refs(refs)
    c_ref, part_ref, k_ref, halo_ref, spread_s, p_ref = refs.take(6)
    out_ref, msg_xa, msg_xb, msg_ya, msg_yb = refs.take(5)
    tracers = c_ref.shape[0]
    factors = [k_ref[i] for i in range(3)]
    for t in range(tracers):
        out_ref[t] = part_ref[t] + sideways(
                rows, factors, sides_of(halo_ref[...], t, tracers + 3, c_ref.shape[1]), spread_s[t], c_ref[t]
            )
    pack(rows, out_ref, p_ref, msg_xa, msg_xb, msg_ya, msg_yb, refs.refs)


def final_kernel(rows, sizes, first_step, *refs):
    refs = Refs(refs)
    c_ref, part_ref, band_ref, got_xa, got_xb, got_ya, got_yb = refs.take(7)
    (speed,) = refs.take(1)
    if not first_step:
        (wet_in,) = refs.take(1)
    out_hbm, spread_s, speed_s, halo_ref, new_s, sems = refs.take(6)
    tracers = c_ref.shape[0]
    halo_ref[...] = x_halo(got_xa, got_xb)
    if first_step:
        spread_rows(rows, got_ya, got_yb, spread_s, tracers + 1)
    wet_out = spread_s[tracers + 1] if first_step else wet_in[...]
    factors = side_factors(rows, sizes, halo_ref, wet_out, speed, speed_s, band_ref, tracers)
    copies = []
    for i, (a, n) in enumerate(chunks(tracers, sems.shape[0])):
        for t in range(a, a + n):
            spread_rows(rows, got_ya, got_yb, spread_s, t)
            new_s[t] = part_ref[t] + sideways(
                rows, factors, sides_of(halo_ref[...], t, tracers + 3, c_ref.shape[1]), spread_s[t], c_ref[t]
            )
        copies.append(pltpu.make_async_copy(new_s.at[pl.ds(a, n)], out_hbm.at[pl.ds(a, n)], sems.at[i]))
        copies[-1].start()
    for copy in copies:
        copy.wait()


def call(kernel, ins, outs, in_specs=None, out_specs=None, scratch=(), flops=1 << 20, moved=1 << 20):
    return pl.pallas_call(
        kernel,
        in_specs=[vmem() for _ in ins] if in_specs is None else in_specs,
        out_specs=[vmem() for _ in outs] if out_specs is None else out_specs,
        out_shape=outs,
        scratch_shapes=list(scratch),
        compiler_params=pltpu.CompilerParams(vmem_limit_bytes=VMEM_LIMIT),
        cost_estimate=pl.CostEstimate(flops=flops, bytes_accessed=moved, transcendentals=0),
    )(*ins)


def per_device(
    sizes,
    zonal_boundary_speed,
    meridional_boundary_speed,
    potential_warmth,
    saltiness_field,
    quiescent_mixing_profile,
    substance_amounts,
    submerged_layer_number,
    solar_radiation,
    interaction_rates,
    photosynthetic_rates,
    saturation_irradiance,
    pigment_per_tracer,
):
    count = sizes[0]
    result_dimensions = zonal_boundary_speed.shape
    all_levels, _, strip, width = result_dimensions
    tracers, levels, rows, _ = substance_amounts.shape
    cells = levels * rows
    total = all_levels * rows
    strip_cells = all_levels * strip
    dma = pltpu.SemaphoreType.DMA
    column = pltpu.VMEM((total, width), F32)
    band_s = pltpu.VMEM((cells, width), F32)

    own = [
        f.reshape(strip_cells, width)
        for f in (
            zonal_boundary_speed,
            meridional_boundary_speed,
            potential_warmth,
            saltiness_field,
            quiescent_mixing_profile,
        )
    ]
    _, height = raw_window(rows, count, strip_cells, 0)
    params = [
        p.reshape(1, tracers) for p in (photosynthetic_rates, saturation_irradiance, pigment_per_tracer)
    ]
    (first,) = call(first_kernel, [], [shape(SUB, width)], flops=1 << 30)
    small = [*params, interaction_rates, submerged_layer_number, solar_radiation]
    raw, window, *small = call(
        functools.partial(raw_kernel, rows, count),
        [first, *own, *small],
        [
            shape(5, strip_cells, width),
            shape(5 * height, width),
            *[jax.ShapeDtypeStruct(v.shape, v.dtype) for v in small],
        ],
    )
    *params, rates, layers, light = small
    raw_others = from_others(window, count)

    sent_pigment = shape(pigment_rows(rows, cells, count), width)
    sent_levels = level_shapes(tracers, rows, width, count)
    cols = shape(cells, width)
    sent_cols = shape(cells // 2, width) if folds(tracers + 3, cells, width) else cols
    field = shape(tracers, cells, width)
    c = substance_amounts.reshape(tracers, cells, width)
    pigment, p_msg = call(
        functools.partial(prep_kernel, rows, count),
        [params[2], c],
        [cols, sent_pigment],
    )
    full = None
    for step in range(STEPS):
        first_step, last_step = step == 0, step == STEPS - 1
        p_others = from_others(p_msg, count)
        if first_step:
            lines = shape(tracers + 2, levels, width)
            xa, xb, ya, yb, depth, solar, *levs = call(
                functools.partial(pack_kernel, rows),
                [layers, light, c, pigment],
                [
                    sent_cols,
                    sent_cols,
                    lines,
                    lines,
                    jax.ShapeDtypeStruct((SUB, width), jnp.int32),
                    shape(SUB, width),
                    *sent_levels,
                ],
                flops=1 << 24,
            )
        ya = lax.ppermute(ya, AXES, pairing(sizes, "gy", 0))
        yb = lax.ppermute(yb, AXES, pairing(sizes, "gy", 1))
        if count == 2:
            lev = from_others(levs[0], count)
        else:
            lev = [
                lax.ppermute(levs[0], "grp", [(i, (i + 1) % count) for i in range(count)]),
                lax.ppermute(levs[1], "grp", [((i + 1) % count, i) for i in range(count)]),
            ]
        band, xa, xb, speed, *full = call(
            functools.partial(ocean_kernel, rows, count, tracers, first_step),
            [depth, solar, xa, xb, pigment, *p_others, *([raw, *raw_others] if first_step else full)],
            [
                shape(7, cells, width),
                sent_cols,
                sent_cols,
                shape(3 * levels, width),
                *[shape(total, width)] * (5 if first_step else 4),
            ],
            scratch=[band_s]
            + [column] * (5 if first_step else 0)
            + [pltpu.VMEM((strip_cells, width), F32)] * (5 * (count - 1) if first_step else 0),
            flops=1<<32,
        )
        xa = lax.ppermute(xa, AXES, pairing(sizes, "gx", 0))
        xb = lax.ppermute(xb, AXES, pairing(sizes, "gx", 1))
        speed = lax.ppermute(speed, AXES, upward(sizes))
        tables = [shape(3, tracers, SUB, width), shape(tracers * SUB, tracers * SUB)]
        part, *rest = call(
            functools.partial(inner_kernel, rows, count, first_step, last_step),
            [*([*params, rates] if first_step else known_rates), c, band, ya, *lev, *(full if last_step else [])],
            [field]
            + ([shape(strip_cells, width)] * 4 if last_step else [cols])
            + (tables if first_step else []),
            out_specs=[vmem()]
            + ([hbm()] * 4 if last_step else [vmem()])
            + ([vmem()] * 2 if first_step else []),
            scratch=([pltpu.VMEM((strip_cells, width), F32)] * 4 + [dma((4,))] if last_step else [])
            + [pltpu.VMEM((tracers, cells, width), F32)],
            flops=1 << 10,
        )
        if first_step:
            *rest, tiles, weights = rest
            known_rates = [tiles, weights]
        known = [] if first_step else [wet_out]
        if not last_step:
            k, halo, spread, wet_out, pigment_next, p_msg = call(
                functools.partial(early_kernel, rows, count, sizes, first_step),
                [c, band, xa, xb, ya, yb, speed, pigment, part, *rest, *known],
                [shape(3, cells, width), sent_cols, shape(tracers + 2, cells, width), cols, cols, sent_pigment],
                scratch=[band_s],
            )
            pigment = pigment_next
            lines = shape(tracers + (0 if step + 1 == STEPS - 1 else 1), levels, width)
            c, xa, xb, ya, yb, *levs = call(
                functools.partial(step_kernel, rows),
                [c, part, k, halo, spread, pigment],
                [field, sent_cols, sent_cols, lines, lines, *sent_levels],
                flops=1<<32,
            )
        else:
            ocean = rest
            (c,) = call(
                functools.partial(final_kernel, rows, sizes, first_step),
                [c, part, band, xa, xb, ya, yb, speed, *known],
                [field],
                out_specs=[hbm()],
                scratch=[
                    pltpu.VMEM((tracers + 2, cells, width), F32),
                    band_s,
                    pltpu.VMEM(sent_cols.shape, F32),
                    pltpu.VMEM((tracers, cells, width), F32),
                    dma((5,)),
                ],
            )
    return tuple(f.reshape(result_dimensions) for f in ocean) + (c.reshape(substance_amounts.shape),)


def solution(mesh):
    ocean = P(None, "gy", "grp", "gx")
    tracer = P(None, "grp", "gy", "gx")
    surface = P("gy", "gx")
    sizes = tuple(mesh.shape[a] for a in AXES)
    return jax.shard_map(
        functools.partial(per_device, sizes),
        mesh=mesh,
        in_specs=(ocean,) * 5 + (tracer, surface, surface) + (P(),) * 4,
        out_specs=(ocean,) * 4 + (tracer,),
        check_vma=False,
    )
```
